32 devices in a mesh: dp: 4 (over y, core), expert: 8 (over z, x).
Axes of the slice: x: 2, y: 2, z: 4, core: 2. Of those that a mesh axis runs over, the one named last changes fastest.
Arguments:
- tokens: bfloat16 [2048, 1024], P(('dp', 'expert')), may hold values from -6 to 6
- cotangent: bfloat16 [2048, 1024], P(('dp', 'expert')), may hold values from -1.5 to 1.5
- routes: int32 [2048, 2], P(('dp', 'expert')), may hold values from 0 to 7, all different within a row
- gates: bfloat16 [2048, 2], P(('dp', 'expert')), may hold values from 0.099609375 to 0.8984375
- proj_in: bfloat16 [8, 1024, 2048], P('expert'), may hold values from -0.1875 to 0.1875
- proj_out: bfloat16 [8, 2048, 1024], P('expert'), may hold values from -0.125 to 0.125
Outputs:
- token_grads: bfloat16 [2048, 1024], P(('dp', 'expert'))
- gate_grads: bfloat16 [2048, 2], P(('dp', 'expert'))
- grad_in: bfloat16 [8, 1024, 2048], P('expert', 'dp')
- grad_out: bfloat16 [8, 2048, 1024], P('expert', 'dp')
The draws below stay inside these ranges and needn't reach their ends.
All inputs are finite; a program needn't handle non-finite values.
Results may differ from the reference program's by a relative error of at most 0.018.
Values may be sent and summed in bfloat16 or wider, within the bound.
No kernel may reach another device: no remote copies, remote signals or barrier semaphores. Data moves between devices by JAX's collectives and lax.ppermute only.
A program may use at most 64 MiB of HBM per device.

```python
import jax
import jax.numpy as jnp
from jax import lax

D = 1024
FFW = 2048
TOK_DEV = 64
CAP = 16
EXPERTS = 8
TOKENS = 2048
N_DP = 4
N_EXPERT = 8


def levels(rng, dims, split, low, largest):
    level, own = 1.0, jax.random.fold_in(rng, 6)
    for dim, parts in split:
        steps = jnp.exp(jax.random.uniform(jax.random.fold_in(own, dim), (parts,), jnp.float32, low / len(split), largest / len(split)))
        level = level * jnp.repeat(steps, dims[dim] // parts).reshape([-1 if axis == dim else 1 for axis in range(len(dims))])
    return level


def picks_of(stream_key, rows, number_of, top, lift):
    sequence = jax.random.permutation(jax.random.fold_in(stream_key, 1), number_of)
    boost = sequence
    for power in range(3):
        boost = boost * boost // number_of
    boost = boost * lift // number_of
    chance = jax.random.randint(jax.random.fold_in(stream_key, 2), (rows, number_of), 0, 4096) + boost
    sure = jax.random.permutation(jax.random.fold_in(stream_key, 3), rows)[jnp.arange(number_of) % rows]
    chance = jnp.where(jnp.arange(rows)[:, None] == sure[None, :], 1 << 14, chance)
    score = chance * number_of + jnp.arange(number_of)
    return lax.top_k(score.astype(jnp.int32), top)[1].astype(jnp.int32)


def gaussian(rng, dims, spread, bound, split=(), held_as=jnp.bfloat16):
    drawn = spread * jax.random.normal(rng, dims, jnp.float32)
    if split:
        drawn = drawn * levels(rng, dims, split, -0.22, 0.18)
    return jnp.clip(drawn, -bound, bound).astype(held_as)


def setup_inputs(seed: int = 0) -> dict:
    splits = jax.random.split(jax.random.key(seed), 7)
    return {
        "tokens": gaussian(splits[0], (TOKENS, D), 1.0, 6.0, ((0, 32),)),
        "cotangent": gaussian(splits[1], (TOKENS, D), 0.25, 1.5, ((0, 32),)),
        "routes": picks_of(splits[2], TOKENS, EXPERTS, 2, 4096),
        "gates": jnp.clip(0.099609375 + 0.7988281 * jax.random.uniform(splits[3], (TOKENS, 2), jnp.float32) ** levels(splits[3], (TOKENS, 2), ((0, 32),), -0.2, 0.2), 0.099609375, 0.8984375).astype(jnp.bfloat16),
        "proj_in": gaussian(splits[4], (EXPERTS, D, FFW), D ** -0.5, 0.1875, ((0, 8),)),
        "proj_out": gaussian(splits[5], (EXPERTS, FFW, D), FFW ** -0.5, 0.125, ((0, 8),)),
    }


def slope_of(pre_act):
    gauss_cdf = 0.5 * (1.0 + jax.scipy.special.erf(pre_act * 0.7071067811865476))
    gauss_pdf = jnp.exp(-0.5 * pre_act * pre_act) * 0.3989422804014327
    return gauss_cdf + pre_act * gauss_pdf


def route_slots(chosen, experts):
    one_hot = (chosen[..., None] == jnp.arange(experts, dtype=jnp.int32)).astype(jnp.int32)
    earlier = jnp.cumsum(one_hot, axis=-2) - one_hot
    slot_pos = jnp.sum(earlier * one_hot, axis=-1)
    kept_mask = slot_pos < CAP
    target = jnp.where(kept_mask, chosen * CAP + slot_pos, experts * CAP).astype(jnp.int32)
    return kept_mask, target


def reference(tokens, cotangent, routes, gates, proj_in, proj_out):
    blocks = N_DP * N_EXPERT
    slots_all = EXPERTS * CAP
    tok_x = tokens.reshape(blocks, TOK_DEV, D)
    tok_dy = cotangent.reshape(blocks, TOK_DEV, D)
    route_blk = routes.reshape(blocks, TOK_DEV, 2)
    gate_blk = gates.reshape(blocks, TOK_DEV, 2)
    chosen = jnp.concatenate([route_blk[:, :, 0], route_blk[:, :, 1]], axis=1)
    kept_mask, target = route_slots(chosen, EXPERTS)
    both_x = jnp.concatenate([tok_x, tok_x], axis=1)
    both_dy = jnp.concatenate([tok_dy, tok_dy], axis=1)
    both_gate = jnp.concatenate([gate_blk[:, :, 0], gate_blk[:, :, 1]], axis=1)

    def place(values, where_to):
        empty = jnp.zeros((slots_all,) + values.shape[1:], values.dtype)
        return empty.at[where_to].set(values, mode="drop")

    def by_expert(values):
        shaped = values.reshape((N_DP, N_EXPERT, EXPERTS, CAP) + values.shape[2:])
        moved = jnp.moveaxis(shaped, 2, 0)
        return moved.reshape((EXPERTS, N_DP, N_EXPERT * CAP) + values.shape[2:])

    ex_x = by_expert(jax.vmap(place)(both_x, target))
    ex_dy = by_expert(jax.vmap(place)(both_dy, target))
    ex_gate = by_expert(jax.vmap(place)(both_gate, target))

    def expert_step(operands):
        recv_x, recv_dy, recv_gate, weight_in, weight_out = operands
        pre_act = jnp.einsum("prd,df->prf", recv_x.astype(jnp.float32), weight_in.astype(jnp.float32))
        hidden = jax.nn.gelu(pre_act, approximate=False).astype(jnp.bfloat16)
        out_rows = jnp.einsum("prf,fd->prd", hidden.astype(jnp.float32), weight_out.astype(jnp.float32))
        dgate_rows = jnp.sum(recv_dy.astype(jnp.float32) * out_rows, axis=-1).astype(jnp.bfloat16)
        scaled = (recv_gate.astype(jnp.float32)[..., None] * recv_dy.astype(jnp.float32)).astype(jnp.bfloat16)
        d_hidden = jnp.einsum("prd,fd->prf", scaled.astype(jnp.float32), weight_out.astype(jnp.float32))
        d_pre = (d_hidden * slope_of(pre_act)).astype(jnp.bfloat16)
        dx_rows = jnp.einsum("prf,df->prd", d_pre.astype(jnp.float32), weight_in.astype(jnp.float32)).astype(jnp.bfloat16)
        part_in = jnp.einsum("prd,prf->pdf", recv_x.astype(jnp.float32), d_pre.astype(jnp.float32)).astype(jnp.bfloat16)
        part_out = jnp.einsum("prf,prd->pfd", hidden.astype(jnp.float32), scaled.astype(jnp.float32)).astype(jnp.bfloat16)
        grad_in = jnp.sum(part_in.astype(jnp.float32), axis=0).astype(jnp.bfloat16)
        grad_out = jnp.sum(part_out.astype(jnp.float32), axis=0).astype(jnp.bfloat16)
        return dx_rows, dgate_rows, grad_in, grad_out

    dx_rows, dgate_rows, grad_in, grad_out = lax.map(expert_step, (ex_x, ex_dy, ex_gate, proj_in, proj_out))

    def back_to_blocks(values):
        shaped = values.reshape((EXPERTS, N_DP, N_EXPERT, CAP) + values.shape[3:])
        moved = jnp.moveaxis(shaped, 0, 2)
        return moved.reshape((blocks, slots_all) + values.shape[3:])

    back_x = back_to_blocks(dx_rows)
    back_gate = back_to_blocks(dgate_rows)
    safe_target = jnp.minimum(target, slots_all - 1).astype(jnp.int32)
    taken_x = jax.vmap(lambda values, where_from: jnp.take(values, where_from, axis=0))(back_x, safe_target)
    taken_x = jnp.where(kept_mask[..., None], taken_x.astype(jnp.float32), 0.0)
    taken_gate = jax.vmap(lambda values, where_from: jnp.take(values, where_from, axis=0))(back_gate, safe_target)
    taken_gate = jnp.where(kept_mask, taken_gate.astype(jnp.float32), 0.0).astype(jnp.bfloat16)
    token_grads = (taken_x[:, :TOK_DEV] + taken_x[:, TOK_DEV:]).astype(jnp.bfloat16).reshape(TOKENS, D)
    gate_grads = jnp.stack([taken_gate[:, :TOK_DEV], taken_gate[:, TOK_DEV:]], axis=-1).reshape(TOKENS, 2)
    return token_grads, gate_grads, grad_in, grad_out
```

```python
import jax
import jax.numpy as jnp
from jax import lax
from jax.sharding import PartitionSpec as P


def slope_of(pre_act):
    gauss_cdf = 0.5 * (1.0 + jax.scipy.special.erf(pre_act * 0.7071067811865476))
    gauss_pdf = jnp.exp(-0.5 * pre_act * pre_act) * 0.3989422804014327
    return gauss_cdf + pre_act * gauss_pdf


def gather_groups(rows):
    groups = lax.axis_size("dp")
    swap = [(i, i ^ 1) for i in range(groups)]
    mine = [rows, lax.ppermute(rows, "dp", swap)]
    for k in range(1, groups // 2):
        other = lax.ppermute(rows, "dp", [(i, (i + 2 * k) % groups) for i in range(groups)])
        mine += [other, lax.ppermute(other, "dp", swap)]
    return mine


def local(tokens, cotangent, routes, gates, proj_in, proj_out):
    tok_count = tokens.shape[0]
    feat_width = tokens.shape[1]
    experts = lax.axis_size("expert")
    groups = lax.axis_size("dp")
    me = lax.axis_index("dp")
    capacity = 2 * tok_count // experts
    slots_all = experts * capacity
    weight_in = proj_in[0]
    weight_out = proj_out[0]
    ffw = weight_in.shape[1]
    chosen = jnp.concatenate([routes[:, 0], routes[:, 1]])
    one_hot = (chosen[:, None] == jnp.arange(experts, dtype=jnp.int32)[None, :]).astype(jnp.int32)
    earlier = jnp.cumsum(one_hot, axis=0) - one_hot
    slot_pos = jnp.sum(earlier * one_hot, axis=1)
    kept_mask = slot_pos < capacity
    target = jnp.where(kept_mask, chosen * capacity + slot_pos, slots_all)
    placing = (jnp.arange(slots_all, dtype=jnp.int32)[:, None] == target[None, :]).astype(
        jnp.bfloat16
    )
    either = placing[:, :tok_count] + placing[:, tok_count:]
    send_x = jnp.dot(either, tokens, preferred_element_type=jnp.float32).astype(jnp.bfloat16)
    scaled_tok = jnp.concatenate(
        [
            (gates[:, k : k + 1].astype(jnp.float32) * cotangent.astype(jnp.float32)).astype(
                jnp.bfloat16
            )
            for k in range(2)
        ],
        axis=0,
    )
    send_s = jnp.dot(placing, scaled_tok, preferred_element_type=jnp.float32).astype(jnp.bfloat16)

    def exchange(rows):
        return lax.all_to_all(
            rows.reshape(experts, capacity, rows.shape[1]),
            "expert",
            split_axis=0,
            concat_axis=0,
            tiled=True,
        ).reshape(slots_all, rows.shape[1])

    x_parts = gather_groups(exchange(send_x))
    s_parts = gather_groups(exchange(send_s))

    def forward(x, s):
        pre_act = jnp.dot(x, weight_in, preferred_element_type=jnp.float32)
        hidden = jax.nn.gelu(pre_act, approximate=False).astype(jnp.bfloat16)
        d_hidden = lax.dot_general(
            s, weight_out, (((1,), (1,)), ((), ())), preferred_element_type=jnp.float32
        )
        d_pre = (d_hidden * slope_of(pre_act)).astype(jnp.bfloat16)
        return hidden, d_hidden, d_pre

    hidden0, d_hidden0, d_pre0 = forward(x_parts[0], s_parts[0])
    dgate = jnp.sum(hidden0.astype(jnp.float32) * d_hidden0, axis=1, keepdims=True)
    dx_rows = lax.dot_general(
        d_pre0, weight_in, (((1,), (1,)), ((), ())), preferred_element_type=jnp.float32
    )
    back = exchange(
        jnp.concatenate([dx_rows, jnp.broadcast_to(dgate, (slots_all, 128))], axis=1).astype(
            jnp.bfloat16
        )
    )
    hidden1, _, d_pre1 = forward(
        jnp.concatenate(x_parts[1:], axis=0), jnp.concatenate(s_parts[1:], axis=0)
    )
    x_all = jnp.concatenate(x_parts, axis=0)
    s_all = jnp.concatenate(s_parts, axis=0)
    hidden = jnp.concatenate([hidden0, hidden1], axis=0)
    d_pre = jnp.concatenate([d_pre0, d_pre1], axis=0)
    x_cut = lax.dynamic_slice_in_dim(x_all, me * (feat_width // groups), feat_width // groups, 1)
    h_cut = lax.dynamic_slice_in_dim(hidden, me * (ffw // groups), ffw // groups, 1)
    grad_in = lax.dot_general(
        x_cut, d_pre, (((0,), (0,)), ((), ())), preferred_element_type=jnp.float32
    ).astype(jnp.bfloat16)
    grad_out = lax.dot_general(
        h_cut, s_all, (((0,), (0,)), ((), ())), preferred_element_type=jnp.float32
    ).astype(jnp.bfloat16)
    token_grads = lax.dot_general(
        either, back[:, :feat_width], (((0,), (0,)), ((), ())), preferred_element_type=jnp.float32
    ).astype(jnp.bfloat16)
    taken_gate = lax.dot_general(
        placing,
        back[:, feat_width : feat_width + 1],
        (((0,), (0,)), ((), ())),
        preferred_element_type=jnp.float32,
    )
    gate_grads = (
        jnp.concatenate([taken_gate[:tok_count], taken_gate[tok_count:]], axis=1)
        / gates.astype(jnp.float32)
    ).astype(jnp.bfloat16)
    return (token_grads, gate_grads, grad_in[None], grad_out[None])


def solution(mesh):
    placed = (
        P(("dp", "expert"), None),
        P(("dp", "expert"), None),
        P(("dp", "expert"), None),
        P(("dp", "expert"), None),
        P("expert", None, None),
        P("expert", None, None),
    )
    return jax.shard_map(
        local,
        mesh=mesh,
        in_specs=placed,
        out_specs=(
            P(("dp", "expert"), None),
            P(("dp", "expert"), None),
            P("expert", "dp", None),
            P("expert", "dp", None),
        ),
        check_vma=False,
    )
```

```python
import functools

import jax
import jax.numpy as jnp
from jax import lax
from jax.experimental import pallas as pl
from jax.experimental.pallas import tpu as pltpu
from jax.sharding import PartitionSpec as P

BF16 = jnp.bfloat16
F32 = jnp.float32
LANES = 128
MIB = 1 << 20


def dot(a, b, over=(1, 0)):
    return lax.dot_general(
        a, b, (((over[0],), (over[1],)), ((), ())), preferred_element_type=F32
    )


def gelu_and_slope(pre_act):
    cdf = 0.5 * (1.0 + lax.erf(pre_act * 0.7071067811865476))
    pdf = jnp.exp(-0.5 * pre_act * pre_act) * 0.3989422804014327
    return (pre_act * cdf).astype(BF16), cdf + pre_act * pdf


def call(kernel, out_shape, args, flops=0, limit=24, scratch=()):
    moved = sum(a.size * a.dtype.itemsize for a in args)
    return pl.pallas_call(
        kernel,
        out_shape=out_shape,
        in_specs=[pl.BlockSpec(memory_space=pltpu.VMEM)] * len(args),
        out_specs=jax.tree.map(lambda _: pl.BlockSpec(memory_space=pltpu.VMEM), out_shape),
        scratch_shapes=list(scratch),
        compiler_params=pltpu.CompilerParams(vmem_limit_bytes=limit * MIB),
        cost_estimate=pl.CostEstimate(flops=flops, bytes_accessed=moved, transcendentals=0),
    )(*args)


def shape(dims, dtype=BF16):
    return jax.ShapeDtypeStruct(dims, dtype)


def route_kernel(experts, capacity, routes, gates, tokens, cotangent, *outs):
    blocks_x, blocks_s = outs[:experts], outs[experts : 2 * experts]
    place_refs = outs[2 * experts :]
    tok_count = tokens.shape[0]
    slots_all = experts * capacity
    me = lax.axis_index("expert")
    rows = max(experts, 16)
    before = (
        lax.broadcasted_iota(jnp.int32, (tok_count, tok_count), 0)
        < lax.broadcasted_iota(jnp.int32, (tok_count, tok_count), 1)
    ).astype(F32).astype(BF16)
    expert_id = lax.broadcasted_iota(jnp.int32, (rows, tok_count), 0)
    slot_id = lax.broadcasted_iota(jnp.int32, (slots_all, tok_count), 0)
    taken = jnp.zeros((rows, 1), F32)
    places, gated = [], jnp.zeros((slots_all, tok_count), F32)
    for choice in range(2):
        chosen = routes[choice : choice + 1, :]
        one_hot = (expert_id == chosen).astype(F32)
        earlier = dot(one_hot.astype(BF16), before) + taken
        taken = taken + jnp.sum(one_hot, axis=1, keepdims=True)
        slot_pos = jnp.sum(earlier * one_hot, axis=0, keepdims=True).astype(jnp.int32)
        target = jnp.where(
            slot_pos < capacity, jnp.bitwise_xor(chosen, me) * capacity + slot_pos, slots_all
        )
        place = (slot_id == target).astype(F32)
        place_refs[choice][...] = place.astype(BF16)
        places.append(place)
        gated = gated + place * gates[choice : choice + 1, :].astype(F32)
    x = dot((places[0] + places[1]).astype(BF16), tokens[...]).astype(BF16)
    s = dot(gated.astype(BF16), cotangent[...]).astype(BF16)
    for k in range(experts):
        blocks_x[k][...] = x[k * capacity : (k + 1) * capacity]
        blocks_s[k][...] = s[k * capacity : (k + 1) * capacity]


def combine_kernel(experts, capacity, place0, place1, gates, *refs):
    blocks, (token_grads, gate_grads, rows) = refs[:experts], refs[experts:]
    tok_count, feat_width = token_grads.shape
    for k in range(experts):
        rows[k * capacity : (k + 1) * capacity, :] = blocks[k][...]
    either = (place0[...].astype(F32) + place1[...].astype(F32)).astype(BF16)
    token_grads[...] = dot(either, rows[:, :feat_width], (0, 0)).astype(BF16)
    dgate = rows[:, feat_width : feat_width + tok_count].astype(F32)
    for choice, place in ((0, place0), (1, place1)):
        row = jnp.sum(place[...].astype(F32) * dgate, axis=0, keepdims=True)
        gate_grads[choice : choice + 1, :] = row / gates[choice : choice + 1, :].astype(F32)


def up_kernel(tile, *refs):
    *x_refs, weight_in, hidden, slope = refs
    for at in range(0, weight_in.shape[1], tile):
        cols = slice(at, at + tile)
        weight = weight_in[:, cols]
        for g, x in enumerate(x_refs):
            rows = slice(g * x.shape[0], (g + 1) * x.shape[0])
            hidden[rows, cols], slope[rows, cols] = gelu_and_slope(dot(x[...], weight))


def own_kernel(tile, experts, s, hidden, slope, weight_in, weight_out, d_pre, *blocks):
    slots_all, feat_width = s.shape
    capacity = slots_all // experts
    dgate = jnp.zeros((slots_all, LANES), F32)
    dx = jnp.zeros((slots_all, feat_width), F32)
    for at in range(0, weight_in.shape[1], tile):
        cols = slice(at, at + tile)
        d_hidden = dot(s[...], weight_out[cols, :], (1, 1))
        part = (d_hidden * slope[:, cols]).astype(BF16)
        d_pre[:, cols] = part
        product = d_hidden * hidden[:, cols].astype(F32)
        for lane in range(0, tile, LANES):
            dgate = dgate + product[:, lane : lane + LANES]
        dx = dx + dot(part, weight_in[:, cols], (1, 1))
    dgate = jnp.broadcast_to(jnp.sum(dgate, axis=1, keepdims=True), (slots_all, LANES))
    for k in range(experts):
        rows = slice(k * capacity, (k + 1) * capacity)
        blocks[k][:, :feat_width] = dx[rows].astype(BF16)
        blocks[k][:, feat_width:] = dgate[rows].astype(BF16)


def grads_kernel(tile, groups, *refs):
    x_refs, s_refs, refs = refs[:groups], refs[groups : 2 * groups], refs[2 * groups :]
    hidden0, d_pre0, hidden1, slope1, weight_out, grad_in, grad_out = refs[:7]
    x_cut, s_all, d_pre = refs[7:]
    me = lax.axis_index("dp")
    slots_all = s_refs[0].shape[0]
    cut = x_cut.shape[1]
    ffw = weight_out.shape[0]
    for g in range(groups):
        rows = slice(g * slots_all, (g + 1) * slots_all)
        x_cut[rows, :] = x_refs[g][:, pl.ds(pl.multiple_of(me * cut, cut), cut)]
        s_all[rows, :] = s_refs[g][...]
    d_pre[:slots_all, :] = d_pre0[...]
    for at in range(0, ffw, tile):
        cols = slice(at, at + tile)
        d_hidden = dot(s_all[slots_all:, :], weight_out[cols, :], (1, 1))
        d_pre[slots_all:, cols] = (d_hidden * slope1[:, cols]).astype(BF16)
        grad_in[:, cols] = dot(x_cut[...], d_pre[:, cols], (0, 0)).astype(BF16)
    mine = pl.ds(pl.multiple_of(me * (ffw // groups), ffw // groups), ffw // groups)
    h_cut = jnp.concatenate([hidden0[:, mine], hidden1[:, mine]], axis=0)
    grad_out[...] = dot(h_cut, s_all[...], (0, 0)).astype(BF16)


def exchange(blocks):
    experts = len(blocks)
    return [blocks[0]] + [
        lax.ppermute(blocks[k], "expert", [(i, i ^ k) for i in range(experts)])
        for k in range(1, experts)
    ]


def gather_groups(rows):
    groups = lax.axis_size("dp")
    swap = [(i, i ^ 1) for i in range(groups)]
    others = [lax.ppermute(rows, "dp", swap)]
    for k in range(1, groups // 2):
        other = lax.ppermute(rows, "dp", [(i, (i + 2 * k) % groups) for i in range(groups)])
        others += [other, lax.ppermute(other, "dp", swap)]
    return others


def local(tokens, cotangent, routes, gates, proj_in, proj_out):
    tok_count, feat_width = tokens.shape
    experts = lax.axis_size("expert")
    groups = lax.axis_size("dp")
    capacity = 2 * tok_count // experts
    slots_all = experts * capacity
    weight_in = pltpu.with_memory_space_constraint(proj_in[0], pltpu.VMEM)
    weight_out = pltpu.with_memory_space_constraint(proj_out[0], pltpu.VMEM)
    ffw = weight_in.shape[1]
    tile = ffw // groups
    product = 2 * slots_all * feat_width * ffw
    block = shape((capacity, feat_width))
    place = shape((slots_all, tok_count))

    routed = call(
        functools.partial(route_kernel, experts, capacity),
        [block] * (2 * experts) + [place] * 2,
        [routes.T, gates.T, tokens, cotangent],
    )
    places = routed[2 * experts :]
    got_x = exchange(routed[:experts])
    got_s = exchange(routed[experts : 2 * experts])
    x = jnp.concatenate(got_x, axis=0)
    x_others = gather_groups(x)
    s = jnp.concatenate(got_s, axis=0)
    s_others = gather_groups(s)
    hidden0, slope0 = call(
        functools.partial(up_kernel, tile),
        [shape((slots_all, ffw)), shape((slots_all, ffw), F32)],
        [x, weight_in],
        product,
    )
    d_pre0, *back = call(
        functools.partial(own_kernel, tile, experts),
        [shape((slots_all, ffw))] + [shape((capacity, feat_width + LANES))] * experts,
        [s, hidden0, slope0, weight_in, weight_out],
        2 * product,
    )
    back = exchange(back)
    others = groups - 1
    hidden1, slope1 = call(
        functools.partial(up_kernel, tile),
        [shape((others * slots_all, ffw)), shape((others * slots_all, ffw), F32)],
        [*x_others, weight_in],
        others * product,
    )
    grad_in, grad_out = call(
        functools.partial(grads_kernel, tile, groups),
        [shape((feat_width // groups, ffw)), shape((ffw // groups, feat_width))],
        [x, *x_others, s, *s_others, hidden0, d_pre0, hidden1, slope1, weight_out],
        (others + 2) * product,
        scratch=[
            pltpu.VMEM((groups * slots_all, feat_width // groups), BF16),
            pltpu.VMEM((groups * slots_all, feat_width), BF16),
            pltpu.VMEM((groups * slots_all, ffw), BF16),
        ],
    )
    token_grads, gate_grads = call(
        functools.partial(combine_kernel, experts, capacity),
        [shape((tok_count, feat_width)), shape((2, tok_count), F32)],
        [*places, gates.T, *back],
        scratch=[pltpu.VMEM((slots_all, feat_width + LANES), BF16)],
    )
    return (token_grads, gate_grads.T.astype(BF16), grad_in[None], grad_out[None])


def local_small_blocks(tokens, cotangent, routes, gates, proj_in, proj_out):
    tok_count, feat_width = tokens.shape
    experts = lax.axis_size("expert")
    groups = lax.axis_size("dp")
    me = lax.axis_index("dp")
    capacity = 2 * tok_count // experts
    slots_all = experts * capacity
    weight_in, weight_out = proj_in[0], proj_out[0]
    ffw = weight_in.shape[1]
    chosen = jnp.concatenate([routes[:, 0], routes[:, 1]])
    one_hot = (chosen[:, None] == jnp.arange(experts, dtype=jnp.int32)[None, :]).astype(jnp.int32)
    slot_pos = jnp.sum((jnp.cumsum(one_hot, axis=0) - one_hot) * one_hot, axis=1)
    target = jnp.where(slot_pos < capacity, chosen * capacity + slot_pos, slots_all)
    placing = (jnp.arange(slots_all, dtype=jnp.int32)[:, None] == target[None, :]).astype(BF16)
    either = placing[:, :tok_count] + placing[:, tok_count:]
    scaled = [
        (gates[:, k : k + 1].astype(F32) * cotangent.astype(F32)).astype(BF16) for k in range(2)
    ]

    def swap_blocks(rows):
        return lax.all_to_all(
            rows.astype(BF16).reshape(experts, capacity, rows.shape[1]), "expert", 0, 0, tiled=True
        ).reshape(slots_all, rows.shape[1])

    x = swap_blocks(dot(either, tokens))
    s = swap_blocks(dot(placing, jnp.concatenate(scaled, axis=0)))
    hidden0, slope0 = gelu_and_slope(dot(x, weight_in))
    d_hidden0 = dot(s, weight_out, (1, 1))
    d_pre0 = (d_hidden0 * slope0).astype(BF16)
    dgate = jnp.sum(hidden0.astype(F32) * d_hidden0, axis=1, keepdims=True)
    dx = dot(d_pre0, weight_in, (1, 1))
    back = swap_blocks(
        jnp.concatenate([dx, jnp.broadcast_to(dgate, (slots_all, LANES))], axis=1)
    )
    x_all = jnp.concatenate([x, *gather_groups(x)], axis=0)
    s_all = jnp.concatenate([s, *gather_groups(s)], axis=0)
    hidden1, slope1 = gelu_and_slope(dot(x_all[slots_all:], weight_in))
    d_pre1 = (dot(s_all[slots_all:], weight_out, (1, 1)) * slope1).astype(BF16)
    hidden = jnp.concatenate([hidden0, hidden1], axis=0)
    d_pre = jnp.concatenate([d_pre0, d_pre1], axis=0)
    x_cut = lax.dynamic_slice_in_dim(x_all, me * (feat_width // groups), feat_width // groups, 1)
    h_cut = lax.dynamic_slice_in_dim(hidden, me * (ffw // groups), ffw // groups, 1)
    grad_in = dot(x_cut, d_pre, (0, 0)).astype(BF16)
    grad_out = dot(h_cut, s_all, (0, 0)).astype(BF16)
    token_grads = dot(either, back[:, :feat_width], (0, 0)).astype(BF16)
    taken = dot(placing, back[:, feat_width : feat_width + 1], (0, 0))
    gate_grads = jnp.concatenate([taken[:tok_count], taken[tok_count:]], axis=1)
    gate_grads = (gate_grads / gates.astype(F32)).astype(BF16)
    return (token_grads, gate_grads, grad_in[None], grad_out[None])


def solution(mesh):
    rows = P(("dp", "expert"), None)
    weights = P("expert", None, None)

    def whole(tokens, *others):
        experts = mesh.shape["expert"]
        capacity = 2 * tokens.shape[0] // (mesh.shape["dp"] * experts) // experts
        tiles = capacity % 16 == 0 and experts & (experts - 1) == 0
        return jax.shard_map(
            local if tiles else local_small_blocks,
            mesh=mesh,
            in_specs=(rows, rows, rows, rows, weights, weights),
            out_specs=(rows, rows, P("expert", "dp", None), P("expert", "dp", None)),
            check_vma=False,
        )(tokens, *others)

    return whole
```

```python
import functools

import jax
import jax.numpy as jnp
from jax import lax
from jax.experimental import pallas as pl
from jax.experimental.pallas import tpu as pltpu
from jax.sharding import PartitionSpec as P

BF16 = jnp.bfloat16
F32 = jnp.float32
LANES = 128
MIB = 1 << 20


def dot(a, b, over=(1, 0)):
    return lax.dot_general(
        a, b, (((over[0],), (over[1],)), ((), ())), preferred_element_type=F32
    )


def gelu_and_slope(pre_act):
    cdf = 0.5 * (1.0 + lax.erf(pre_act * 0.7071067811865476))
    pdf = jnp.exp(-0.5 * pre_act * pre_act) * 0.3989422804014327
    return (pre_act * cdf).astype(BF16), cdf + pre_act * pdf


def call(kernel, out_shape, args, flops=0, limit=24, scratch=(), in_space=pltpu.VMEM):
    moved = sum(a.size * a.dtype.itemsize for a in args)
    if in_space == pltpu.HBM:
        args = [pltpu.with_memory_space_constraint(a, pltpu.HBM) for a in args]
    return pl.pallas_call(
        kernel,
        out_shape=out_shape,
        in_specs=[pl.BlockSpec(memory_space=in_space)] * len(args),
        out_specs=jax.tree.map(lambda _: pl.BlockSpec(memory_space=pltpu.VMEM), out_shape),
        scratch_shapes=list(scratch),
        compiler_params=pltpu.CompilerParams(vmem_limit_bytes=limit * MIB),
        cost_estimate=pl.CostEstimate(flops=flops, bytes_accessed=moved, transcendentals=0),
    )(*args)


def shape(dims, dtype=BF16):
    return jax.ShapeDtypeStruct(dims, dtype)


def route_kernel(experts, capacity, routes_hbm, gates_hbm, tokens_hbm, cotangent_hbm, *refs):
    blocks, place_refs, scratch = refs[:experts], refs[experts : experts + 2], refs[experts + 2 :]
    routes, gates, tokens, cotangent, sems = scratch
    copies = [
        pltpu.make_async_copy(source, target, sems.at[i])
        for i, (source, target) in enumerate(
            (
                (routes_hbm, routes),
                (gates_hbm, gates),
                (tokens_hbm, tokens),
                (cotangent_hbm, cotangent),
            )
        )
    ]
    for copy in copies:
        copy.start()
    tok_count, feat_width = tokens.shape
    slots_all = experts * capacity
    me = lax.axis_index("expert")
    rows = max(experts, 16)
    before = (
        lax.broadcasted_iota(jnp.int32, (tok_count, tok_count), 0)
        < lax.broadcasted_iota(jnp.int32, (tok_count, tok_count), 1)
    ).astype(F32).astype(BF16)
    expert_id = lax.broadcasted_iota(jnp.int32, (rows, tok_count), 0)
    slot_id = lax.broadcasted_iota(jnp.int32, (slots_all, tok_count), 0)
    taken = jnp.zeros((rows, 1), F32)
    places, gated = [], jnp.zeros((slots_all, tok_count), F32)
    copies[0].wait()
    copies[1].wait()
    for choice in range(2):
        chosen = routes[choice : choice + 1, :]
        one_hot = (expert_id == chosen).astype(F32)
        earlier = dot(one_hot.astype(BF16), before) + taken
        taken = taken + jnp.sum(one_hot, axis=1, keepdims=True)
        slot_pos = jnp.sum(earlier * one_hot, axis=0, keepdims=True).astype(jnp.int32)
        target = jnp.where(
            slot_pos < capacity, jnp.bitwise_xor(chosen, me) * capacity + slot_pos, slots_all
        )
        place = (slot_id == target).astype(F32)
        place_refs[choice][...] = place.astype(BF16)
        places.append(place)
        gated = gated + place * gates[choice : choice + 1, :].astype(F32)
    copies[2].wait()
    x = dot((places[0] + places[1]).astype(BF16), tokens[...]).astype(BF16)
    copies[3].wait()
    s = dot(gated.astype(BF16), cotangent[...]).astype(BF16)
    for k in range(experts):
        blocks[k][:, :feat_width] = x[k * capacity : (k + 1) * capacity]
        blocks[k][:, feat_width:] = s[k * capacity : (k + 1) * capacity]


def load_kernel(in_hbm, out_hbm, weight_in, weight_out, sems):
    copies = [
        pltpu.make_async_copy(source, target, sems.at[i])
        for i, (source, target) in enumerate(((in_hbm, weight_in), (out_hbm, weight_out)))
    ]
    for copy in copies:
        copy.start()
    for copy in copies:
        copy.wait()


def combine_kernel(experts, capacity, place0, place1, gates, *refs):
    blocks, (token_grads, gate_grads, rows) = refs[:experts], refs[experts:]
    tok_count, feat_width = token_grads.shape
    for k in range(experts):
        rows[k * capacity : (k + 1) * capacity, :] = blocks[k][...]
    either = (place0[...].astype(F32) + place1[...].astype(F32)).astype(BF16)
    token_grads[...] = dot(either, rows[:, :feat_width], (0, 0)).astype(BF16)
    dgate = rows[:, feat_width : feat_width + tok_count].astype(F32)
    for choice, place in ((0, place0), (1, place1)):
        row = jnp.sum(place[...].astype(F32) * dgate, axis=0, keepdims=True)
        gate_grads[choice : choice + 1, :] = row / gates[choice : choice + 1, :].astype(F32)


def stack(refs, part, width):
    return jnp.concatenate([ref[:, part * width : (part + 1) * width] for ref in refs], axis=0)


def my_part(ref):
    width = ref.shape[1] // lax.axis_size("dp")
    return ref[:, pl.ds(pl.multiple_of(lax.axis_index("dp") * width, width), width)]


def own_kernel(tile, pieces, experts, *refs):
    row_refs, (weight_in, weight_out, d_pre, h_cut, *blocks, hidden) = (
        refs[:pieces],
        refs[pieces:],
    )
    feat_width, ffw = weight_in.shape
    x, s = stack(row_refs, 0, feat_width), stack(row_refs, 1, feat_width)
    slots_all = x.shape[0]
    capacity = slots_all // experts
    dgate = jnp.zeros((slots_all, LANES), F32)
    dx = jnp.zeros((slots_all, feat_width), F32)
    for at in range(0, ffw, tile):
        cols = slice(at, at + tile)
        act, slope = gelu_and_slope(dot(x, weight_in[:, cols]))
        hidden[:, cols] = act
        d_hidden = dot(s, weight_out[cols, :], (1, 1))
        part = (d_hidden * slope).astype(BF16)
        d_pre[:, cols] = part
        product = d_hidden * act.astype(F32)
        for lane in range(0, tile, LANES):
            dgate = dgate + product[:, lane : lane + LANES]
        dx = dx + dot(part, weight_in[:, cols], (1, 1))
    h_cut[...] = my_part(hidden)
    dgate = jnp.broadcast_to(jnp.sum(dgate, axis=1, keepdims=True), (slots_all, LANES))
    for k in range(experts):
        rows = slice(k * capacity, (k + 1) * capacity)
        blocks[k][:, :feat_width] = dx[rows].astype(BF16)
        blocks[k][:, feat_width:] = dgate[rows].astype(BF16)


def backward_tiles(tile, x, s, weight_in, weight_out, hidden, d_pre, rows):
    for at in range(0, weight_in.shape[1], tile):
        cols = slice(at, at + tile)
        act, slope = gelu_and_slope(dot(x, weight_in[:, cols]))
        hidden[:, cols] = act
        d_pre[rows, cols] = (dot(s, weight_out[cols, :], (1, 1)) * slope).astype(BF16)


def early_kernel(tile, pieces, *refs):
    row_refs, (weight_in, weight_out, d_pre, h_cut, hidden) = refs[:pieces], refs[pieces:]
    width = weight_in.shape[0]
    x, s = stack(row_refs, 0, width), stack(row_refs, 1, width)
    backward_tiles(tile, x, s, weight_in, weight_out, hidden, d_pre, slice(None))
    h_cut[...] = my_part(hidden)


def grads_kernel(tile, own, early, late, *refs):
    pieces = own + early + late
    row_refs, refs = refs[:pieces], refs[pieces:]
    d_pre0, h_cut0, d_pre1, h_cut1, weight_in, weight_out, grad_in, grad_out = refs[:8]
    hidden, d_pre = refs[8:]
    width, ffw = weight_in.shape
    x, s = stack(row_refs[-late:], 0, width), stack(row_refs[-late:], 1, width)
    first, second = d_pre0.shape[0], d_pre0.shape[0] + d_pre1.shape[0]
    d_pre[:first, :] = d_pre0[...]
    d_pre[first:second, :] = d_pre1[...]
    cut = grad_in.shape[0]
    mine = pl.ds(pl.multiple_of(lax.axis_index("dp") * cut, cut), cut)
    x_cut = jnp.concatenate([ref[:, mine] for ref in row_refs], axis=0)
    backward_tiles(tile, x, s, weight_in, weight_out, hidden, d_pre, slice(second, None))
    for at in range(0, ffw, tile):
        cols = slice(at, at + tile)
        grad_in[:, cols] = dot(x_cut, d_pre[:, cols], (0, 0)).astype(BF16)
    h_cut = jnp.concatenate([h_cut0[...], h_cut1[...], my_part(hidden)], axis=0)
    grad_out[...] = dot(h_cut, stack(row_refs, 1, width), (0, 0)).astype(BF16)


def after(value, *first):
    return lax.optimization_barrier((value, *first))[0]


def permute(block, k):
    return lax.ppermute(block, "expert", [(i, i ^ k) for i in range(lax.axis_size("expert"))])


def swap_cores(rows):
    return lax.ppermute(rows, "dp", [(i, i ^ 1) for i in range(lax.axis_size("dp"))])


def shift_chips(rows, k):
    groups = lax.axis_size("dp")
    return lax.ppermute(rows, "dp", [(i, (i + 2 * k) % groups) for i in range(groups)])


def gather_groups(rows):
    others = [swap_cores(rows)]
    for k in range(1, lax.axis_size("dp") // 2):
        other = shift_chips(rows, k)
        others += [other, swap_cores(other)]
    return others


def local(tokens, cotangent, routes, gates, proj_in, proj_out):
    tok_count, feat_width = tokens.shape
    experts = lax.axis_size("expert")
    groups = lax.axis_size("dp")
    capacity = 2 * tok_count // experts
    slots_all = experts * capacity
    half = experts // 2
    ffw = proj_in.shape[2]
    tile = ffw // groups
    product = 2 * slots_all * feat_width * ffw
    place = shape((slots_all, tok_count))

    routed = call(
        functools.partial(route_kernel, experts, capacity),
        [shape((capacity, 2 * feat_width))] * experts + [place] * 2,
        [routes.T, gates.T, tokens, cotangent],
        in_space=pltpu.HBM,
        scratch=[
            pltpu.VMEM((2, tok_count), jnp.int32),
            pltpu.VMEM((2, tok_count), BF16),
            pltpu.VMEM((tok_count, feat_width), BF16),
            pltpu.VMEM((tok_count, feat_width), BF16),
            pltpu.SemaphoreType.DMA((4,)),
        ],
    )
    blocks, places = routed[:experts], routed[experts:]
    weight_in, weight_out = call(
        load_kernel,
        [pltpu.VMEM((feat_width, ffw), BF16), pltpu.VMEM((ffw, feat_width), BF16)],
        [after(proj_in[0], places[0]), after(proj_out[0], places[0])],
        in_space=pltpu.HBM,
        scratch=[pltpu.SemaphoreType.DMA((2,))],
    )
    weights = [
        pltpu.with_memory_space_constraint(w, pltpu.VMEM) for w in (weight_in, weight_out)
    ]
    got = {0: blocks[0]}
    near = list(range(1, half))
    far = list(range(half, experts))
    first, second = far[len(far) // 2 :], far[: len(far) // 2]
    for k in near + first:
        got[k] = permute(blocks[k], k)
    for k in second:
        got[k] = permute(after(blocks[k], *[got[j] for j in near]), k)
    rows_a = jnp.concatenate([got[k] for k in range(half)], axis=0)
    rows_b = jnp.concatenate([got[k] for k in range(half, experts)], axis=0)
    core_a = swap_cores(rows_a)
    chips_a = [shift_chips(rows_a, k) for k in range(1, groups // 2)]
    rows_b = after(rows_b, core_a)
    chips_b = [shift_chips(rows_b, k) for k in range(1, groups // 2)]
    d_pre0, h_cut0, *back = call(
        functools.partial(own_kernel, tile, 2, experts),
        [shape((slots_all, ffw)), shape((slots_all, tile))]
        + [shape((capacity, feat_width + LANES))] * experts,
        [rows_a, rows_b, *weights],
        3 * product,
        scratch=[pltpu.VMEM((slots_all, ffw), BF16)],
    )
    relayed_a = [swap_cores(after(rows, d_pre0)) for rows in chips_a]
    core_b = swap_cores(after(rows_b, d_pre0))
    early = [core_a, core_b, *chips_a, *relayed_a]
    early_rows = sum(piece.shape[0] for piece in early)
    d_pre1, h_cut1 = call(
        functools.partial(early_kernel, tile, len(early)),
        [shape((early_rows, ffw)), shape((early_rows, tile))],
        [*early, *weights],
        2 * product * early_rows // slots_all,
        scratch=[pltpu.VMEM((early_rows, ffw), BF16)],
    )
    returned = {0: back[0]}
    for k in first:
        returned[k] = permute(back[k], k)
    for k in second:
        returned[k] = permute(after(back[k], core_b, *relayed_a), k)
    for k in near:
        returned[k] = permute(after(back[k], d_pre1), k)
    back = [returned[k] for k in range(experts)]
    chips_b += [swap_cores(rows) for rows in chips_b]
    late_rows = sum(piece.shape[0] for piece in chips_b)
    grad_in, grad_out = call(
        functools.partial(grads_kernel, tile, 2, len(early), len(chips_b)),
        [shape((feat_width // groups, ffw)), shape((ffw // groups, feat_width))],
        [rows_a, rows_b, *early, *chips_b, d_pre0, h_cut0, d_pre1, h_cut1, *weights],
        4 * product,
        scratch=[
            pltpu.VMEM((late_rows, ffw), BF16),
            pltpu.VMEM((groups * slots_all, ffw), BF16),
        ],
    )
    token_grads, gate_grads = call(
        functools.partial(combine_kernel, experts, capacity),
        [shape((tok_count, feat_width)), shape((2, tok_count), F32)],
        [*places, gates.T, *back],
        scratch=[pltpu.VMEM((slots_all, feat_width + LANES), BF16)],
    )
    return (token_grads, gate_grads.T.astype(BF16), grad_in[None], grad_out[None])


def local_small_blocks(tokens, cotangent, routes, gates, proj_in, proj_out):
    tok_count, feat_width = tokens.shape
    experts = lax.axis_size("expert")
    groups = lax.axis_size("dp")
    me = lax.axis_index("dp")
    capacity = 2 * tok_count // experts
    slots_all = experts * capacity
    weight_in, weight_out = proj_in[0], proj_out[0]
    ffw = weight_in.shape[1]
    chosen = jnp.concatenate([routes[:, 0], routes[:, 1]])
    one_hot = (chosen[:, None] == jnp.arange(experts, dtype=jnp.int32)[None, :]).astype(jnp.int32)
    slot_pos = jnp.sum((jnp.cumsum(one_hot, axis=0) - one_hot) * one_hot, axis=1)
    target = jnp.where(slot_pos < capacity, chosen * capacity + slot_pos, slots_all)
    placing = (jnp.arange(slots_all, dtype=jnp.int32)[:, None] == target[None, :]).astype(BF16)
    either = placing[:, :tok_count] + placing[:, tok_count:]
    scaled = [
        (gates[:, k : k + 1].astype(F32) * cotangent.astype(F32)).astype(BF16) for k in range(2)
    ]

    def swap_blocks(rows):
        return lax.all_to_all(
            rows.astype(BF16).reshape(experts, capacity, rows.shape[1]), "expert", 0, 0, tiled=True
        ).reshape(slots_all, rows.shape[1])

    x = swap_blocks(dot(either, tokens))
    s = swap_blocks(dot(placing, jnp.concatenate(scaled, axis=0)))
    hidden0, slope0 = gelu_and_slope(dot(x, weight_in))
    d_hidden0 = dot(s, weight_out, (1, 1))
    d_pre0 = (d_hidden0 * slope0).astype(BF16)
    dgate = jnp.sum(hidden0.astype(F32) * d_hidden0, axis=1, keepdims=True)
    dx = dot(d_pre0, weight_in, (1, 1))
    back = swap_blocks(
        jnp.concatenate([dx, jnp.broadcast_to(dgate, (slots_all, LANES))], axis=1)
    )
    x_all = jnp.concatenate([x, *gather_groups(x)], axis=0)
    s_all = jnp.concatenate([s, *gather_groups(s)], axis=0)
    hidden1, slope1 = gelu_and_slope(dot(x_all[slots_all:], weight_in))
    d_pre1 = (dot(s_all[slots_all:], weight_out, (1, 1)) * slope1).astype(BF16)
    hidden = jnp.concatenate([hidden0, hidden1], axis=0)
    d_pre = jnp.concatenate([d_pre0, d_pre1], axis=0)
    x_cut = lax.dynamic_slice_in_dim(x_all, me * (feat_width // groups), feat_width // groups, 1)
    h_cut = lax.dynamic_slice_in_dim(hidden, me * (ffw // groups), ffw // groups, 1)
    grad_in = dot(x_cut, d_pre, (0, 0)).astype(BF16)
    grad_out = dot(h_cut, s_all, (0, 0)).astype(BF16)
    token_grads = dot(either, back[:, :feat_width], (0, 0)).astype(BF16)
    taken = dot(placing, back[:, feat_width : feat_width + 1], (0, 0))
    gate_grads = jnp.concatenate([taken[:tok_count], taken[tok_count:]], axis=1)
    gate_grads = (gate_grads / gates.astype(F32)).astype(BF16)
    return (token_grads, gate_grads, grad_in[None], grad_out[None])


def solution(mesh):
    rows = P(("dp", "expert"), None)
    weights = P("expert", None, None)

    def whole(tokens, *others):
        experts = mesh.shape["expert"]
        capacity = 2 * tokens.shape[0] // (mesh.shape["dp"] * experts) // experts
        tiles = capacity % 16 == 0 and experts & (experts - 1) == 0
        return jax.shard_map(
            local if tiles else local_small_blocks,
            mesh=mesh,
            in_specs=(rows, rows, rows, rows, weights, weights),
            out_specs=(rows, rows, P("expert", "dp", None), P("expert", "dp", None)),
            check_vma=False,
        )(tokens, *others)

    return whole
```

```python
import functools

import jax
import jax.numpy as jnp
from jax import lax
from jax.experimental import pallas as pl
from jax.experimental.pallas import tpu as pltpu
from jax.sharding import PartitionSpec as P

BF16 = jnp.bfloat16
F32 = jnp.float32
LANES = 128
MIB = 1 << 20


def dot(a, b, over=(1, 0)):
    return lax.dot_general(
        a, b, (((over[0],), (over[1],)), ((), ())), preferred_element_type=F32
    )


def gelu_and_slope(pre_act):
    cdf = 0.5 * (1.0 + lax.erf(pre_act * 0.7071067811865476))
    pdf = jnp.exp(-0.5 * pre_act * pre_act) * 0.3989422804014327
    return (pre_act * cdf).astype(BF16), cdf + pre_act * pdf


def call(kernel, out_shape, args, flops=0, limit=24, scratch=(), in_space=pltpu.VMEM):
    moved = sum(a.size * a.dtype.itemsize for a in args)
    if in_space == pltpu.HBM:
        args = [pltpu.with_memory_space_constraint(a, pltpu.HBM) for a in args]
    return pl.pallas_call(
        kernel,
        out_shape=out_shape,
        in_specs=[pl.BlockSpec(memory_space=in_space)] * len(args),
        out_specs=jax.tree.map(lambda _: pl.BlockSpec(memory_space=pltpu.VMEM), out_shape),
        scratch_shapes=list(scratch),
        compiler_params=pltpu.CompilerParams(vmem_limit_bytes=limit * MIB),
        cost_estimate=pl.CostEstimate(flops=flops, bytes_accessed=moved, transcendentals=0),
    )(*args)


def shape(dims, dtype=BF16):
    return jax.ShapeDtypeStruct(dims, dtype)


def route_kernel(experts, capacity, routes_hbm, gates_hbm, tokens_hbm, cotangent_hbm, *refs):
    blocks, place_refs, scratch = refs[:experts], refs[experts : experts + 2], refs[experts + 2 :]
    routes, gates, tokens, cotangent, sems = scratch
    copies = [
        pltpu.make_async_copy(source, target, sems.at[i])
        for i, (source, target) in enumerate(
            (
                (routes_hbm, routes),
                (gates_hbm, gates),
                (tokens_hbm, tokens),
                (cotangent_hbm, cotangent),
            )
        )
    ]
    for copy in copies:
        copy.start()
    tok_count, feat_width = tokens.shape
    slots_all = experts * capacity
    me = lax.axis_index("expert")
    rows = max(experts, 16)
    before = (
        lax.broadcasted_iota(jnp.int32, (tok_count, tok_count), 0)
        < lax.broadcasted_iota(jnp.int32, (tok_count, tok_count), 1)
    ).astype(F32).astype(BF16)
    expert_id = lax.broadcasted_iota(jnp.int32, (rows, tok_count), 0)
    slot_id = lax.broadcasted_iota(jnp.int32, (slots_all, tok_count), 0)
    taken = jnp.zeros((rows, 1), F32)
    places, gated = [], jnp.zeros((slots_all, tok_count), F32)
    copies[0].wait()
    copies[1].wait()
    for choice in range(2):
        chosen = routes[choice : choice + 1, :]
        one_hot = (expert_id == chosen).astype(F32)
        earlier = dot(one_hot.astype(BF16), before) + taken
        taken = taken + jnp.sum(one_hot, axis=1, keepdims=True)
        slot_pos = jnp.sum(earlier * one_hot, axis=0, keepdims=True).astype(jnp.int32)
        target = jnp.where(
            slot_pos < capacity, jnp.bitwise_xor(chosen, me) * capacity + slot_pos, slots_all
        )
        place = (slot_id == target).astype(F32)
        place_refs[choice][...] = place.astype(BF16)
        places.append(place)
        gated = gated + place * gates[choice : choice + 1, :].astype(F32)
    copies[2].wait()
    x = dot((places[0] + places[1]).astype(BF16), tokens[...]).astype(BF16)
    copies[3].wait()
    s = dot(gated.astype(BF16), cotangent[...]).astype(BF16)
    for k in range(experts):
        blocks[k][:, :feat_width] = x[k * capacity : (k + 1) * capacity]
        blocks[k][:, feat_width:] = s[k * capacity : (k + 1) * capacity]


def block_rows(me, k, capacity):
    return pl.ds(pl.multiple_of(jnp.bitwise_xor(me, k) * capacity, capacity), capacity)


def load_kernel(in_hbm, out_hbm, weight_in, weight_out, sems):
    copies = [
        pltpu.make_async_copy(source, target, sems.at[i])
        for i, (source, target) in enumerate(((in_hbm, weight_in), (out_hbm, weight_out)))
    ]
    for copy in copies:
        copy.start()
    for copy in copies:
        copy.wait()


def combine_kernel(experts, capacity, place0, place1, gates, back, token_grads, gate_grads, rows):
    tok_count, feat_width = token_grads.shape
    me = lax.axis_index("expert")
    for k in range(experts):
        rows[k * capacity : (k + 1) * capacity, :] = back[block_rows(me, k, capacity), :]
    either = (place0[...].astype(F32) + place1[...].astype(F32)).astype(BF16)
    token_grads[...] = dot(either, rows[:, :feat_width], (0, 0)).astype(BF16)
    dgate = rows[:, feat_width : feat_width + tok_count].astype(F32)
    taken = [
        jnp.sum(place[...].astype(F32) * dgate, axis=0, keepdims=True) for place in (place0, place1)
    ]
    gate_grads[...] = (jnp.concatenate(taken, axis=0) / gates[...].astype(F32)).astype(BF16)


def stack(refs, part, width):
    return jnp.concatenate([ref[:, part * width : (part + 1) * width] for ref in refs], axis=0)


def my_part(ref):
    width = ref.shape[1] // lax.axis_size("dp")
    return ref[:, pl.ds(pl.multiple_of(lax.axis_index("dp") * width, width), width)]


def own_kernel(tile, order, *refs):
    row_refs, (weight_in, weight_out, d_pre, h_cut, back, hidden) = refs[:2], refs[2:]
    me = lax.axis_index("expert")
    feat_width, ffw = weight_in.shape
    x, s = stack(row_refs, 0, feat_width), stack(row_refs, 1, feat_width)
    slots_all = x.shape[0]
    capacity = slots_all // len(order)
    dgate = jnp.zeros((slots_all, LANES), F32)
    dx = jnp.zeros((slots_all, feat_width), F32)
    for at in range(0, ffw, tile):
        cols = slice(at, at + tile)
        act, slope = gelu_and_slope(dot(x, weight_in[:, cols]))
        hidden[:, cols] = act
        d_hidden = dot(s, weight_out[cols, :], (1, 1))
        part = (d_hidden * slope).astype(BF16)
        d_pre[:, cols] = part
        product = d_hidden * act.astype(F32)
        for lane in range(0, tile, LANES):
            dgate = dgate + product[:, lane : lane + LANES]
        dx = dx + dot(part, weight_in[:, cols], (1, 1))
    h_cut[...] = my_part(hidden)
    dgate = jnp.broadcast_to(jnp.sum(dgate, axis=1, keepdims=True), (slots_all, LANES))
    for i, k in enumerate(order):
        rows, target = slice(i * capacity, (i + 1) * capacity), block_rows(me, k, capacity)
        back[target, :feat_width] = dx[rows].astype(BF16)
        back[target, feat_width:] = dgate[rows].astype(BF16)


def backward_tiles(tile, x, s, weight_in, weight_out, hidden, d_pre, rows):
    for at in range(0, weight_in.shape[1], tile):
        cols = slice(at, at + tile)
        act, slope = gelu_and_slope(dot(x, weight_in[:, cols]))
        hidden[:, cols] = act
        d_pre[rows, cols] = (dot(s, weight_out[cols, :], (1, 1)) * slope).astype(BF16)


def early_kernel(tile, pieces, *refs):
    row_refs, (weight_in, weight_out, d_pre, h_cut, hidden) = refs[:pieces], refs[pieces:]
    width = weight_in.shape[0]
    x, s = stack(row_refs, 0, width), stack(row_refs, 1, width)
    backward_tiles(tile, x, s, weight_in, weight_out, hidden, d_pre, slice(None))
    h_cut[...] = my_part(hidden)


def grads_kernel(tile, own, early, late, *refs):
    pieces = own + early + late
    row_refs, refs = refs[:pieces], refs[pieces:]
    d_pre0, h_cut0, d_pre1, h_cut1, weight_in, weight_out, grad_in, grad_out = refs[:8]
    hidden, d_pre = refs[8:]
    width, ffw = weight_in.shape
    x, s = stack(row_refs[-late:], 0, width), stack(row_refs[-late:], 1, width)
    first, second = d_pre0.shape[0], d_pre0.shape[0] + d_pre1.shape[0]
    d_pre[:first, :] = d_pre0[...]
    d_pre[first:second, :] = d_pre1[...]
    cut = grad_in.shape[0]
    mine = pl.ds(pl.multiple_of(lax.axis_index("dp") * cut, cut), cut)
    x_cut = jnp.concatenate([ref[:, mine] for ref in row_refs], axis=0)
    backward_tiles(tile, x, s, weight_in, weight_out, hidden, d_pre, slice(second, None))
    for at in range(0, ffw, tile):
        cols = slice(at, at + tile)
        grad_in[:, cols] = dot(x_cut, d_pre[:, cols], (0, 0)).astype(BF16)
    h_cut = jnp.concatenate([h_cut0[...], h_cut1[...], my_part(hidden)], axis=0)
    grad_out[...] = dot(h_cut, stack(row_refs, 1, width), (0, 0)).astype(BF16)


def after(value, *first):
    return lax.optimization_barrier((value, *first))[0]


def permute(block, k):
    return lax.ppermute(block, "expert", [(i, i ^ k) for i in range(lax.axis_size("expert"))])


def swap_cores(rows):
    return lax.ppermute(rows, "dp", [(i, i ^ 1) for i in range(lax.axis_size("dp"))])


def shift_chips(rows, k):
    groups = lax.axis_size("dp")
    return lax.ppermute(rows, "dp", [(i, (i + 2 * k) % groups) for i in range(groups)])


def gather_groups(rows):
    others = [swap_cores(rows)]
    for k in range(1, lax.axis_size("dp") // 2):
        other = shift_chips(rows, k)
        others += [other, swap_cores(other)]
    return others


def local(tokens, cotangent, routes, gates, proj_in, proj_out):
    tok_count, feat_width = tokens.shape
    experts = lax.axis_size("expert")
    groups = lax.axis_size("dp")
    capacity = 2 * tok_count // experts
    slots_all = experts * capacity
    half = experts // 2
    ffw = proj_in.shape[2]
    tile = ffw // groups
    product = 2 * slots_all * feat_width * ffw
    place = shape((slots_all, tok_count))

    routed = call(
        functools.partial(route_kernel, experts, capacity),
        [shape((capacity, 2 * feat_width))] * experts + [place] * 2,
        [routes.T, gates.T, tokens, cotangent],
        in_space=pltpu.HBM,
        scratch=[
            pltpu.VMEM((2, tok_count), jnp.int32),
            pltpu.VMEM((2, tok_count), BF16),
            pltpu.VMEM((tok_count, feat_width), BF16),
            pltpu.VMEM((tok_count, feat_width), BF16),
            pltpu.SemaphoreType.DMA((4,)),
        ],
    )
    blocks, places = routed[:experts], routed[experts:]
    weight_in, weight_out = call(
        load_kernel,
        [pltpu.VMEM((feat_width, ffw), BF16), pltpu.VMEM((ffw, feat_width), BF16)],
        [after(proj_in[0], places[0]), after(proj_out[0], places[0])],
        in_space=pltpu.HBM,
        scratch=[pltpu.SemaphoreType.DMA((2,))],
    )
    weights = [
        pltpu.with_memory_space_constraint(w, pltpu.VMEM) for w in (weight_in, weight_out)
    ]
    rest = list(range(experts - 1, 1, -1))
    order = [0, *rest[:2], 1, *rest[2:]]
    order_a, order_b = order[:half], order[half:]
    got_a = [blocks[0]] + [permute(blocks[k], k) for k in order_a[1:]]
    got_b = [
        permute(blocks[k] if i < 2 else after(blocks[k], *got_a[1:]), k)
        for i, k in enumerate(order_b)
    ]
    rows_a = jnp.concatenate(got_a, axis=0)
    chips_a = [shift_chips(rows_a, k) for k in range(1, groups // 2)]
    core_a = swap_cores(after(rows_a, got_b[0]))
    rows_b = jnp.concatenate(got_b, axis=0)
    chips_b = [shift_chips(rows_b, k) for k in range(1, groups // 2)]
    core_b = swap_cores(rows_b)
    d_pre0, h_cut0, back = call(
        functools.partial(own_kernel, tile, order),
        [
            shape((slots_all, ffw)),
            shape((slots_all, tile)),
            shape((slots_all, feat_width + LANES)),
        ],
        [rows_a, rows_b, *weights],
        20 * product,
        scratch=[pltpu.VMEM((slots_all, ffw), BF16)],
    )
    back = lax.all_to_all(
        back.reshape(experts, capacity, feat_width + LANES), "expert", 0, 0, tiled=True
    ).reshape(slots_all, feat_width + LANES)
    relayed_a = [swap_cores(after(rows, d_pre0)) for rows in chips_a]
    early = [core_a, core_b, *chips_a, *relayed_a]
    early_rows = sum(piece.shape[0] for piece in early)
    d_pre1, h_cut1 = call(
        functools.partial(early_kernel, tile, len(early)),
        [shape((early_rows, ffw)), shape((early_rows, tile))],
        [*early, *weights],
        product,
        scratch=[pltpu.VMEM((early_rows, ffw), BF16)],
    )
    chips_b += [swap_cores(rows) for rows in chips_b]
    late_rows = sum(piece.shape[0] for piece in chips_b)
    grad_in, grad_out = call(
        functools.partial(grads_kernel, tile, 2, len(early), len(chips_b)),
        [shape((feat_width // groups, ffw)), shape((ffw // groups, feat_width))],
        [rows_a, rows_b, *early, *chips_b, d_pre0, h_cut0, d_pre1, h_cut1, *weights],
        4 * product,
        scratch=[
            pltpu.VMEM((late_rows, ffw), BF16),
            pltpu.VMEM((groups * slots_all, ffw), BF16),
        ],
    )
    token_grads, gate_grads = call(
        functools.partial(combine_kernel, experts, capacity),
        [shape((tok_count, feat_width)), shape((2, tok_count))],
        [*places, gates.T, back],
        scratch=[pltpu.VMEM((slots_all, feat_width + LANES), BF16)],
    )
    return (token_grads, gate_grads.T, grad_in[None], grad_out[None])


def local_small_blocks(tokens, cotangent, routes, gates, proj_in, proj_out):
    tok_count, feat_width = tokens.shape
    experts = lax.axis_size("expert")
    groups = lax.axis_size("dp")
    me = lax.axis_index("dp")
    capacity = 2 * tok_count // experts
    slots_all = experts * capacity
    weight_in, weight_out = proj_in[0], proj_out[0]
    ffw = weight_in.shape[1]
    chosen = jnp.concatenate([routes[:, 0], routes[:, 1]])
    one_hot = (chosen[:, None] == jnp.arange(experts, dtype=jnp.int32)[None, :]).astype(jnp.int32)
    slot_pos = jnp.sum((jnp.cumsum(one_hot, axis=0) - one_hot) * one_hot, axis=1)
    target = jnp.where(slot_pos < capacity, chosen * capacity + slot_pos, slots_all)
    placing = (jnp.arange(slots_all, dtype=jnp.int32)[:, None] == target[None, :]).astype(BF16)
    either = placing[:, :tok_count] + placing[:, tok_count:]
    scaled = [
        (gates[:, k : k + 1].astype(F32) * cotangent.astype(F32)).astype(BF16) for k in range(2)
    ]

    def swap_blocks(rows):
        return lax.all_to_all(
            rows.astype(BF16).reshape(experts, capacity, rows.shape[1]), "expert", 0, 0, tiled=True
        ).reshape(slots_all, rows.shape[1])

    x = swap_blocks(dot(either, tokens))
    s = swap_blocks(dot(placing, jnp.concatenate(scaled, axis=0)))
    hidden0, slope0 = gelu_and_slope(dot(x, weight_in))
    d_hidden0 = dot(s, weight_out, (1, 1))
    d_pre0 = (d_hidden0 * slope0).astype(BF16)
    dgate = jnp.sum(hidden0.astype(F32) * d_hidden0, axis=1, keepdims=True)
    dx = dot(d_pre0, weight_in, (1, 1))
    back = swap_blocks(
        jnp.concatenate([dx, jnp.broadcast_to(dgate, (slots_all, LANES))], axis=1)
    )
    x_all = jnp.concatenate([x, *gather_groups(x)], axis=0)
    s_all = jnp.concatenate([s, *gather_groups(s)], axis=0)
    hidden1, slope1 = gelu_and_slope(dot(x_all[slots_all:], weight_in))
    d_pre1 = (dot(s_all[slots_all:], weight_out, (1, 1)) * slope1).astype(BF16)
    hidden = jnp.concatenate([hidden0, hidden1], axis=0)
    d_pre = jnp.concatenate([d_pre0, d_pre1], axis=0)
    x_cut = lax.dynamic_slice_in_dim(x_all, me * (feat_width // groups), feat_width // groups, 1)
    h_cut = lax.dynamic_slice_in_dim(hidden, me * (ffw // groups), ffw // groups, 1)
    grad_in = dot(x_cut, d_pre, (0, 0)).astype(BF16)
    grad_out = dot(h_cut, s_all, (0, 0)).astype(BF16)
    token_grads = dot(either, back[:, :feat_width], (0, 0)).astype(BF16)
    taken = dot(placing, back[:, feat_width : feat_width + 1], (0, 0))
    gate_grads = jnp.concatenate([taken[:tok_count], taken[tok_count:]], axis=1)
    gate_grads = (gate_grads / gates.astype(F32)).astype(BF16)
    return (token_grads, gate_grads, grad_in[None], grad_out[None])


def solution(mesh):
    rows = P(("dp", "expert"), None)
    weights = P("expert", None, None)

    def whole(tokens, *others):
        experts = mesh.shape["expert"]
        capacity = 2 * tokens.shape[0] // (mesh.shape["dp"] * experts) // experts
        tiles = capacity % 16 == 0 and experts & (experts - 1) == 0
        return jax.shard_map(
            local if tiles else local_small_blocks,
            mesh=mesh,
            in_specs=(rows, rows, rows, rows, weights, weights),
            out_specs=(rows, rows, P("expert", "dp", None), P("expert", "dp", None)),
            check_vma=False,
        )(tokens, *others)

    return whole
```

```python
import functools

import jax
import jax.numpy as jnp
from jax import lax
from jax.experimental import pallas as pl
from jax.experimental.pallas import tpu as pltpu
from jax.sharding import PartitionSpec as P

BF16 = jnp.bfloat16
F32 = jnp.float32
LANES = 128
MIB = 1 << 20


def dot(a, b, over=(1, 0)):
    return lax.dot_general(
        a, b, (((over[0],), (over[1],)), ((), ())), preferred_element_type=F32
    )


def gelu_and_slope(pre_act):
    cdf = 0.5 * (1.0 + lax.erf(pre_act * 0.7071067811865476))
    pdf = jnp.exp(-0.5 * pre_act * pre_act) * 0.3989422804014327
    return (pre_act * cdf).astype(BF16), cdf + pre_act * pdf


def call(kernel, out_shape, args, flops=0, limit=24, scratch=(), spaces=None):
    spaces = spaces or [pltpu.VMEM] * len(args)
    moved = sum(a.size * a.dtype.itemsize for a in args)
    args = [
        pltpu.with_memory_space_constraint(a, space) if space == pltpu.HBM else a
        for a, space in zip(args, spaces)
    ]
    return pl.pallas_call(
        kernel,
        out_shape=out_shape,
        in_specs=[pl.BlockSpec(memory_space=space) for space in spaces],
        out_specs=[
            pl.BlockSpec(memory_space=getattr(out, "memory_space", pltpu.VMEM))
            for out in out_shape
        ],
        scratch_shapes=list(scratch),
        compiler_params=pltpu.CompilerParams(vmem_limit_bytes=limit * MIB),
        cost_estimate=pl.CostEstimate(flops=flops, bytes_accessed=moved, transcendentals=0),
    )(*args)


def shape(dims, dtype=BF16):
    return jax.ShapeDtypeStruct(dims, dtype)


def route_kernel(experts, capacity, routes_hbm, gates_hbm, tokens_hbm, cotangent_hbm, *refs):
    blocks, place_refs, scratch = refs[:experts], refs[experts : experts + 2], refs[experts + 2 :]
    routes, gates, tokens, cotangent, sems = scratch
    copies = [
        pltpu.make_async_copy(source, target, sems.at[i])
        for i, (source, target) in enumerate(
            (
                (routes_hbm, routes),
                (gates_hbm, gates),
                (tokens_hbm, tokens),
                (cotangent_hbm, cotangent),
            )
        )
    ]
    for copy in copies:
        copy.start()
    tok_count, feat_width = tokens.shape
    slots_all = experts * capacity
    me = lax.axis_index("expert")
    rows = max(experts, 16)
    before = (
        lax.broadcasted_iota(jnp.int32, (tok_count, tok_count), 0)
        < lax.broadcasted_iota(jnp.int32, (tok_count, tok_count), 1)
    ).astype(F32).astype(BF16)
    expert_id = lax.broadcasted_iota(jnp.int32, (rows, tok_count), 0)
    slot_id = lax.broadcasted_iota(jnp.int32, (slots_all, tok_count), 0)
    taken = jnp.zeros((rows, 1), F32)
    places, gated = [], jnp.zeros((slots_all, tok_count), F32)
    copies[0].wait()
    copies[1].wait()
    for choice in range(2):
        chosen = routes[choice : choice + 1, :]
        one_hot = (expert_id == chosen).astype(F32)
        earlier = dot(one_hot.astype(BF16), before) + taken
        taken = taken + jnp.sum(one_hot, axis=1, keepdims=True)
        slot_pos = jnp.sum(earlier * one_hot, axis=0, keepdims=True).astype(jnp.int32)
        target = jnp.where(
            slot_pos < capacity, jnp.bitwise_xor(chosen, me) * capacity + slot_pos, slots_all
        )
        place = (slot_id == target).astype(F32)
        place_refs[choice][...] = place.astype(BF16)
        places.append(place)
        gated = gated + place * gates[choice : choice + 1, :].astype(F32)
    copies[2].wait()
    x = dot((places[0] + places[1]).astype(BF16), tokens[...]).astype(BF16)
    copies[3].wait()
    s = dot(gated.astype(BF16), cotangent[...]).astype(BF16)
    for k in range(experts):
        blocks[k][:, :feat_width] = x[k * capacity : (k + 1) * capacity]
        blocks[k][:, feat_width:] = s[k * capacity : (k + 1) * capacity]


def block_rows(me, k, capacity):
    return pl.ds(pl.multiple_of(jnp.bitwise_xor(me, k) * capacity, capacity), capacity)


def load_kernel(in_hbm, out_hbm, weight_in, weight_out, sems):
    copies = [
        pltpu.make_async_copy(source, target, sems.at[i])
        for i, (source, target) in enumerate(((in_hbm, weight_in), (out_hbm, weight_out)))
    ]
    for copy in copies:
        copy.start()
    for copy in copies:
        copy.wait()


def combine_kernel(experts, capacity, place0, place1, gates, back, token_grads, gate_grads, rows):
    tok_count, feat_width = token_grads.shape
    me = lax.axis_index("expert")
    for k in range(experts):
        rows[k * capacity : (k + 1) * capacity, :] = back[block_rows(me, k, capacity), :]
    either = (place0[...].astype(F32) + place1[...].astype(F32)).astype(BF16)
    token_grads[...] = dot(either, rows[:, :feat_width], (0, 0)).astype(BF16)
    dgate = rows[:, feat_width : feat_width + tok_count].astype(F32)
    taken = [
        jnp.sum(place[...].astype(F32) * dgate, axis=0, keepdims=True) for place in (place0, place1)
    ]
    gate_grads[...] = (jnp.concatenate(taken, axis=0) / gates[...].astype(F32)).astype(BF16)


def stack(refs, part, width):
    return jnp.concatenate([ref[:, part * width : (part + 1) * width] for ref in refs], axis=0)


def my_part(ref):
    width = ref.shape[1] // lax.axis_size("dp")
    return ref[:, pl.ds(pl.multiple_of(lax.axis_index("dp") * width, width), width)]


def own_kernel(tile, order, *refs):
    row_refs, (weight_in, weight_out, d_pre_hbm, h_cut, back_hbm, *scratch) = refs[:2], refs[2:]
    hidden, d_pre, back, sems = scratch
    me = lax.axis_index("expert")
    feat_width, ffw = weight_in.shape
    x, s = stack(row_refs, 0, feat_width), stack(row_refs, 1, feat_width)
    slots_all = x.shape[0]
    capacity = slots_all // len(order)
    dgate = jnp.zeros((slots_all, LANES), F32)
    dx = jnp.zeros((slots_all, feat_width), F32)
    for at in range(0, ffw, tile):
        cols = slice(at, at + tile)
        act, slope = gelu_and_slope(dot(x, weight_in[:, cols]))
        hidden[:, cols] = act
        d_hidden = dot(s, weight_out[cols, :], (1, 1))
        part = (d_hidden * slope).astype(BF16)
        d_pre[:, cols] = part
        product = d_hidden * act.astype(F32)
        for lane in range(0, tile, LANES):
            dgate = dgate + product[:, lane : lane + LANES]
        dx = dx + dot(part, weight_in[:, cols], (1, 1))
    d_pre_out = pltpu.make_async_copy(d_pre, d_pre_hbm, sems.at[0])
    d_pre_out.start()
    dgate = jnp.broadcast_to(jnp.sum(dgate, axis=1, keepdims=True), (slots_all, LANES))
    for i, k in enumerate(order):
        rows, target = slice(i * capacity, (i + 1) * capacity), block_rows(me, k, capacity)
        back[target, :feat_width] = dx[rows].astype(BF16)
        back[target, feat_width:] = dgate[rows].astype(BF16)
    back_out = pltpu.make_async_copy(back, back_hbm, sems.at[1])
    back_out.start()
    h_cut[...] = my_part(hidden)
    d_pre_out.wait()
    back_out.wait()


def grads_kernel(tile, pieces, *refs):
    row_refs, refs = refs[:pieces], refs[pieces:]
    d_pre0, h_cut0, in_hbm, out_hbm, grad_in_hbm, grad_out_hbm = refs[:6]
    rows, weight_in, weight_out, hidden, h_cut, d_pre, grad_in, grad_out, sems, out_sems = refs[6:]
    width, ffw = weight_in.shape
    tiles = [slice(at, at + tile) for at in range(0, ffw, tile)]
    own = d_pre0.shape[0]
    piece = row_refs[0].shape[0]
    todo = []

    def fetch(source, target):
        todo.append(pltpu.make_async_copy(source, target, sems.at[len(todo)]))
        todo[-1].start()
        return todo[-1]

    first = [
        fetch(ref, rows.at[pl.ds(i * piece, piece)])
        for i, ref in enumerate(row_refs)
        if i * piece >= own
    ]
    weights = [
        fetch(*pair)
        for cols in tiles
        for pair in (
            (in_hbm.at[:, cols], weight_in.at[:, cols]),
            (out_hbm.at[cols, :], weight_out.at[cols, :]),
        )
    ]
    rest = [
        fetch(ref, rows.at[pl.ds(i * piece, piece)])
        for i, ref in enumerate(row_refs)
        if i * piece < own
    ]
    rest += [fetch(d_pre0, d_pre.at[:own, :]), fetch(h_cut0, h_cut.at[:own, :])]
    for copy in first + weights[:2]:
        copy.wait()
    x, s = rows[own:, :width], rows[own:, width:]
    cut = grad_in.shape[0]
    mine = pl.ds(pl.multiple_of(lax.axis_index("dp") * cut, cut), cut)
    outs = []
    for t, cols in enumerate(tiles):
        if t == 1:
            for copy in weights[2:] + rest:
                copy.wait()
        act, slope = gelu_and_slope(dot(x, weight_in[:, cols]))
        hidden[:, cols] = act
        d_pre[own:, cols] = (dot(s, weight_out[cols, :], (1, 1)) * slope).astype(BF16)
    for t, cols in enumerate(tiles):
        grad_in[:, cols] = dot(rows[:, mine], d_pre[:, cols], (0, 0)).astype(BF16)
        outs.append(
            pltpu.make_async_copy(grad_in.at[:, cols], grad_in_hbm.at[:, cols], out_sems.at[t])
        )
        outs[-1].start()
    h_cut[own:, :] = my_part(hidden)
    grad_out[...] = dot(h_cut[...], rows[:, width:], (0, 0)).astype(BF16)
    outs.append(pltpu.make_async_copy(grad_out, grad_out_hbm, out_sems.at[len(tiles)]))
    outs[-1].start()
    for copy in outs:
        copy.wait()


def after(value, *first):
    return lax.optimization_barrier((value, *first))[0]


def permute(block, k):
    return lax.ppermute(block, "expert", [(i, i ^ k) for i in range(lax.axis_size("expert"))])


def swap_cores(rows):
    return lax.ppermute(rows, "dp", [(i, i ^ 1) for i in range(lax.axis_size("dp"))])


def shift_chips(rows, k):
    groups = lax.axis_size("dp")
    return lax.ppermute(rows, "dp", [(i, (i + 2 * k) % groups) for i in range(groups)])


def gather_groups(rows):
    others = [swap_cores(rows)]
    for k in range(1, lax.axis_size("dp") // 2):
        other = shift_chips(rows, k)
        others += [other, swap_cores(other)]
    return others


def local(tokens, cotangent, routes, gates, proj_in, proj_out):
    tok_count, feat_width = tokens.shape
    experts = lax.axis_size("expert")
    groups = lax.axis_size("dp")
    capacity = 2 * tok_count // experts
    slots_all = experts * capacity
    half = experts // 2
    ffw = proj_in.shape[2]
    tile = ffw // groups
    product = 2 * slots_all * feat_width * ffw
    place = shape((slots_all, tok_count))

    routed = call(
        functools.partial(route_kernel, experts, capacity),
        [shape((capacity, 2 * feat_width))] * experts + [place] * 2,
        [routes.T, gates.T, tokens, cotangent],
        spaces=[pltpu.HBM] * 4,
        scratch=[
            pltpu.VMEM((2, tok_count), jnp.int32),
            pltpu.VMEM((2, tok_count), BF16),
            pltpu.VMEM((tok_count, feat_width), BF16),
            pltpu.VMEM((tok_count, feat_width), BF16),
            pltpu.SemaphoreType.DMA((4,)),
        ],
    )
    blocks, places = routed[:experts], routed[experts:]
    rest = list(range(experts - 1, 1, -1))
    order = [0, *rest[:2], 1, *rest[2:]]
    order_a, order_b = order[:half], order[half:]
    got_a = [blocks[0]] + [permute(blocks[k], k) for k in order_a[1:]]
    got_b = [
        permute(blocks[k] if i < 2 else after(blocks[k], got_a[1 - i]), k)
        for i, k in enumerate(order_b)
    ]
    weight_in, weight_out = call(
        load_kernel,
        [pltpu.VMEM((feat_width, ffw), BF16), pltpu.VMEM((ffw, feat_width), BF16)],
        [after(proj_in[0], got_b[0]), after(proj_out[0], got_b[0])],
        spaces=[pltpu.HBM] * 2,
        scratch=[pltpu.SemaphoreType.DMA((2,))],
    )
    weights = [
        pltpu.with_memory_space_constraint(w, pltpu.VMEM) for w in (weight_in, weight_out)
    ]
    rows_a = jnp.concatenate(got_a, axis=0)
    chips_a = [shift_chips(rows_a, k) for k in range(1, groups // 2)]
    core_a = swap_cores(after(rows_a, got_b[0]))
    rows_b = jnp.concatenate(got_b, axis=0)
    chips_b = [shift_chips(rows_b, k) for k in range(1, groups // 2)]
    core_b = swap_cores(rows_b)
    d_pre0, h_cut0, back = call(
        functools.partial(own_kernel, tile, order),
        [
            pltpu.HBM((slots_all, ffw), BF16),
            shape((slots_all, tile)),
            pltpu.HBM((slots_all, feat_width + LANES), BF16),
        ],
        [rows_a, rows_b, *weights],
        20 * product,
        scratch=[
            pltpu.VMEM((slots_all, ffw), BF16),
            pltpu.VMEM((slots_all, ffw), BF16),
            pltpu.VMEM((slots_all, feat_width + LANES), BF16),
            pltpu.SemaphoreType.DMA((2,)),
        ],
    )
    back = lax.all_to_all(
        back.reshape(experts, capacity, feat_width + LANES), "expert", 0, 0, tiled=True
    ).reshape(slots_all, feat_width + LANES)
    relayed_a = [swap_cores(after(rows, d_pre0)) for rows in chips_a]
    relayed_b = [swap_cores(rows) for rows in chips_b]
    pieces = [rows_a, rows_b, core_a, core_b, *chips_a, *relayed_a, *chips_b, *relayed_b]
    rows_all = groups * slots_all
    grad_in, grad_out = call(
        functools.partial(grads_kernel, tile, len(pieces)),
        [
            pltpu.HBM((feat_width // groups, ffw), BF16),
            pltpu.HBM((ffw // groups, feat_width), BF16),
        ],
        [*pieces, d_pre0, h_cut0, proj_in[0], proj_out[0]],
        4 * product,
        limit=32,
        scratch=[
            pltpu.VMEM((rows_all, 2 * feat_width), BF16),
            pltpu.VMEM((feat_width, ffw), BF16),
            pltpu.VMEM((ffw, feat_width), BF16),
            pltpu.VMEM((rows_all - slots_all, ffw), BF16),
            pltpu.VMEM((rows_all, tile), BF16),
            pltpu.VMEM((rows_all, ffw), BF16),
            pltpu.VMEM((feat_width // groups, ffw), BF16),
            pltpu.VMEM((ffw // groups, feat_width), BF16),
            pltpu.SemaphoreType.DMA((len(pieces) + 2 * groups + 2,)),
            pltpu.SemaphoreType.DMA((groups + 1,)),
        ],
        spaces=[pl.ANY] * len(pieces) + [pltpu.HBM, pl.ANY] + [pltpu.HBM] * 2,
    )
    token_grads, gate_grads = call(
        functools.partial(combine_kernel, experts, capacity),
        [shape((tok_count, feat_width)), shape((2, tok_count))],
        [*places, gates.T, back],
        scratch=[pltpu.VMEM((slots_all, feat_width + LANES), BF16)],
    )
    return (token_grads, gate_grads.T, grad_in[None], grad_out[None])


def local_small_blocks(tokens, cotangent, routes, gates, proj_in, proj_out):
    tok_count, feat_width = tokens.shape
    experts = lax.axis_size("expert")
    groups = lax.axis_size("dp")
    me = lax.axis_index("dp")
    capacity = 2 * tok_count // experts
    slots_all = experts * capacity
    weight_in, weight_out = proj_in[0], proj_out[0]
    ffw = weight_in.shape[1]
    chosen = jnp.concatenate([routes[:, 0], routes[:, 1]])
    one_hot = (chosen[:, None] == jnp.arange(experts, dtype=jnp.int32)[None, :]).astype(jnp.int32)
    slot_pos = jnp.sum((jnp.cumsum(one_hot, axis=0) - one_hot) * one_hot, axis=1)
    target = jnp.where(slot_pos < capacity, chosen * capacity + slot_pos, slots_all)
    placing = (jnp.arange(slots_all, dtype=jnp.int32)[:, None] == target[None, :]).astype(BF16)
    either = placing[:, :tok_count] + placing[:, tok_count:]
    scaled = [
        (gates[:, k : k + 1].astype(F32) * cotangent.astype(F32)).astype(BF16) for k in range(2)
    ]

    def swap_blocks(rows):
        return lax.all_to_all(
            rows.astype(BF16).reshape(experts, capacity, rows.shape[1]), "expert", 0, 0, tiled=True
        ).reshape(slots_all, rows.shape[1])

    x = swap_blocks(dot(either, tokens))
    s = swap_blocks(dot(placing, jnp.concatenate(scaled, axis=0)))
    hidden0, slope0 = gelu_and_slope(dot(x, weight_in))
    d_hidden0 = dot(s, weight_out, (1, 1))
    d_pre0 = (d_hidden0 * slope0).astype(BF16)
    dgate = jnp.sum(hidden0.astype(F32) * d_hidden0, axis=1, keepdims=True)
    dx = dot(d_pre0, weight_in, (1, 1))
    back = swap_blocks(
        jnp.concatenate([dx, jnp.broadcast_to(dgate, (slots_all, LANES))], axis=1)
    )
    x_all = jnp.concatenate([x, *gather_groups(x)], axis=0)
    s_all = jnp.concatenate([s, *gather_groups(s)], axis=0)
    hidden1, slope1 = gelu_and_slope(dot(x_all[slots_all:], weight_in))
    d_pre1 = (dot(s_all[slots_all:], weight_out, (1, 1)) * slope1).astype(BF16)
    hidden = jnp.concatenate([hidden0, hidden1], axis=0)
    d_pre = jnp.concatenate([d_pre0, d_pre1], axis=0)
    x_cut = lax.dynamic_slice_in_dim(x_all, me * (feat_width // groups), feat_width // groups, 1)
    h_cut = lax.dynamic_slice_in_dim(hidden, me * (ffw // groups), ffw // groups, 1)
    grad_in = dot(x_cut, d_pre, (0, 0)).astype(BF16)
    grad_out = dot(h_cut, s_all, (0, 0)).astype(BF16)
    token_grads = dot(either, back[:, :feat_width], (0, 0)).astype(BF16)
    taken = dot(placing, back[:, feat_width : feat_width + 1], (0, 0))
    gate_grads = jnp.concatenate([taken[:tok_count], taken[tok_count:]], axis=1)
    gate_grads = (gate_grads / gates.astype(F32)).astype(BF16)
    return (token_grads, gate_grads, grad_in[None], grad_out[None])


def solution(mesh):
    rows = P(("dp", "expert"), None)
    weights = P("expert", None, None)

    def whole(tokens, *others):
        experts = mesh.shape["expert"]
        capacity = 2 * tokens.shape[0] // (mesh.shape["dp"] * experts) // experts
        tiles = capacity % 16 == 0 and experts & (experts - 1) == 0
        return jax.shard_map(
            local if tiles else local_small_blocks,
            mesh=mesh,
            in_specs=(rows, rows, rows, rows, weights, weights),
            out_specs=(rows, rows, P("expert", "dp", None), P("expert", "dp", None)),
            check_vma=False,
        )(tokens, *others)

    return whole
```

```python
import functools

import jax
import jax.numpy as jnp
from jax import lax
from jax.experimental import pallas as pl
from jax.experimental.pallas import tpu as pltpu
from jax.sharding import PartitionSpec as P

BF16 = jnp.bfloat16
F32 = jnp.float32
LANES = 128
MIB = 1 << 20


def dot(a, b, over=(1, 0)):
    return lax.dot_general(
        a, b, (((over[0],), (over[1],)), ((), ())), preferred_element_type=F32
    )


def gelu_and_slope(pre_act):
    cdf = 0.5 * (1.0 + lax.erf(pre_act * 0.7071067811865476))
    pdf = jnp.exp(-0.5 * pre_act * pre_act) * 0.3989422804014327
    return (pre_act * cdf).astype(BF16), cdf + pre_act * pdf


def call(kernel, out_shape, args, flops=0, limit=24, scratch=(), spaces=None):
    spaces = spaces or [pltpu.VMEM] * len(args)
    moved = sum(a.size * a.dtype.itemsize for a in args)
    args = [
        pltpu.with_memory_space_constraint(a, space) if space == pltpu.HBM else a
        for a, space in zip(args, spaces)
    ]
    return pl.pallas_call(
        kernel,
        out_shape=out_shape,
        in_specs=[pl.BlockSpec(memory_space=space) for space in spaces],
        out_specs=[
            pl.BlockSpec(memory_space=getattr(out, "memory_space", pltpu.VMEM))
            for out in out_shape
        ],
        scratch_shapes=list(scratch),
        compiler_params=pltpu.CompilerParams(vmem_limit_bytes=limit * MIB),
        cost_estimate=pl.CostEstimate(flops=flops, bytes_accessed=moved, transcendentals=0),
    )(*args)


def shape(dims, dtype=BF16):
    return jax.ShapeDtypeStruct(dims, dtype)


def route_kernel(experts, capacity, routes_hbm, gates_hbm, tokens_hbm, cotangent_hbm, *refs):
    blocks, place_refs, scratch = refs[:experts], refs[experts : experts + 2], refs[experts + 2 :]
    routes, gates, tokens, cotangent, sems = scratch
    copies = [
        pltpu.make_async_copy(source, target, sems.at[i])
        for i, (source, target) in enumerate(
            (
                (routes_hbm, routes),
                (gates_hbm, gates),
                (tokens_hbm, tokens),
                (cotangent_hbm, cotangent),
            )
        )
    ]
    for copy in copies:
        copy.start()
    tok_count, feat_width = tokens.shape
    slots_all = experts * capacity
    me = lax.axis_index("expert")
    rows = max(experts, 16)
    before = (
        lax.broadcasted_iota(jnp.int32, (tok_count, tok_count), 0)
        < lax.broadcasted_iota(jnp.int32, (tok_count, tok_count), 1)
    ).astype(F32).astype(BF16)
    expert_id = lax.broadcasted_iota(jnp.int32, (rows, tok_count), 0)
    slot_id = lax.broadcasted_iota(jnp.int32, (slots_all, tok_count), 0)
    taken = jnp.zeros((rows, 1), F32)
    places, gated = [], jnp.zeros((slots_all, tok_count), F32)
    copies[0].wait()
    copies[1].wait()
    for choice in range(2):
        chosen = routes[choice : choice + 1, :]
        one_hot = (expert_id == chosen).astype(F32)
        earlier = dot(one_hot.astype(BF16), before) + taken
        taken = taken + jnp.sum(one_hot, axis=1, keepdims=True)
        slot_pos = jnp.sum(earlier * one_hot, axis=0, keepdims=True).astype(jnp.int32)
        target = jnp.where(
            slot_pos < capacity, jnp.bitwise_xor(chosen, me) * capacity + slot_pos, slots_all
        )
        place = (slot_id == target).astype(F32)
        place_refs[choice][...] = place.astype(BF16)
        places.append(place)
        gated = gated + place * gates[choice : choice + 1, :].astype(F32)
    copies[2].wait()
    x = dot((places[0] + places[1]).astype(BF16), tokens[...]).astype(BF16)
    copies[3].wait()
    s = dot(gated.astype(BF16), cotangent[...]).astype(BF16)
    for k in range(experts):
        blocks[k][:, :feat_width] = x[k * capacity : (k + 1) * capacity]
        blocks[k][:, feat_width:] = s[k * capacity : (k + 1) * capacity]


def block_rows(me, k, capacity):
    return pl.ds(pl.multiple_of(jnp.bitwise_xor(me, k) * capacity, capacity), capacity)


def combine_kernel(experts, capacity, place0, place1, gates, back, token_grads, gate_grads, rows):
    tok_count, feat_width = token_grads.shape
    me = lax.axis_index("expert")
    for k in range(experts):
        rows[k * capacity : (k + 1) * capacity, :] = back[block_rows(me, k, capacity), :]
    either = (place0[...].astype(F32) + place1[...].astype(F32)).astype(BF16)
    token_grads[...] = dot(either, rows[:, :feat_width], (0, 0)).astype(BF16)
    dgate = rows[:, feat_width : feat_width + tok_count].astype(F32)
    taken = [
        jnp.sum(place[...].astype(F32) * dgate, axis=0, keepdims=True) for place in (place0, place1)
    ]
    gate_grads[...] = (jnp.concatenate(taken, axis=0) / gates[...].astype(F32)).astype(BF16)


def stack(refs, part, width):
    return jnp.concatenate([ref[:, part * width : (part + 1) * width] for ref in refs], axis=0)


def my_part(ref):
    width = ref.shape[1] // lax.axis_size("dp")
    return ref[:, pl.ds(pl.multiple_of(lax.axis_index("dp") * width, width), width)]


def rows_backward(tiles, x, s, weight_in, weight_out, hidden, d_pre, rows, before, dgate=None):
    for t, cols in enumerate(tiles):
        if t == 1:
            for copy in before:
                copy.wait()
        act, slope = gelu_and_slope(dot(x, weight_in[:, cols]))
        hidden[:, cols] = act
        d_hidden = dot(s, weight_out[cols, :], (1, 1))
        d_pre[rows, cols] = (d_hidden * slope).astype(BF16)
        if dgate is not None:
            product = d_hidden * act.astype(F32)
            for lane in range(0, product.shape[1], LANES):
                dgate = dgate + product[:, lane : lane + LANES]
    if dgate is not None:
        return jnp.broadcast_to(jnp.sum(dgate, axis=1, keepdims=True), dgate.shape)


def fetch_weights(fetch, tiles, in_hbm, out_hbm, weight_in, weight_out):
    copies = []
    for cols in tiles:
        copies.append(fetch(in_hbm.at[:, cols], weight_in.at[:, cols]))
        copies.append(fetch(out_hbm.at[cols, :], weight_out.at[cols, :]))
    return copies


def fetcher(sems):
    count = iter(range(sems.shape[0]))

    def fetch(source, target):
        copy = pltpu.make_async_copy(source, target, sems.at[next(count)])
        copy.start()
        return copy

    return fetch


def own_first_kernel(tile, *refs):
    rows, in_hbm, out_hbm, weight_in, weight_out, d_pre_hbm, h_cut_hbm, back, *scratch = refs
    hidden, d_pre, h_cut, sems = scratch
    width, ffw = weight_in.shape
    tiles = [slice(at, at + tile) for at in range(0, ffw, tile)]
    fetch = fetcher(sems)
    copies = fetch_weights(fetch, tiles, in_hbm, out_hbm, weight_in, weight_out)
    for copy in copies[:2]:
        copy.wait()
    x, s = rows[:, :width], rows[:, width:]
    zero = jnp.zeros((x.shape[0], LANES), F32)
    back[:, width:] = rows_backward(
        tiles, x, s, weight_in, weight_out, hidden, d_pre, slice(None), copies[2:], zero
    ).astype(BF16)
    h_cut[...] = my_part(hidden)
    outs = [fetch(d_pre, d_pre_hbm), fetch(h_cut, h_cut_hbm)]
    wide = width // 4
    for at in range(0, width, wide):
        cols = slice(at, at + wide)
        back[:, cols] = dot(d_pre[...], weight_in[cols, :], (1, 1)).astype(BF16)
    for copy in outs:
        copy.wait()


def own_second_kernel(tile, order, *refs):
    rows, first_back, weight_in, weight_out, d_pre_hbm, h_cut_hbm, back_hbm, *scratch = refs
    hidden, d_pre, h_cut, back, sems = scratch
    me = lax.axis_index("expert")
    width, ffw = weight_in.shape
    tiles = [slice(at, at + tile) for at in range(0, ffw, tile)]
    fetch = fetcher(sems)
    capacity = 2 * rows.shape[0] // len(order)
    half = len(order) // 2
    spans = [slice(i * capacity, (i + 1) * capacity) for i in range(half)]
    targets = [block_rows(me, k, capacity) for k in order]
    for span, target in zip(spans, targets[:half]):
        back[target, :] = first_back[span, :]
    x, s = rows[:, :width], rows[:, width:]
    zero = jnp.zeros((x.shape[0], LANES), F32)
    dgate = rows_backward(
        tiles, x, s, weight_in, weight_out, hidden, d_pre, slice(None), [], zero
    )
    h_cut[...] = my_part(hidden)
    outs = [fetch(d_pre, d_pre_hbm), fetch(h_cut, h_cut_hbm)]
    for span, target in zip(spans, targets[half:]):
        back[target, width:] = dgate[span].astype(BF16)
    outs.append(fetch(back.at[:, width:], back_hbm.at[:, width:]))
    wide = width // 4
    for at in range(0, width, wide):
        cols = slice(at, at + wide)
        dx = dot(d_pre[...], weight_in[cols, :], (1, 1)).astype(BF16)
        for span, target in zip(spans, targets[half:]):
            back[target, cols] = dx[span]
        outs.append(fetch(back.at[:, cols], back_hbm.at[:, cols]))
    for copy in outs:
        copy.wait()


def early_kernel(tile, pieces, *refs):
    row_refs, refs = refs[:pieces], refs[pieces:]
    in_hbm, out_hbm, weight_in, weight_out, d_pre, h_cut, rows, hidden, sems = refs
    width, ffw = weight_in.shape
    piece = row_refs[0].shape[0]
    tiles = [slice(at, at + tile) for at in range(0, ffw, tile)]
    fetch = fetcher(sems)
    copies = [fetch(ref, rows.at[pl.ds(i * piece, piece)]) for i, ref in enumerate(row_refs)]
    copies += fetch_weights(fetch, tiles, in_hbm, out_hbm, weight_in, weight_out)
    for copy in copies[: pieces + 2]:
        copy.wait()
    x, s = rows[:, :width], rows[:, width:]
    rest = copies[pieces + 2 :]
    rows_backward(tiles, x, s, weight_in, weight_out, hidden, d_pre, slice(None), rest)
    h_cut[...] = my_part(hidden)


def grads_kernel(tile, pieces, late, *refs):
    row_refs, refs = refs[:pieces], refs[pieces:]
    d_pre_refs, h_cut_refs, refs = refs[:3], refs[3:6], refs[6:]
    weight_in, weight_out, grad_in_hbm, grad_out_hbm = refs[:4]
    rows, hidden, h_cut, d_pre, grad_in, grad_out, sems, out_sems = refs[4:]
    width, ffw = weight_in.shape
    tiles = [slice(at, at + tile) for at in range(0, ffw, tile)]
    piece = row_refs[0].shape[0]
    known = (pieces - late) * piece
    fetch = fetcher(sems)
    copies = [
        fetch(row_refs[i], rows.at[pl.ds(i * piece, piece)])
        for i in [*range(pieces - late, pieces), *range(pieces - late)]
    ]
    at = 0
    for source, cut_source in zip(d_pre_refs, h_cut_refs):
        span = pl.ds(at, source.shape[0])
        copies += [fetch(source, d_pre.at[span]), fetch(cut_source, h_cut.at[span])]
        at += source.shape[0]
    for copy in copies[:late]:
        copy.wait()
    x, s = rows[known:, :width], rows[known:, width:]
    rows_backward(
        tiles, x, s, weight_in, weight_out, hidden, d_pre, slice(known, None), copies[late:]
    )
    cut = grad_in.shape[0]
    mine = pl.ds(pl.multiple_of(lax.axis_index("dp") * cut, cut), cut)
    send = fetcher(out_sems)
    outs = []
    for cols in tiles:
        grad_in[:, cols] = dot(rows[:, mine], d_pre[:, cols], (0, 0)).astype(BF16)
        outs.append(send(grad_in.at[:, cols], grad_in_hbm.at[:, cols]))
    h_cut[known:, :] = my_part(hidden)
    wide = width // 4
    for at in range(0, width, wide):
        cols = slice(at, at + wide)
        s_cols = slice(width + at, width + at + wide)
        grad_out[:, cols] = dot(h_cut[...], rows[:, s_cols], (0, 0)).astype(BF16)
        outs.append(send(grad_out.at[:, cols], grad_out_hbm.at[:, cols]))
    for copy in outs:
        copy.wait()


def after(value, *first):
    return lax.optimization_barrier((value, *first))[0]


def permute(block, k):
    return lax.ppermute(block, "expert", [(i, i ^ k) for i in range(lax.axis_size("expert"))])


def swap_cores(rows):
    return lax.ppermute(rows, "dp", [(i, i ^ 1) for i in range(lax.axis_size("dp"))])


def shift_chips(rows, k):
    groups = lax.axis_size("dp")
    return lax.ppermute(rows, "dp", [(i, (i + 2 * k) % groups) for i in range(groups)])


def gather_groups(rows):
    others = [swap_cores(rows)]
    for k in range(1, lax.axis_size("dp") // 2):
        other = shift_chips(rows, k)
        others += [other, swap_cores(other)]
    return others


def local(tokens, cotangent, routes, gates, proj_in, proj_out):
    tok_count, feat_width = tokens.shape
    experts = lax.axis_size("expert")
    groups = lax.axis_size("dp")
    capacity = 2 * tok_count // experts
    slots_all = experts * capacity
    half = experts // 2
    ffw = proj_in.shape[2]
    tile = ffw // groups
    product = 2 * slots_all * feat_width * ffw
    place = shape((slots_all, tok_count))

    routed = call(
        functools.partial(route_kernel, experts, capacity),
        [shape((capacity, 2 * feat_width))] * experts + [place] * 2,
        [routes.T, gates.T, tokens, cotangent],
        spaces=[pltpu.HBM] * 4,
        scratch=[
            pltpu.VMEM((2, tok_count), jnp.int32),
            pltpu.VMEM((2, tok_count), BF16),
            pltpu.VMEM((tok_count, feat_width), BF16),
            pltpu.VMEM((tok_count, feat_width), BF16),
            pltpu.SemaphoreType.DMA((4,)),
        ],
    )
    blocks, places = routed[:experts], routed[experts:]
    rest = list(range(experts - 1, 1, -1))
    order = [0, *rest[:2], 1, *rest[2:]]
    order_a, order_b = order[:half], order[half:]
    got_a = [blocks[0]] + [permute(blocks[k], k) for k in order_a[1:]]
    got_b = [
        permute(blocks[k] if i < 2 else after(blocks[k], got_a[1 - i]), k)
        for i, k in enumerate(order_b)
    ]
    rows_a = jnp.concatenate(got_a, axis=0)
    chips_a = [shift_chips(rows_a, k) for k in range(1, groups // 2)]
    core_a = swap_cores(after(rows_a, got_b[0]))
    rows_b = jnp.concatenate(got_b, axis=0)
    chips_b = [shift_chips(rows_b, k) for k in range(1, groups // 2)]
    core_b = swap_cores(rows_b)
    hbm_weights = [proj_in[0], proj_out[0]]
    vmem_weights = [pltpu.VMEM((feat_width, ffw), BF16), pltpu.VMEM((ffw, feat_width), BF16)]
    own = slots_all // 2
    own_out = [pltpu.HBM((own, ffw), BF16), pltpu.HBM((own, tile), BF16)]
    own_scratch = [
        pltpu.VMEM((own, ffw), BF16),
        pltpu.VMEM((own, ffw), BF16),
        pltpu.VMEM((own, tile), BF16),
    ]
    weight_in, weight_out, d_pre_a, h_cut_a, back_a = call(
        functools.partial(own_first_kernel, tile),
        [*vmem_weights, *own_out, shape((own, feat_width + LANES))],
        [rows_a, *hbm_weights],
        10 * product,
        scratch=[*own_scratch, pltpu.SemaphoreType.DMA((2 * groups + 2,))],
        spaces=[pltpu.VMEM] + [pltpu.HBM] * 2,
    )
    weights = [
        pltpu.with_memory_space_constraint(w, pltpu.VMEM) for w in (weight_in, weight_out)
    ]
    d_pre_b, h_cut_b, back = call(
        functools.partial(own_second_kernel, tile, order),
        [*own_out, pltpu.HBM((slots_all, feat_width + LANES), BF16)],
        [rows_b, back_a, *weights],
        10 * product,
        scratch=[
            *own_scratch,
            pltpu.VMEM((slots_all, feat_width + LANES), BF16),
            pltpu.SemaphoreType.DMA((7,)),
        ],
    )
    back = lax.all_to_all(
        after(back, core_a, core_b).reshape(experts, capacity, feat_width + LANES), "expert", 0, 0, tiled=True
    ).reshape(slots_all, feat_width + LANES)
    relayed_a = [swap_cores(after(rows, d_pre_b)) for rows in chips_a]
    relayed_b = [swap_cores(rows) for rows in chips_b]
    early = [core_a, core_b, *chips_a]
    early_rows = sum(piece.shape[0] for piece in early)
    weight_in, weight_out, d_pre1, h_cut1 = call(
        functools.partial(early_kernel, tile, len(early)),
        [*vmem_weights, shape((early_rows, ffw)), shape((early_rows, tile))],
        [*early, *hbm_weights],
        product,
        scratch=[
            pltpu.VMEM((early_rows, 2 * feat_width), BF16),
            pltpu.VMEM((early_rows, ffw), BF16),
            pltpu.SemaphoreType.DMA((len(early) + 2 * groups,)),
        ],
        spaces=[pl.ANY] * len(early) + [pltpu.HBM] * 2,
    )
    late = [*relayed_a, *chips_b, *relayed_b]
    pieces = [rows_a, rows_b, *early, *late]
    rows_all = groups * slots_all
    weights = [
        pltpu.with_memory_space_constraint(w, pltpu.VMEM) for w in (weight_in, weight_out)
    ]
    grad_in, grad_out = call(
        functools.partial(grads_kernel, tile, len(pieces), len(late)),
        [
            pltpu.HBM((feat_width // groups, ffw), BF16),
            pltpu.HBM((ffw // groups, feat_width), BF16),
        ],
        [*pieces, d_pre_a, d_pre_b, d_pre1, h_cut_a, h_cut_b, h_cut1, *weights],
        4 * product,
        limit=32,
        scratch=[
            pltpu.VMEM((rows_all, 2 * feat_width), BF16),
            pltpu.VMEM((rows_all - slots_all - early_rows, ffw), BF16),
            pltpu.VMEM((rows_all, tile), BF16),
            pltpu.VMEM((rows_all, ffw), BF16),
            pltpu.VMEM((feat_width // groups, ffw), BF16),
            pltpu.VMEM((ffw // groups, feat_width), BF16),
            pltpu.SemaphoreType.DMA((len(pieces) + 6,)),
            pltpu.SemaphoreType.DMA((groups + 4,)),
        ],
        spaces=[pl.ANY] * len(pieces)
        + [pltpu.HBM, pltpu.HBM, pl.ANY] * 2
        + [pltpu.VMEM] * 2,
    )
    token_grads, gate_grads = call(
        functools.partial(combine_kernel, experts, capacity),
        [shape((tok_count, feat_width)), shape((2, tok_count))],
        [*places, gates.T, after(back, grad_in)],
        scratch=[pltpu.VMEM((slots_all, feat_width + LANES), BF16)],
    )
    return (token_grads, gate_grads.T, grad_in[None], grad_out[None])


def local_small_blocks(tokens, cotangent, routes, gates, proj_in, proj_out):
    tok_count, feat_width = tokens.shape
    experts = lax.axis_size("expert")
    groups = lax.axis_size("dp")
    me = lax.axis_index("dp")
    capacity = 2 * tok_count // experts
    slots_all = experts * capacity
    weight_in, weight_out = proj_in[0], proj_out[0]
    ffw = weight_in.shape[1]
    chosen = jnp.concatenate([routes[:, 0], routes[:, 1]])
    one_hot = (chosen[:, None] == jnp.arange(experts, dtype=jnp.int32)[None, :]).astype(jnp.int32)
    slot_pos = jnp.sum((jnp.cumsum(one_hot, axis=0) - one_hot) * one_hot, axis=1)
    target = jnp.where(slot_pos < capacity, chosen * capacity + slot_pos, slots_all)
    placing = (jnp.arange(slots_all, dtype=jnp.int32)[:, None] == target[None, :]).astype(BF16)
    either = placing[:, :tok_count] + placing[:, tok_count:]
    scaled = [
        (gates[:, k : k + 1].astype(F32) * cotangent.astype(F32)).astype(BF16) for k in range(2)
    ]

    def swap_blocks(rows):
        return lax.all_to_all(
            rows.astype(BF16).reshape(experts, capacity, rows.shape[1]), "expert", 0, 0, tiled=True
        ).reshape(slots_all, rows.shape[1])

    x = swap_blocks(dot(either, tokens))
    s = swap_blocks(dot(placing, jnp.concatenate(scaled, axis=0)))
    hidden0, slope0 = gelu_and_slope(dot(x, weight_in))
    d_hidden0 = dot(s, weight_out, (1, 1))
    d_pre0 = (d_hidden0 * slope0).astype(BF16)
    dgate = jnp.sum(hidden0.astype(F32) * d_hidden0, axis=1, keepdims=True)
    dx = dot(d_pre0, weight_in, (1, 1))
    back = swap_blocks(
        jnp.concatenate([dx, jnp.broadcast_to(dgate, (slots_all, LANES))], axis=1)
    )
    x_all = jnp.concatenate([x, *gather_groups(x)], axis=0)
    s_all = jnp.concatenate([s, *gather_groups(s)], axis=0)
    hidden1, slope1 = gelu_and_slope(dot(x_all[slots_all:], weight_in))
    d_pre1 = (dot(s_all[slots_all:], weight_out, (1, 1)) * slope1).astype(BF16)
    hidden = jnp.concatenate([hidden0, hidden1], axis=0)
    d_pre = jnp.concatenate([d_pre0, d_pre1], axis=0)
    x_cut = lax.dynamic_slice_in_dim(x_all, me * (feat_width // groups), feat_width // groups, 1)
    h_cut = lax.dynamic_slice_in_dim(hidden, me * (ffw // groups), ffw // groups, 1)
    grad_in = dot(x_cut, d_pre, (0, 0)).astype(BF16)
    grad_out = dot(h_cut, s_all, (0, 0)).astype(BF16)
    token_grads = dot(either, back[:, :feat_width], (0, 0)).astype(BF16)
    taken = dot(placing, back[:, feat_width : feat_width + 1], (0, 0))
    gate_grads = jnp.concatenate([taken[:tok_count], taken[tok_count:]], axis=1)
    gate_grads = (gate_grads / gates.astype(F32)).astype(BF16)
    return (token_grads, gate_grads, grad_in[None], grad_out[None])


def solution(mesh):
    rows = P(("dp", "expert"), None)
    weights = P("expert", None, None)

    def whole(tokens, *others):
        experts = mesh.shape["expert"]
        capacity = 2 * tokens.shape[0] // (mesh.shape["dp"] * experts) // experts
        tiles = capacity % 16 == 0 and experts & (experts - 1) == 0
        return jax.shard_map(
            local if tiles else local_small_blocks,
            mesh=mesh,
            in_specs=(rows, rows, rows, rows, weights, weights),
            out_specs=(rows, rows, P("expert", "dp", None), P("expert", "dp", None)),
            check_vma=False,
        )(tokens, *others)

    return whole
```

```python
import functools

import jax
import jax.numpy as jnp
from jax import lax
from jax.experimental import pallas as pl
from jax.experimental.pallas import tpu as pltpu
from jax.sharding import PartitionSpec as P

BF16 = jnp.bfloat16
F32 = jnp.float32
LANES = 128
MIB = 1 << 20


def dot(a, b, over=(1, 0)):
    return lax.dot_general(
        a, b, (((over[0],), (over[1],)), ((), ())), preferred_element_type=F32
    )


def gelu_and_slope(pre_act):
    cdf = 0.5 * (1.0 + lax.erf(pre_act * 0.7071067811865476))
    pdf = jnp.exp(-0.5 * pre_act * pre_act) * 0.3989422804014327
    return (pre_act * cdf).astype(BF16), cdf + pre_act * pdf


def call(kernel, out_shape, args, flops=0, limit=24, scratch=(), spaces=None):
    spaces = spaces or [pltpu.VMEM] * len(args)
    moved = sum(a.size * a.dtype.itemsize for a in args)
    args = [
        pltpu.with_memory_space_constraint(a, space) if space == pltpu.HBM else a
        for a, space in zip(args, spaces)
    ]
    return pl.pallas_call(
        kernel,
        out_shape=out_shape,
        in_specs=[pl.BlockSpec(memory_space=space) for space in spaces],
        out_specs=[
            pl.BlockSpec(memory_space=getattr(out, "memory_space", pltpu.VMEM))
            for out in out_shape
        ],
        scratch_shapes=list(scratch),
        compiler_params=pltpu.CompilerParams(vmem_limit_bytes=limit * MIB),
        cost_estimate=pl.CostEstimate(flops=flops, bytes_accessed=moved, transcendentals=0),
    )(*args)


def shape(dims, dtype=BF16):
    return jax.ShapeDtypeStruct(dims, dtype)


def route_kernel(experts, capacity, routes_hbm, gates_hbm, tokens_hbm, cotangent_hbm, *refs):
    blocks, place_refs, scratch = refs[:experts], refs[experts : experts + 2], refs[experts + 2 :]
    routes, gates, tokens, cotangent, sems = scratch
    copies = [
        pltpu.make_async_copy(source, target, sems.at[i])
        for i, (source, target) in enumerate(
            (
                (routes_hbm, routes),
                (gates_hbm, gates),
                (tokens_hbm, tokens),
                (cotangent_hbm, cotangent),
            )
        )
    ]
    for copy in copies:
        copy.start()
    tok_count, feat_width = tokens.shape
    slots_all = experts * capacity
    me = lax.axis_index("expert")
    rows = max(experts, 16)
    before = (
        lax.broadcasted_iota(jnp.int32, (tok_count, tok_count), 0)
        < lax.broadcasted_iota(jnp.int32, (tok_count, tok_count), 1)
    ).astype(F32).astype(BF16)
    expert_id = lax.broadcasted_iota(jnp.int32, (rows, tok_count), 0)
    slot_id = lax.broadcasted_iota(jnp.int32, (slots_all, tok_count), 0)
    taken = jnp.zeros((rows, 1), F32)
    places, gated = [], jnp.zeros((slots_all, tok_count), F32)
    copies[0].wait()
    copies[1].wait()
    for choice in range(2):
        chosen = routes[choice : choice + 1, :]
        one_hot = (expert_id == chosen).astype(F32)
        earlier = dot(one_hot.astype(BF16), before) + taken
        taken = taken + jnp.sum(one_hot, axis=1, keepdims=True)
        slot_pos = jnp.sum(earlier * one_hot, axis=0, keepdims=True).astype(jnp.int32)
        target = jnp.where(
            slot_pos < capacity, jnp.bitwise_xor(chosen, me) * capacity + slot_pos, slots_all
        )
        place = (slot_id == target).astype(F32)
        place_refs[choice][...] = place.astype(BF16)
        places.append(place)
        gated = gated + place * gates[choice : choice + 1, :].astype(F32)
    copies[2].wait()
    x = dot((places[0] + places[1]).astype(BF16), tokens[...]).astype(BF16)
    copies[3].wait()
    s = dot(gated.astype(BF16), cotangent[...]).astype(BF16)
    for k in range(experts):
        blocks[k][:, :feat_width] = x[k * capacity : (k + 1) * capacity]
        blocks[k][:, feat_width:] = s[k * capacity : (k + 1) * capacity]


def block_rows(me, k, capacity):
    return pl.ds(pl.multiple_of(jnp.bitwise_xor(me, k) * capacity, capacity), capacity)


def combine_kernel(experts, capacity, place0, place1, gates, back, token_grads, gate_grads, rows):
    tok_count, feat_width = token_grads.shape
    me = lax.axis_index("expert")
    for k in range(experts):
        rows[k * capacity : (k + 1) * capacity, :] = back[block_rows(me, k, capacity), :]
    either = (place0[...].astype(F32) + place1[...].astype(F32)).astype(BF16)
    token_grads[...] = dot(either, rows[:, :feat_width], (0, 0)).astype(BF16)
    dgate = rows[:, feat_width : feat_width + tok_count].astype(F32)
    taken = [
        jnp.sum(place[...].astype(F32) * dgate, axis=0, keepdims=True) for place in (place0, place1)
    ]
    gate_grads[...] = (jnp.concatenate(taken, axis=0) / gates[...].astype(F32)).astype(BF16)


def stack(refs, part, width):
    return jnp.concatenate([ref[:, part * width : (part + 1) * width] for ref in refs], axis=0)


def my_part(ref):
    width = ref.shape[1] // lax.axis_size("dp")
    return ref[:, pl.ds(pl.multiple_of(lax.axis_index("dp") * width, width), width)]


def fetcher(sems):
    count = iter(range(sems.shape[0]))

    def fetch(source, target):
        copy = pltpu.make_async_copy(source, target, sems.at[next(count)])
        copy.start()
        return copy

    return fetch


def own_kernel(tile, order, *refs):
    row_refs, refs = refs[:2], refs[2:]
    in_hbm, out_hbm, d_pre_hbm, h_cut_hbm, back_hbm, *scratch = refs
    weight_in, weight_out, hidden, d_pre, h_cut, back, sems = scratch
    me = lax.axis_index("expert")
    width, ffw = weight_in.shape
    tiles = [slice(at, at + tile) for at in range(0, ffw, tile)]
    fetch = fetcher(sems)
    copies = [
        (
            fetch(in_hbm.at[:, cols], weight_in.at[:, cols]),
            fetch(out_hbm.at[cols, :], weight_out.at[cols, :]),
        )
        for cols in tiles
    ]
    x, s = stack(row_refs, 0, width), stack(row_refs, 1, width)
    slots_all = x.shape[0]
    capacity = slots_all // len(order)
    dgate = jnp.zeros((slots_all, LANES), F32)
    for cols, (copy_in, copy_out) in zip(tiles, copies):
        copy_in.wait()
        act, slope = gelu_and_slope(dot(x, weight_in[:, cols]))
        hidden[:, cols] = act
        copy_out.wait()
        d_hidden = dot(s, weight_out[cols, :], (1, 1))
        d_pre[:, cols] = (d_hidden * slope).astype(BF16)
        product = d_hidden * act.astype(F32)
        for lane in range(0, tile, LANES):
            dgate = dgate + product[:, lane : lane + LANES]
    h_cut[...] = my_part(hidden)
    dgate = jnp.broadcast_to(jnp.sum(dgate, axis=1, keepdims=True), (slots_all, LANES))
    places = [
        (slice(i * capacity, (i + 1) * capacity), block_rows(me, k, capacity))
        for i, k in enumerate(order)
    ]
    for rows, target in places:
        back[target, width:] = dgate[rows].astype(BF16)
    outs = [
        fetch(d_pre, d_pre_hbm),
        fetch(h_cut, h_cut_hbm),
        fetch(back.at[:, width:], back_hbm.at[:, width:]),
    ]
    wide = width // 4
    for at in range(0, width, wide):
        cols = slice(at, at + wide)
        dx = dot(d_pre[...], weight_in[cols, :], (1, 1)).astype(BF16)
        for rows, target in places:
            back[target, cols] = dx[rows]
        outs.append(fetch(back.at[:, cols], back_hbm.at[:, cols]))
    for copy in outs:
        copy.wait()


def grads_kernel(tile, pieces, *refs):
    row_refs, refs = refs[:pieces], refs[pieces:]
    d_pre_own, h_cut_own, in_hbm, out_hbm, grad_in_hbm, grad_out_hbm, *scratch = refs
    rows, weight_in, weight_out, hidden, h_cut, d_pre, grad_in, grad_out, sems, out_sems = scratch
    width, ffw = weight_in.shape
    tiles = [slice(at, at + tile) for at in range(0, ffw, tile)]
    own, piece = d_pre_own.shape[0], row_refs[0].shape[0]
    fetch, send = fetcher(sems), fetcher(out_sems)

    def fetch_rows(which):
        return [fetch(row_refs[i], rows.at[pl.ds(i * piece, piece)]) for i in which]

    def fetch_weights(cols):
        return (
            fetch(in_hbm.at[:, cols], weight_in.at[:, cols]),
            fetch(out_hbm.at[cols, :], weight_out.at[cols, :]),
        )

    first = fetch_rows(range(own // piece, pieces))
    weights = [fetch_weights(tiles[0])]
    rest = fetch_rows(range(own // piece))
    rest.append(fetch(d_pre_own, d_pre.at[pl.ds(0, own)]))
    rest.append(fetch(h_cut_own, h_cut.at[pl.ds(0, own)]))
    weights += [fetch_weights(cols) for cols in tiles[1:]]
    for copy in first:
        copy.wait()
    x, s = rows[own:, :width], rows[own:, width:]
    cut = grad_in.shape[0]
    mine = pl.ds(pl.multiple_of(lax.axis_index("dp") * cut, cut), cut)
    outs = []
    for t, (cols, (copy_in, copy_out)) in enumerate(zip(tiles, weights)):
        copy_in.wait()
        act, slope = gelu_and_slope(dot(x, weight_in[:, cols]))
        hidden[:, cols] = act
        copy_out.wait()
        d_pre[own:, cols] = (dot(s, weight_out[cols, :], (1, 1)) * slope).astype(BF16)
        if t == 0:
            for copy in rest:
                copy.wait()
        grad_in[:, cols] = dot(rows[:, mine], d_pre[:, cols], (0, 0)).astype(BF16)
        outs.append(send(grad_in.at[:, cols], grad_in_hbm.at[:, cols]))
    h_cut[own:, :] = my_part(hidden)
    wide = width // 4
    for at in range(0, width, wide):
        cols = slice(at, at + wide)
        s_cols = slice(width + at, width + at + wide)
        grad_out[:, cols] = dot(h_cut[...], rows[:, s_cols], (0, 0)).astype(BF16)
        outs.append(send(grad_out.at[:, cols], grad_out_hbm.at[:, cols]))
    for copy in outs:
        copy.wait()


def after(value, *first):
    return lax.optimization_barrier((value, *first))[0]


def permute(block, k):
    return lax.ppermute(block, "expert", [(i, i ^ k) for i in range(lax.axis_size("expert"))])


def swap_cores(rows):
    return lax.ppermute(rows, "dp", [(i, i ^ 1) for i in range(lax.axis_size("dp"))])


def shift_chips(rows, k):
    groups = lax.axis_size("dp")
    return lax.ppermute(rows, "dp", [(i, (i + 2 * k) % groups) for i in range(groups)])


def gather_groups(rows):
    others = [swap_cores(rows)]
    for k in range(1, lax.axis_size("dp") // 2):
        other = shift_chips(rows, k)
        others += [other, swap_cores(other)]
    return others


def local(tokens, cotangent, routes, gates, proj_in, proj_out):
    tok_count, feat_width = tokens.shape
    experts = lax.axis_size("expert")
    groups = lax.axis_size("dp")
    capacity = 2 * tok_count // experts
    slots_all = experts * capacity
    half = experts // 2
    ffw = proj_in.shape[2]
    tile = ffw // groups
    product = 2 * slots_all * feat_width * ffw
    place = shape((slots_all, tok_count))

    routed = call(
        functools.partial(route_kernel, experts, capacity),
        [shape((capacity, 2 * feat_width))] * experts + [place] * 2,
        [routes.T, gates.T, tokens, cotangent],
        spaces=[pltpu.HBM] * 4,
        scratch=[
            pltpu.VMEM((2, tok_count), jnp.int32),
            pltpu.VMEM((2, tok_count), BF16),
            pltpu.VMEM((tok_count, feat_width), BF16),
            pltpu.VMEM((tok_count, feat_width), BF16),
            pltpu.SemaphoreType.DMA((4,)),
        ],
    )
    blocks, places = routed[:experts], routed[experts:]
    rest = list(range(experts - 1, 1, -1))
    order = [0, *rest[:2], 1, *rest[2:]]
    order_a, order_b = order[:half], order[half:]
    got_a = [blocks[0]] + [permute(blocks[k], k) for k in order_a[1:]]
    got_b = [
        permute(blocks[k] if i < 2 else after(blocks[k], got_a[1 - i]), k)
        for i, k in enumerate(order_b)
    ]
    rows_a = jnp.concatenate(got_a, axis=0)
    chips_a = [shift_chips(rows_a, k) for k in range(1, groups // 2)]
    core_a = swap_cores(after(rows_a, got_b[0]))
    rows_b = jnp.concatenate(got_b, axis=0)
    chips_b = [shift_chips(rows_b, k) for k in range(1, groups // 2)]
    core_b = swap_cores(rows_b)
    weights = [proj_in[0], proj_out[0]]
    weight_space = [pltpu.VMEM((feat_width, ffw), BF16), pltpu.VMEM((ffw, feat_width), BF16)]
    d_pre, h_cut, back = call(
        functools.partial(own_kernel, tile, order),
        [
            pltpu.HBM((slots_all, ffw), BF16),
            pltpu.HBM((slots_all, tile), BF16),
            pltpu.HBM((slots_all, feat_width + LANES), BF16),
        ],
        [rows_a, rows_b, *weights],
        20 * product,
        scratch=[
            *weight_space,
            pltpu.VMEM((slots_all, ffw), BF16),
            pltpu.VMEM((slots_all, ffw), BF16),
            pltpu.VMEM((slots_all, tile), BF16),
            pltpu.VMEM((slots_all, feat_width + LANES), BF16),
            pltpu.SemaphoreType.DMA((2 * groups + 7,)),
        ],
        spaces=[pltpu.VMEM] * 2 + [pltpu.HBM] * 2,
    )
    back = lax.all_to_all(
        after(back, core_a, core_b).reshape(experts, capacity, feat_width + LANES),
        "expert",
        0,
        0,
        tiled=True,
    ).reshape(slots_all, feat_width + LANES)
    relayed_a = [swap_cores(after(rows, d_pre)) for rows in chips_a]
    relayed_b = [swap_cores(rows) for rows in chips_b]
    pieces = [rows_a, rows_b, core_a, core_b, *chips_a, *relayed_a, *chips_b, *relayed_b]
    rows_all = groups * slots_all
    grad_in, grad_out = call(
        functools.partial(grads_kernel, tile, len(pieces)),
        [
            pltpu.HBM((feat_width // groups, ffw), BF16),
            pltpu.HBM((ffw // groups, feat_width), BF16),
        ],
        [*pieces, d_pre, h_cut, *weights],
        4 * product,
        limit=32,
        scratch=[
            pltpu.VMEM((rows_all, 2 * feat_width), BF16),
            *weight_space,
            pltpu.VMEM((rows_all - slots_all, ffw), BF16),
            pltpu.VMEM((rows_all, tile), BF16),
            pltpu.VMEM((rows_all, ffw), BF16),
            pltpu.VMEM((feat_width // groups, ffw), BF16),
            pltpu.VMEM((ffw // groups, feat_width), BF16),
            pltpu.SemaphoreType.DMA((len(pieces) + 2 * groups + 2,)),
            pltpu.SemaphoreType.DMA((groups + 4,)),
        ],
        spaces=[pl.ANY] * len(pieces) + [pltpu.HBM] * 4,
    )
    token_grads, gate_grads = call(
        functools.partial(combine_kernel, experts, capacity),
        [shape((tok_count, feat_width)), shape((2, tok_count))],
        [*places, gates.T, after(back, grad_in)],
        scratch=[pltpu.VMEM((slots_all, feat_width + LANES), BF16)],
    )
    return (token_grads, gate_grads.T, grad_in[None], grad_out[None])


def local_small_blocks(tokens, cotangent, routes, gates, proj_in, proj_out):
    tok_count, feat_width = tokens.shape
    experts = lax.axis_size("expert")
    groups = lax.axis_size("dp")
    me = lax.axis_index("dp")
    capacity = 2 * tok_count // experts
    slots_all = experts * capacity
    weight_in, weight_out = proj_in[0], proj_out[0]
    ffw = weight_in.shape[1]
    chosen = jnp.concatenate([routes[:, 0], routes[:, 1]])
    one_hot = (chosen[:, None] == jnp.arange(experts, dtype=jnp.int32)[None, :]).astype(jnp.int32)
    slot_pos = jnp.sum((jnp.cumsum(one_hot, axis=0) - one_hot) * one_hot, axis=1)
    target = jnp.where(slot_pos < capacity, chosen * capacity + slot_pos, slots_all)
    placing = (jnp.arange(slots_all, dtype=jnp.int32)[:, None] == target[None, :]).astype(BF16)
    either = placing[:, :tok_count] + placing[:, tok_count:]
    scaled = [
        (gates[:, k : k + 1].astype(F32) * cotangent.astype(F32)).astype(BF16) for k in range(2)
    ]

    def swap_blocks(rows):
        return lax.all_to_all(
            rows.astype(BF16).reshape(experts, capacity, rows.shape[1]), "expert", 0, 0, tiled=True
        ).reshape(slots_all, rows.shape[1])

    x = swap_blocks(dot(either, tokens))
    s = swap_blocks(dot(placing, jnp.concatenate(scaled, axis=0)))
    hidden0, slope0 = gelu_and_slope(dot(x, weight_in))
    d_hidden0 = dot(s, weight_out, (1, 1))
    d_pre0 = (d_hidden0 * slope0).astype(BF16)
    dgate = jnp.sum(hidden0.astype(F32) * d_hidden0, axis=1, keepdims=True)
    dx = dot(d_pre0, weight_in, (1, 1))
    back = swap_blocks(
        jnp.concatenate([dx, jnp.broadcast_to(dgate, (slots_all, LANES))], axis=1)
    )
    x_all = jnp.concatenate([x, *gather_groups(x)], axis=0)
    s_all = jnp.concatenate([s, *gather_groups(s)], axis=0)
    hidden1, slope1 = gelu_and_slope(dot(x_all[slots_all:], weight_in))
    d_pre1 = (dot(s_all[slots_all:], weight_out, (1, 1)) * slope1).astype(BF16)
    hidden = jnp.concatenate([hidden0, hidden1], axis=0)
    d_pre = jnp.concatenate([d_pre0, d_pre1], axis=0)
    x_cut = lax.dynamic_slice_in_dim(x_all, me * (feat_width // groups), feat_width // groups, 1)
    h_cut = lax.dynamic_slice_in_dim(hidden, me * (ffw // groups), ffw // groups, 1)
    grad_in = dot(x_cut, d_pre, (0, 0)).astype(BF16)
    grad_out = dot(h_cut, s_all, (0, 0)).astype(BF16)
    token_grads = dot(either, back[:, :feat_width], (0, 0)).astype(BF16)
    taken = dot(placing, back[:, feat_width : feat_width + 1], (0, 0))
    gate_grads = jnp.concatenate([taken[:tok_count], taken[tok_count:]], axis=1)
    gate_grads = (gate_grads / gates.astype(F32)).astype(BF16)
    return (token_grads, gate_grads, grad_in[None], grad_out[None])


def solution(mesh):
    rows = P(("dp", "expert"), None)
    weights = P("expert", None, None)

    def whole(tokens, *others):
        experts = mesh.shape["expert"]
        capacity = 2 * tokens.shape[0] // (mesh.shape["dp"] * experts) // experts
        tiles = capacity % 16 == 0 and experts & (experts - 1) == 0
        return jax.shard_map(
            local if tiles else local_small_blocks,
            mesh=mesh,
            in_specs=(rows, rows, rows, rows, weights, weights),
            out_specs=(rows, rows, P("expert", "dp", None), P("expert", "dp", None)),
            check_vma=False,
        )(tokens, *others)

    return whole
```

```python
import functools

import jax
import jax.numpy as jnp
from jax import lax
from jax.experimental import pallas as pl
from jax.experimental.pallas import tpu as pltpu
from jax.sharding import PartitionSpec as P

BF16 = jnp.bfloat16
F32 = jnp.float32
LANES = 128
MIB = 1 << 20


def dot(a, b, over=(1, 0)):
    return lax.dot_general(
        a, b, (((over[0],), (over[1],)), ((), ())), preferred_element_type=F32
    )


ERFCX = (
    0.253879726412498,
    0.2540954353994894,
    0.22517936671423447,
    0.19823402024047995,
    0.02224511740159976,
    0.22829329587490593,
    -0.2514442500538998,
    0.06951765914158435,
)


def gelu_and_slope(pre_act, invert=lambda v: 1.0 / v):
    gauss = jnp.exp(-0.5 * pre_act * pre_act)
    t = invert(1.0 + (0.45 * 0.7071067811865476) * jnp.abs(pre_act))
    poly = 0.5 * ERFCX[-1]
    for c in ERFCX[-2::-1]:
        poly = poly * t + 0.5 * c
    tail = gauss * t * poly
    cdf = jnp.where(pre_act < 0.0, tail, 1.0 - tail)
    return (pre_act * cdf).astype(BF16), cdf + pre_act * (gauss * 0.3989422804014327)


def activate(pre_act):
    return gelu_and_slope(
        pre_act, functools.partial(pltpu.reciprocal, approx=False, full_range=False)
    )


def call(kernel, out_shape, args, flops=0, limit=24, scratch=(), spaces=None):
    spaces = spaces or [pltpu.VMEM] * len(args)
    moved = sum(a.size * a.dtype.itemsize for a in args)
    args = [
        pltpu.with_memory_space_constraint(a, space) if space == pltpu.HBM else a
        for a, space in zip(args, spaces)
    ]
    return pl.pallas_call(
        kernel,
        out_shape=out_shape,
        in_specs=[pl.BlockSpec(memory_space=space) for space in spaces],
        out_specs=[
            pl.BlockSpec(memory_space=getattr(out, "memory_space", pltpu.VMEM))
            for out in out_shape
        ],
        scratch_shapes=list(scratch),
        compiler_params=pltpu.CompilerParams(vmem_limit_bytes=limit * MIB),
        cost_estimate=pl.CostEstimate(flops=flops, bytes_accessed=moved, transcendentals=0),
    )(*args)


def shape(dims, dtype=BF16):
    return jax.ShapeDtypeStruct(dims, dtype)


def route_kernel(experts, capacity, routes_hbm, gates_hbm, tokens_hbm, cotangent_hbm, *refs):
    blocks, place_refs, scratch = refs[:experts], refs[experts : experts + 2], refs[experts + 2 :]
    routes, gates, tokens, cotangent, sems = scratch
    copies = [
        pltpu.make_async_copy(source, target, sems.at[i])
        for i, (source, target) in enumerate(
            (
                (routes_hbm, routes),
                (gates_hbm, gates),
                (tokens_hbm, tokens),
                (cotangent_hbm, cotangent),
            )
        )
    ]
    for copy in copies:
        copy.start()
    tok_count, feat_width = tokens.shape
    slots_all = experts * capacity
    me = lax.axis_index("expert")
    rows = max(experts, 16)
    before = (
        lax.broadcasted_iota(jnp.int32, (tok_count, tok_count), 0)
        < lax.broadcasted_iota(jnp.int32, (tok_count, tok_count), 1)
    ).astype(F32).astype(BF16)
    expert_id = lax.broadcasted_iota(jnp.int32, (rows, tok_count), 0)
    slot_id = lax.broadcasted_iota(jnp.int32, (slots_all, tok_count), 0)
    taken = jnp.zeros((rows, 1), F32)
    places, gated = [], jnp.zeros((slots_all, tok_count), F32)
    copies[0].wait()
    copies[1].wait()
    for choice in range(2):
        chosen = routes[choice : choice + 1, :]
        one_hot = (expert_id == chosen).astype(F32)
        earlier = dot(one_hot.astype(BF16), before) + taken
        taken = taken + jnp.sum(one_hot, axis=1, keepdims=True)
        slot_pos = jnp.sum(earlier * one_hot, axis=0, keepdims=True).astype(jnp.int32)
        target = jnp.where(
            slot_pos < capacity, jnp.bitwise_xor(chosen, me) * capacity + slot_pos, slots_all
        )
        place = (slot_id == target).astype(F32)
        place_refs[choice][...] = place.astype(BF16)
        places.append(place)
        gated = gated + place * gates[choice : choice + 1, :].astype(F32)
    copies[2].wait()
    x = dot((places[0] + places[1]).astype(BF16), tokens[...]).astype(BF16)
    copies[3].wait()
    s = dot(gated.astype(BF16), cotangent[...]).astype(BF16)
    for k in range(experts):
        blocks[k][:, :feat_width] = x[k * capacity : (k + 1) * capacity]
        blocks[k][:, feat_width:] = s[k * capacity : (k + 1) * capacity]


def block_rows(me, k, capacity):
    return pl.ds(pl.multiple_of(jnp.bitwise_xor(me, k) * capacity, capacity), capacity)


def combine_kernel(experts, capacity, place0, place1, gates, back, token_grads, gate_grads, rows):
    tok_count, feat_width = token_grads.shape
    me = lax.axis_index("expert")
    for k in range(experts):
        rows[k * capacity : (k + 1) * capacity, :] = back[block_rows(me, k, capacity), :]
    either = (place0[...].astype(F32) + place1[...].astype(F32)).astype(BF16)
    token_grads[...] = dot(either, rows[:, :feat_width], (0, 0)).astype(BF16)
    dgate = rows[:, feat_width : feat_width + tok_count].astype(F32)
    taken = [
        jnp.sum(place[...].astype(F32) * dgate, axis=0, keepdims=True) for place in (place0, place1)
    ]
    gate_grads[...] = (jnp.concatenate(taken, axis=0) / gates[...].astype(F32)).astype(BF16)


def stack(refs, part, width):
    return jnp.concatenate([ref[:, part * width : (part + 1) * width] for ref in refs], axis=0)


def my_part(ref):
    width = ref.shape[1] // lax.axis_size("dp")
    return ref[:, pl.ds(pl.multiple_of(lax.axis_index("dp") * width, width), width)]


def fetcher(sems):
    count = iter(range(sems.shape[0]))

    def fetch(source, target):
        copy = pltpu.make_async_copy(source, target, sems.at[next(count)])
        copy.start()
        return copy

    return fetch


def own_kernel(tile, order, *refs):
    row_refs, refs = refs[:2], refs[2:]
    weight_in, weight_out, d_pre_hbm, h_cut_hbm, back_hbm, *scratch = refs
    hidden, d_pre, h_cut, back, sems = scratch
    me = lax.axis_index("expert")
    width, ffw = weight_in.shape
    tiles = [slice(at, at + tile) for at in range(0, ffw, tile)]
    fetch = fetcher(sems)
    x, s = stack(row_refs, 0, width), stack(row_refs, 1, width)
    slots_all = x.shape[0]
    capacity = slots_all // len(order)
    dgate = jnp.zeros((slots_all, LANES), F32)
    for cols in tiles:
        act, slope = activate(dot(x, weight_in[:, cols]))
        hidden[:, cols] = act
        d_hidden = dot(s, weight_out[cols, :], (1, 1))
        d_pre[:, cols] = (d_hidden * slope).astype(BF16)
        product = d_hidden * act.astype(F32)
        for lane in range(0, tile, LANES):
            dgate = dgate + product[:, lane : lane + LANES]
    h_cut[...] = my_part(hidden)
    dgate = jnp.broadcast_to(jnp.sum(dgate, axis=1, keepdims=True), (slots_all, LANES))
    places = [
        (slice(i * capacity, (i + 1) * capacity), block_rows(me, k, capacity))
        for i, k in enumerate(order)
    ]
    for rows, target in places:
        back[target, width:] = dgate[rows].astype(BF16)
    outs = [
        fetch(d_pre, d_pre_hbm),
        fetch(h_cut, h_cut_hbm),
        fetch(back.at[:, width:], back_hbm.at[:, width:]),
    ]
    wide = width // 4
    for at in range(0, width, wide):
        cols = slice(at, at + wide)
        dx = dot(d_pre[...], weight_in[cols, :], (1, 1)).astype(BF16)
        for rows, target in places:
            back[target, cols] = dx[rows]
        outs.append(fetch(back.at[:, cols], back_hbm.at[:, cols]))
    for copy in outs:
        copy.wait()


def grads_kernel(tile, pieces, *refs):
    row_refs, refs = refs[:pieces], refs[pieces:]
    d_pre_own, h_cut_own, in_hbm, out_hbm, grad_in_hbm, grad_out_hbm, *scratch = refs
    rows, weight_in, weight_out, hidden, h_cut, d_pre, grad_in, grad_out, sems, out_sems = scratch
    width, ffw = weight_in.shape
    tiles = [slice(at, at + tile) for at in range(0, ffw, tile)]
    own, piece = d_pre_own.shape[0], row_refs[0].shape[0]
    fetch, send = fetcher(sems), fetcher(out_sems)

    def fetch_rows(which):
        return [fetch(row_refs[i], rows.at[pl.ds(i * piece, piece)]) for i in which]

    def fetch_weights(cols):
        return (
            fetch(in_hbm.at[:, cols], weight_in.at[:, cols]),
            fetch(out_hbm.at[cols, :], weight_out.at[cols, :]),
        )

    first = fetch_rows(range(own // piece, pieces))
    weights = [fetch_weights(tiles[0])]
    rest = fetch_rows(range(own // piece))
    rest.append(fetch(d_pre_own, d_pre.at[pl.ds(0, own)]))
    rest.append(fetch(h_cut_own, h_cut.at[pl.ds(0, own)]))
    weights += [fetch_weights(cols) for cols in tiles[1:]]
    for copy in first:
        copy.wait()
    x, s = rows[own:, :width], rows[own:, width:]
    cut = grad_in.shape[0]
    mine = pl.ds(pl.multiple_of(lax.axis_index("dp") * cut, cut), cut)
    outs = []
    for t, cols in enumerate(tiles):
        if t == 1:
            for copy in [copy for pair in weights[1:] for copy in pair] + rest:
                copy.wait()
        if t == 0:
            for copy in weights[0]:
                copy.wait()
        act, slope = activate(dot(x, weight_in[:, cols]))
        hidden[:, cols] = act
        d_pre[own:, cols] = (dot(s, weight_out[cols, :], (1, 1)) * slope).astype(BF16)
    for cols in tiles:
        grad_in[:, cols] = dot(rows[:, mine], d_pre[:, cols], (0, 0)).astype(BF16)
        outs.append(send(grad_in.at[:, cols], grad_in_hbm.at[:, cols]))
    h_cut[own:, :] = my_part(hidden)
    wide = width // 4
    for at in range(0, width, wide):
        cols = slice(at, at + wide)
        s_cols = slice(width + at, width + at + wide)
        grad_out[:, cols] = dot(h_cut[...], rows[:, s_cols], (0, 0)).astype(BF16)
        outs.append(send(grad_out.at[:, cols], grad_out_hbm.at[:, cols]))
    for copy in outs:
        copy.wait()


def after(value, *first):
    return lax.optimization_barrier((value, *first))[0]


def permute(block, k):
    return lax.ppermute(block, "expert", [(i, i ^ k) for i in range(lax.axis_size("expert"))])


def swap_cores(rows):
    return lax.ppermute(rows, "dp", [(i, i ^ 1) for i in range(lax.axis_size("dp"))])


def shift_chips(rows, k):
    groups = lax.axis_size("dp")
    return lax.ppermute(rows, "dp", [(i, (i + 2 * k) % groups) for i in range(groups)])


def gather_groups(rows):
    others = [swap_cores(rows)]
    for k in range(1, lax.axis_size("dp") // 2):
        other = shift_chips(rows, k)
        others += [other, swap_cores(other)]
    return others


def local(tokens, cotangent, routes, gates, proj_in, proj_out):
    tok_count, feat_width = tokens.shape
    experts = lax.axis_size("expert")
    groups = lax.axis_size("dp")
    capacity = 2 * tok_count // experts
    slots_all = experts * capacity
    half = experts // 2
    ffw = proj_in.shape[2]
    tile = ffw // groups
    product = 2 * slots_all * feat_width * ffw
    place = shape((slots_all, tok_count))

    routed = call(
        functools.partial(route_kernel, experts, capacity),
        [shape((capacity, 2 * feat_width))] * experts + [place] * 2,
        [routes.T, gates.T, tokens, cotangent],
        30 * product,
        spaces=[pltpu.HBM] * 4,
        scratch=[
            pltpu.VMEM((2, tok_count), jnp.int32),
            pltpu.VMEM((2, tok_count), BF16),
            pltpu.VMEM((tok_count, feat_width), BF16),
            pltpu.VMEM((tok_count, feat_width), BF16),
            pltpu.SemaphoreType.DMA((4,)),
        ],
    )
    blocks, places = routed[:experts], routed[experts:]
    rest = list(range(experts - 1, 1, -1))
    if len(rest) > 4:
        rest.insert(2, rest.pop(-2))
    order = [0, *rest[:2], 1, *rest[2:]]
    order_a, order_b = order[:half], order[half:]
    got_a = [blocks[0]] + [permute(blocks[k], k) for k in order_a[1:]]
    got_b = [
        permute(blocks[k] if i < 2 else after(blocks[k], got_a[-1]), k)
        for i, k in enumerate(order_b)
    ]
    rows_a = jnp.concatenate(got_a, axis=0)
    chips_a = [shift_chips(rows_a, k) for k in range(1, groups // 2)]
    core_a = swap_cores(after(rows_a, got_b[0]))
    rows_b = jnp.concatenate(got_b, axis=0)
    chips_b = [shift_chips(rows_b, k) for k in range(1, groups // 2)]
    core_b = swap_cores(rows_b)
    weights = [proj_in[0], proj_out[0]]
    weight_space = [pltpu.VMEM((feat_width, ffw), BF16), pltpu.VMEM((ffw, feat_width), BF16)]
    d_pre, h_cut, back = call(
        functools.partial(own_kernel, tile, order),
        [
            pltpu.HBM((slots_all, ffw), BF16),
            pltpu.HBM((slots_all, tile), BF16),
            pltpu.HBM((slots_all, feat_width + LANES), BF16),
        ],
        [
            rows_a,
            rows_b,
            *[pltpu.with_memory_space_constraint(w, pltpu.VMEM) for w in weights],
        ],
        20 * product,
        scratch=[
            pltpu.VMEM((slots_all, ffw), BF16),
            pltpu.VMEM((slots_all, ffw), BF16),
            pltpu.VMEM((slots_all, tile), BF16),
            pltpu.VMEM((slots_all, feat_width + LANES), BF16),
            pltpu.SemaphoreType.DMA((7,)),
        ],
    )
    back = lax.all_to_all(
        after(back, core_a, core_b).reshape(experts, capacity, feat_width + LANES),
        "expert",
        0,
        0,
        tiled=True,
    ).reshape(slots_all, feat_width + LANES)
    relayed_a = [swap_cores(after(rows, d_pre)) for rows in chips_a]
    relayed_b = [swap_cores(rows) for rows in chips_b]
    pieces = [rows_a, rows_b, core_a, core_b, *chips_a, *relayed_a, *chips_b, *relayed_b]
    rows_all = groups * slots_all
    grad_in, grad_out = call(
        functools.partial(grads_kernel, tile, len(pieces)),
        [
            pltpu.HBM((feat_width // groups, ffw), BF16),
            pltpu.HBM((ffw // groups, feat_width), BF16),
        ],
        [*pieces, d_pre, h_cut, *weights],
        4 * product,
        limit=32,
        scratch=[
            pltpu.VMEM((rows_all, 2 * feat_width), BF16),
            *weight_space,
            pltpu.VMEM((rows_all - slots_all, ffw), BF16),
            pltpu.VMEM((rows_all, tile), BF16),
            pltpu.VMEM((rows_all, ffw), BF16),
            pltpu.VMEM((feat_width // groups, ffw), BF16),
            pltpu.VMEM((ffw // groups, feat_width), BF16),
            pltpu.SemaphoreType.DMA((len(pieces) + 2 * groups + 2,)),
            pltpu.SemaphoreType.DMA((groups + 4,)),
        ],
        spaces=[pl.ANY] * len(pieces) + [pltpu.HBM] * 4,
    )
    token_grads, gate_grads = call(
        functools.partial(combine_kernel, experts, capacity),
        [shape((tok_count, feat_width)), shape((2, tok_count))],
        [*places, gates.T, after(back, grad_in)],
        scratch=[pltpu.VMEM((slots_all, feat_width + LANES), BF16)],
    )
    return (token_grads, gate_grads.T, grad_in[None], grad_out[None])


def local_small_blocks(tokens, cotangent, routes, gates, proj_in, proj_out):
    tok_count, feat_width = tokens.shape
    experts = lax.axis_size("expert")
    groups = lax.axis_size("dp")
    me = lax.axis_index("dp")
    capacity = 2 * tok_count // experts
    slots_all = experts * capacity
    weight_in, weight_out = proj_in[0], proj_out[0]
    ffw = weight_in.shape[1]
    chosen = jnp.concatenate([routes[:, 0], routes[:, 1]])
    one_hot = (chosen[:, None] == jnp.arange(experts, dtype=jnp.int32)[None, :]).astype(jnp.int32)
    slot_pos = jnp.sum((jnp.cumsum(one_hot, axis=0) - one_hot) * one_hot, axis=1)
    target = jnp.where(slot_pos < capacity, chosen * capacity + slot_pos, slots_all)
    placing = (jnp.arange(slots_all, dtype=jnp.int32)[:, None] == target[None, :]).astype(BF16)
    either = placing[:, :tok_count] + placing[:, tok_count:]
    scaled = [
        (gates[:, k : k + 1].astype(F32) * cotangent.astype(F32)).astype(BF16) for k in range(2)
    ]

    def swap_blocks(rows):
        return lax.all_to_all(
            rows.astype(BF16).reshape(experts, capacity, rows.shape[1]), "expert", 0, 0, tiled=True
        ).reshape(slots_all, rows.shape[1])

    x = swap_blocks(dot(either, tokens))
    s = swap_blocks(dot(placing, jnp.concatenate(scaled, axis=0)))
    hidden0, slope0 = gelu_and_slope(dot(x, weight_in))
    d_hidden0 = dot(s, weight_out, (1, 1))
    d_pre0 = (d_hidden0 * slope0).astype(BF16)
    dgate = jnp.sum(hidden0.astype(F32) * d_hidden0, axis=1, keepdims=True)
    dx = dot(d_pre0, weight_in, (1, 1))
    back = swap_blocks(
        jnp.concatenate([dx, jnp.broadcast_to(dgate, (slots_all, LANES))], axis=1)
    )
    x_all = jnp.concatenate([x, *gather_groups(x)], axis=0)
    s_all = jnp.concatenate([s, *gather_groups(s)], axis=0)
    hidden1, slope1 = gelu_and_slope(dot(x_all[slots_all:], weight_in))
    d_pre1 = (dot(s_all[slots_all:], weight_out, (1, 1)) * slope1).astype(BF16)
    hidden = jnp.concatenate([hidden0, hidden1], axis=0)
    d_pre = jnp.concatenate([d_pre0, d_pre1], axis=0)
    x_cut = lax.dynamic_slice_in_dim(x_all, me * (feat_width // groups), feat_width // groups, 1)
    h_cut = lax.dynamic_slice_in_dim(hidden, me * (ffw // groups), ffw // groups, 1)
    grad_in = dot(x_cut, d_pre, (0, 0)).astype(BF16)
    grad_out = dot(h_cut, s_all, (0, 0)).astype(BF16)
    token_grads = dot(either, back[:, :feat_width], (0, 0)).astype(BF16)
    taken = dot(placing, back[:, feat_width : feat_width + 1], (0, 0))
    gate_grads = jnp.concatenate([taken[:tok_count], taken[tok_count:]], axis=1)
    gate_grads = (gate_grads / gates.astype(F32)).astype(BF16)
    return (token_grads, gate_grads, grad_in[None], grad_out[None])


def solution(mesh):
    rows = P(("dp", "expert"), None)
    weights = P("expert", None, None)

    def whole(tokens, *others):
        experts = mesh.shape["expert"]
        capacity = 2 * tokens.shape[0] // (mesh.shape["dp"] * experts) // experts
        tiles = capacity % 16 == 0 and experts & (experts - 1) == 0
        return jax.shard_map(
            local if tiles else local_small_blocks,
            mesh=mesh,
            in_specs=(rows, rows, rows, rows, weights, weights),
            out_specs=(rows, rows, P("expert", "dp", None), P("expert", "dp", None)),
            check_vma=False,
        )(tokens, *others)

    return whole
```

```python
import functools

import jax
import jax.numpy as jnp
from jax import lax
from jax.experimental import pallas as pl
from jax.experimental.pallas import tpu as pltpu
from jax.sharding import PartitionSpec as P

BF16 = jnp.bfloat16
F32 = jnp.float32
LANES = 128
MIB = 1 << 20


def dot(a, b, over=(1, 0)):
    return lax.dot_general(
        a, b, (((over[0],), (over[1],)), ((), ())), preferred_element_type=F32
    )


def activate(pre_act):
    cdf = 0.5 * (1.0 + lax.erf(pre_act * 0.7071067811865476))
    pdf = jnp.exp(-0.5 * pre_act * pre_act) * 0.3989422804014327
    return (pre_act * cdf).astype(BF16), cdf + pre_act * pdf


def call(kernel, out_shape, args, flops=0, limit=24, scratch=(), spaces=None):
    spaces = spaces or [pltpu.VMEM] * len(args)
    moved = sum(a.size * a.dtype.itemsize for a in args)
    args = [
        pltpu.with_memory_space_constraint(a, space) if space == pltpu.HBM else a
        for a, space in zip(args, spaces)
    ]
    return pl.pallas_call(
        kernel,
        out_shape=out_shape,
        in_specs=[pl.BlockSpec(memory_space=space) for space in spaces],
        out_specs=[
            pl.BlockSpec(memory_space=getattr(out, "memory_space", pltpu.VMEM))
            for out in out_shape
        ],
        scratch_shapes=list(scratch),
        compiler_params=pltpu.CompilerParams(vmem_limit_bytes=limit * MIB),
        cost_estimate=pl.CostEstimate(flops=flops, bytes_accessed=moved, transcendentals=0),
    )(*args)


def shape(dims, dtype=BF16):
    return jax.ShapeDtypeStruct(dims, dtype)


def route_kernel(experts, capacity, routes_hbm, gates_hbm, tokens_hbm, cotangent_hbm, *refs):
    blocks, place_refs, scratch = refs[:experts], refs[experts : experts + 2], refs[experts + 2 :]
    routes, gates, tokens, cotangent, sems = scratch
    copies = [
        pltpu.make_async_copy(source, target, sems.at[i])
        for i, (source, target) in enumerate(
            (
                (routes_hbm, routes),
                (gates_hbm, gates),
                (tokens_hbm, tokens),
                (cotangent_hbm, cotangent),
            )
        )
    ]
    for copy in copies:
        copy.start()
    tok_count, feat_width = tokens.shape
    slots_all = experts * capacity
    me = lax.axis_index("expert")
    rows = max(experts, 16)
    before = (
        lax.broadcasted_iota(jnp.int32, (tok_count, tok_count), 0)
        < lax.broadcasted_iota(jnp.int32, (tok_count, tok_count), 1)
    ).astype(F32).astype(BF16)
    expert_id = lax.broadcasted_iota(jnp.int32, (rows, tok_count), 0)
    slot_id = lax.broadcasted_iota(jnp.int32, (slots_all, tok_count), 0)
    taken = jnp.zeros((rows, 1), F32)
    places, gated = [], jnp.zeros((slots_all, tok_count), F32)
    copies[0].wait()
    copies[1].wait()
    for choice in range(2):
        chosen = routes[choice : choice + 1, :]
        one_hot = (expert_id == chosen).astype(F32)
        earlier = dot(one_hot.astype(BF16), before) + taken
        taken = taken + jnp.sum(one_hot, axis=1, keepdims=True)
        slot_pos = jnp.sum(earlier * one_hot, axis=0, keepdims=True).astype(jnp.int32)
        target = jnp.where(
            slot_pos < capacity, jnp.bitwise_xor(chosen, me) * capacity + slot_pos, slots_all
        )
        place = (slot_id == target).astype(F32)
        place_refs[choice][...] = place.astype(BF16)
        places.append(place)
        gated = gated + place * gates[choice : choice + 1, :].astype(F32)
    copies[2].wait()
    x = dot((places[0] + places[1]).astype(BF16), tokens[...]).astype(BF16)
    copies[3].wait()
    s = dot(gated.astype(BF16), cotangent[...]).astype(BF16)
    for k in range(experts):
        blocks[k][:, :feat_width] = x[k * capacity : (k + 1) * capacity]
        blocks[k][:, feat_width:] = s[k * capacity : (k + 1) * capacity]


def block_rows(me, k, capacity):
    return pl.ds(pl.multiple_of(jnp.bitwise_xor(me, k) * capacity, capacity), capacity)


def combine_kernel(experts, capacity, place0, place1, gates, back, token_grads, gate_grads, rows):
    tok_count, feat_width = token_grads.shape
    me = lax.axis_index("expert")
    for k in range(experts):
        rows[k * capacity : (k + 1) * capacity, :] = back[block_rows(me, k, capacity), :]
    either = (place0[...].astype(F32) + place1[...].astype(F32)).astype(BF16)
    token_grads[...] = dot(either, rows[:, :feat_width], (0, 0)).astype(BF16)
    dgate = rows[:, feat_width : feat_width + tok_count].astype(F32)
    taken = [
        jnp.sum(place[...].astype(F32) * dgate, axis=0, keepdims=True) for place in (place0, place1)
    ]
    gate_grads[...] = (jnp.concatenate(taken, axis=0) / gates[...].astype(F32)).astype(BF16)


def stack(refs, part, width):
    return jnp.concatenate([ref[:, part * width : (part + 1) * width] for ref in refs], axis=0)


def my_part(ref):
    width = ref.shape[1] // lax.axis_size("dp")
    return ref[:, pl.ds(pl.multiple_of(lax.axis_index("dp") * width, width), width)]


def fetcher(sems):
    count = iter(range(sems.shape[0]))

    def fetch(source, target):
        copy = pltpu.make_async_copy(source, target, sems.at[next(count)])
        copy.start()
        return copy

    return fetch


def own_kernel(tile, order, *refs):
    row_refs, refs = refs[:2], refs[2:]
    weight_in, weight_out, d_pre_hbm, h_cut_hbm, back_hbm, *scratch = refs
    hidden, d_pre, h_cut, back, sems = scratch
    me = lax.axis_index("expert")
    width, ffw = weight_in.shape
    tiles = [slice(at, at + tile) for at in range(0, ffw, tile)]
    fetch = fetcher(sems)
    x, s = stack(row_refs, 0, width), stack(row_refs, 1, width)
    slots_all = x.shape[0]
    capacity = slots_all // len(order)
    dgate = jnp.zeros((slots_all, LANES), F32)
    for cols in tiles:
        act, slope = activate(dot(x, weight_in[:, cols]))
        hidden[:, cols] = act
        d_hidden = dot(s, weight_out[cols, :], (1, 1))
        d_pre[:, cols] = (d_hidden * slope).astype(BF16)
        product = d_hidden * act.astype(F32)
        for lane in range(0, tile, LANES):
            dgate = dgate + product[:, lane : lane + LANES]
    h_cut[...] = my_part(hidden)
    dgate = jnp.broadcast_to(jnp.sum(dgate, axis=1, keepdims=True), (slots_all, LANES))
    places = [
        (slice(i * capacity, (i + 1) * capacity), block_rows(me, k, capacity))
        for i, k in enumerate(order)
    ]
    for rows, target in places:
        back[target, width:] = dgate[rows].astype(BF16)
    outs = [
        fetch(d_pre, d_pre_hbm),
        fetch(h_cut, h_cut_hbm),
        fetch(back.at[:, width:], back_hbm.at[:, width:]),
    ]
    wide = width // 4
    for at in range(0, width, wide):
        cols = slice(at, at + wide)
        dx = dot(d_pre[...], weight_in[cols, :], (1, 1)).astype(BF16)
        for rows, target in places:
            back[target, cols] = dx[rows]
        outs.append(fetch(back.at[:, cols], back_hbm.at[:, cols]))
    for copy in outs:
        copy.wait()


def early_kernel(tile, pieces, *refs):
    row_refs, refs = refs[:pieces], refs[pieces:]
    in_hbm, out_hbm, weight_in, weight_out, d_pre, h_cut, rows, hidden, sems = refs
    width, ffw = weight_in.shape
    piece = row_refs[0].shape[0]
    tiles = [slice(at, at + tile) for at in range(0, ffw, tile)]
    fetch = fetcher(sems)
    first = [fetch(ref, rows.at[pl.ds(i * piece, piece)]) for i, ref in enumerate(row_refs)]
    weights = [
        (
            fetch(in_hbm.at[:, cols], weight_in.at[:, cols]),
            fetch(out_hbm.at[cols, :], weight_out.at[cols, :]),
        )
        for cols in tiles
    ]
    for copy in first:
        copy.wait()
    x, s = rows[:, :width], rows[:, width:]
    for cols, (copy_in, copy_out) in zip(tiles, weights):
        copy_in.wait()
        copy_out.wait()
        act, slope = activate(dot(x, weight_in[:, cols]))
        hidden[:, cols] = act
        d_pre[:, cols] = (dot(s, weight_out[cols, :], (1, 1)) * slope).astype(BF16)
    h_cut[...] = my_part(hidden)


def grads_kernel(tile, pieces, late, *refs):
    row_refs, refs = refs[:pieces], refs[pieces:]
    d_pre_refs, h_cut_refs, refs = refs[:2], refs[2:4], refs[4:]
    weight_in, weight_out, grad_in_hbm, grad_out_hbm, *scratch = refs
    rows, hidden, h_cut, d_pre, grad_in, grad_out, sems, out_sems = scratch
    width, ffw = weight_in.shape
    tiles = [slice(at, at + tile) for at in range(0, ffw, tile)]
    piece = row_refs[0].shape[0]
    known = (pieces - late) * piece
    fetch, send = fetcher(sems), fetcher(out_sems)
    copies = [
        fetch(row_refs[i], rows.at[pl.ds(i * piece, piece)])
        for i in [*range(pieces - late, pieces), *range(pieces - late)]
    ]
    at = 0
    for source, cut_source in zip(d_pre_refs, h_cut_refs):
        span = pl.ds(at, source.shape[0])
        copies += [fetch(source, d_pre.at[span]), fetch(cut_source, h_cut.at[span])]
        at += source.shape[0]
    for copy in copies[:late]:
        copy.wait()
    x, s = rows[known:, :width], rows[known:, width:]
    for cols in tiles:
        act, slope = activate(dot(x, weight_in[:, cols]))
        hidden[:, cols] = act
        d_pre[known:, cols] = (dot(s, weight_out[cols, :], (1, 1)) * slope).astype(BF16)
    for copy in copies[late:]:
        copy.wait()
    cut = grad_in.shape[0]
    mine = pl.ds(pl.multiple_of(lax.axis_index("dp") * cut, cut), cut)
    outs = []
    for cols in tiles:
        grad_in[:, cols] = dot(rows[:, mine], d_pre[:, cols], (0, 0)).astype(BF16)
        outs.append(send(grad_in.at[:, cols], grad_in_hbm.at[:, cols]))
    h_cut[known:, :] = my_part(hidden)
    wide = width // 4
    for at in range(0, width, wide):
        cols = slice(at, at + wide)
        s_cols = slice(width + at, width + at + wide)
        grad_out[:, cols] = dot(h_cut[...], rows[:, s_cols], (0, 0)).astype(BF16)
        outs.append(send(grad_out.at[:, cols], grad_out_hbm.at[:, cols]))
    for copy in outs:
        copy.wait()


def after(value, *first):
    return lax.optimization_barrier((value, *first))[0]


def permute(block, k):
    return lax.ppermute(block, "expert", [(i, i ^ k) for i in range(lax.axis_size("expert"))])


def swap_cores(rows):
    return lax.ppermute(rows, "dp", [(i, i ^ 1) for i in range(lax.axis_size("dp"))])


def shift_chips(rows, k):
    groups = lax.axis_size("dp")
    return lax.ppermute(rows, "dp", [(i, (i + 2 * k) % groups) for i in range(groups)])


def gather_groups(rows):
    others = [swap_cores(rows)]
    for k in range(1, lax.axis_size("dp") // 2):
        other = shift_chips(rows, k)
        others += [other, swap_cores(other)]
    return others


def local(tokens, cotangent, routes, gates, proj_in, proj_out):
    tok_count, feat_width = tokens.shape
    experts = lax.axis_size("expert")
    groups = lax.axis_size("dp")
    capacity = 2 * tok_count // experts
    slots_all = experts * capacity
    half = experts // 2
    ffw = proj_in.shape[2]
    tile = ffw // groups
    product = 2 * slots_all * feat_width * ffw
    place = shape((slots_all, tok_count))

    routed = call(
        functools.partial(route_kernel, experts, capacity),
        [shape((capacity, 2 * feat_width))] * experts + [place] * 2,
        [routes.T, gates.T, tokens, cotangent],
        30 * product,
        spaces=[pltpu.HBM] * 4,
        scratch=[
            pltpu.VMEM((2, tok_count), jnp.int32),
            pltpu.VMEM((2, tok_count), BF16),
            pltpu.VMEM((tok_count, feat_width), BF16),
            pltpu.VMEM((tok_count, feat_width), BF16),
            pltpu.SemaphoreType.DMA((4,)),
        ],
    )
    blocks, places = routed[:experts], routed[experts:]
    rest = list(range(experts - 1, 1, -1))
    if len(rest) > 4:
        rest.insert(2, rest.pop(-2))
    order = [0, *rest[:2], 1, *rest[2:]]
    order_a, order_b = order[:half], order[half:]
    got_a = [blocks[0]] + [permute(blocks[k], k) for k in order_a[1:]]
    got_b = [
        permute(blocks[k] if i < 2 else after(blocks[k], got_a[-1]), k)
        for i, k in enumerate(order_b)
    ]
    rows_a = jnp.concatenate(got_a, axis=0)
    chips_a = [shift_chips(rows_a, k) for k in range(1, groups // 2)]
    core_a = swap_cores(after(rows_a, got_b[0]))
    rows_b = jnp.concatenate(got_b, axis=0)
    chips_b = [shift_chips(rows_b, k) for k in range(1, groups // 2)]
    core_b = swap_cores(rows_b)
    weights = [proj_in[0], proj_out[0]]
    weight_space = [pltpu.VMEM((feat_width, ffw), BF16), pltpu.VMEM((ffw, feat_width), BF16)]
    d_pre, h_cut, back = call(
        functools.partial(own_kernel, tile, order),
        [
            pltpu.HBM((slots_all, ffw), BF16),
            pltpu.HBM((slots_all, tile), BF16),
            pltpu.HBM((slots_all, feat_width + LANES), BF16),
        ],
        [
            rows_a,
            rows_b,
            *[pltpu.with_memory_space_constraint(w, pltpu.VMEM) for w in weights],
        ],
        20 * product,
        scratch=[
            pltpu.VMEM((slots_all, ffw), BF16),
            pltpu.VMEM((slots_all, ffw), BF16),
            pltpu.VMEM((slots_all, tile), BF16),
            pltpu.VMEM((slots_all, feat_width + LANES), BF16),
            pltpu.SemaphoreType.DMA((7,)),
        ],
    )
    back = lax.all_to_all(
        after(back, core_a, core_b).reshape(experts, capacity, feat_width + LANES),
        "expert",
        0,
        0,
        tiled=True,
    ).reshape(slots_all, feat_width + LANES)
    relayed_a = [swap_cores(after(rows, d_pre)) for rows in chips_a]
    relayed_b = [swap_cores(rows) for rows in chips_b]
    early = [core_a, core_b, *chips_a]
    late = [*relayed_a, *chips_b, *relayed_b]
    early_rows = sum(piece.shape[0] for piece in early)
    late_rows = sum(piece.shape[0] for piece in late)
    weight_in, weight_out, d_pre_early, h_cut_early = call(
        functools.partial(early_kernel, tile, len(early)),
        [*weight_space, shape((early_rows, ffw)), shape((early_rows, tile))],
        [*early, *weights],
        2 * product,
        scratch=[
            pltpu.VMEM((early_rows, 2 * feat_width), BF16),
            pltpu.VMEM((early_rows, ffw), BF16),
            pltpu.SemaphoreType.DMA((len(early) + 2 * groups,)),
        ],
        spaces=[pl.ANY] * len(early) + [pltpu.HBM] * 2,
    )
    pieces = [rows_a, rows_b, *early, *late]
    rows_all = groups * slots_all
    grad_in, grad_out = call(
        functools.partial(grads_kernel, tile, len(pieces), len(late)),
        [
            pltpu.HBM((feat_width // groups, ffw), BF16),
            pltpu.HBM((ffw // groups, feat_width), BF16),
        ],
        [
            *pieces,
            *[d_pre, d_pre_early, h_cut, h_cut_early],
            *[
                pltpu.with_memory_space_constraint(w, pltpu.VMEM)
                for w in (weight_in, weight_out)
            ],
        ],
        4 * product,
        limit=32,
        scratch=[
            pltpu.VMEM((rows_all, 2 * feat_width), BF16),
            pltpu.VMEM((late_rows, ffw), BF16),
            pltpu.VMEM((rows_all, tile), BF16),
            pltpu.VMEM((rows_all, ffw), BF16),
            pltpu.VMEM((feat_width // groups, ffw), BF16),
            pltpu.VMEM((ffw // groups, feat_width), BF16),
            pltpu.SemaphoreType.DMA((len(pieces) + 4,)),
            pltpu.SemaphoreType.DMA((groups + 4,)),
        ],
        spaces=[pl.ANY] * len(pieces)
        + [pltpu.HBM, pl.ANY] * 2
        + [pltpu.VMEM] * 2,
    )
    token_grads, gate_grads = call(
        functools.partial(combine_kernel, experts, capacity),
        [shape((tok_count, feat_width)), shape((2, tok_count))],
        [*places, gates.T, after(back, grad_in)],
        scratch=[pltpu.VMEM((slots_all, feat_width + LANES), BF16)],
    )
    return (token_grads, gate_grads.T, grad_in[None], grad_out[None])


def local_small_blocks(tokens, cotangent, routes, gates, proj_in, proj_out):
    tok_count, feat_width = tokens.shape
    experts = lax.axis_size("expert")
    groups = lax.axis_size("dp")
    me = lax.axis_index("dp")
    capacity = 2 * tok_count // experts
    slots_all = experts * capacity
    weight_in, weight_out = proj_in[0], proj_out[0]
    ffw = weight_in.shape[1]
    chosen = jnp.concatenate([routes[:, 0], routes[:, 1]])
    one_hot = (chosen[:, None] == jnp.arange(experts, dtype=jnp.int32)[None, :]).astype(jnp.int32)
    slot_pos = jnp.sum((jnp.cumsum(one_hot, axis=0) - one_hot) * one_hot, axis=1)
    target = jnp.where(slot_pos < capacity, chosen * capacity + slot_pos, slots_all)
    placing = (jnp.arange(slots_all, dtype=jnp.int32)[:, None] == target[None, :]).astype(BF16)
    either = placing[:, :tok_count] + placing[:, tok_count:]
    scaled = [
        (gates[:, k : k + 1].astype(F32) * cotangent.astype(F32)).astype(BF16) for k in range(2)
    ]

    def swap_blocks(rows):
        return lax.all_to_all(
            rows.astype(BF16).reshape(experts, capacity, rows.shape[1]), "expert", 0, 0, tiled=True
        ).reshape(slots_all, rows.shape[1])

    x = swap_blocks(dot(either, tokens))
    s = swap_blocks(dot(placing, jnp.concatenate(scaled, axis=0)))
    hidden0, slope0 = activate(dot(x, weight_in))
    d_hidden0 = dot(s, weight_out, (1, 1))
    d_pre0 = (d_hidden0 * slope0).astype(BF16)
    dgate = jnp.sum(hidden0.astype(F32) * d_hidden0, axis=1, keepdims=True)
    dx = dot(d_pre0, weight_in, (1, 1))
    back = swap_blocks(
        jnp.concatenate([dx, jnp.broadcast_to(dgate, (slots_all, LANES))], axis=1)
    )
    x_all = jnp.concatenate([x, *gather_groups(x)], axis=0)
    s_all = jnp.concatenate([s, *gather_groups(s)], axis=0)
    hidden1, slope1 = activate(dot(x_all[slots_all:], weight_in))
    d_pre1 = (dot(s_all[slots_all:], weight_out, (1, 1)) * slope1).astype(BF16)
    hidden = jnp.concatenate([hidden0, hidden1], axis=0)
    d_pre = jnp.concatenate([d_pre0, d_pre1], axis=0)
    x_cut = lax.dynamic_slice_in_dim(x_all, me * (feat_width // groups), feat_width // groups, 1)
    h_cut = lax.dynamic_slice_in_dim(hidden, me * (ffw // groups), ffw // groups, 1)
    grad_in = dot(x_cut, d_pre, (0, 0)).astype(BF16)
    grad_out = dot(h_cut, s_all, (0, 0)).astype(BF16)
    token_grads = dot(either, back[:, :feat_width], (0, 0)).astype(BF16)
    taken = dot(placing, back[:, feat_width : feat_width + 1], (0, 0))
    gate_grads = jnp.concatenate([taken[:tok_count], taken[tok_count:]], axis=1)
    gate_grads = (gate_grads / gates.astype(F32)).astype(BF16)
    return (token_grads, gate_grads, grad_in[None], grad_out[None])


def solution(mesh):
    rows = P(("dp", "expert"), None)
    weights = P("expert", None, None)

    def whole(tokens, *others):
        experts = mesh.shape["expert"]
        capacity = 2 * tokens.shape[0] // (mesh.shape["dp"] * experts) // experts
        tiles = capacity % 16 == 0 and experts & (experts - 1) == 0
        return jax.shard_map(
            local if tiles else local_small_blocks,
            mesh=mesh,
            in_specs=(rows, rows, rows, rows, weights, weights),
            out_specs=(rows, rows, P("expert", "dp", None), P("expert", "dp", None)),
            check_vma=False,
        )(tokens, *others)

    return whole
```

```python
import functools

import jax
import jax.numpy as jnp
from jax import lax
from jax.experimental import pallas as pl
from jax.experimental.pallas import tpu as pltpu
from jax.sharding import PartitionSpec as P

BF16 = jnp.bfloat16
F32 = jnp.float32
LANES = 128
MIB = 1 << 20


def dot(a, b, over=(1, 0)):
    return lax.dot_general(
        a, b, (((over[0],), (over[1],)), ((), ())), preferred_element_type=F32
    )


def activate(pre_act):
    cdf = 0.5 * (1.0 + lax.erf(pre_act * 0.7071067811865476))
    pdf = jnp.exp(-0.5 * pre_act * pre_act) * 0.3989422804014327
    return (pre_act * cdf).astype(BF16), cdf + pre_act * pdf


def call(kernel, out_shape, args, flops=0, limit=24, scratch=(), spaces=None):
    spaces = spaces or [pltpu.VMEM] * len(args)
    moved = sum(a.size * a.dtype.itemsize for a in args)
    args = [
        pltpu.with_memory_space_constraint(a, space) if space == pltpu.HBM else a
        for a, space in zip(args, spaces)
    ]
    return pl.pallas_call(
        kernel,
        out_shape=out_shape,
        in_specs=[pl.BlockSpec(memory_space=space) for space in spaces],
        out_specs=[
            pl.BlockSpec(memory_space=getattr(out, "memory_space", pltpu.VMEM))
            for out in out_shape
        ],
        scratch_shapes=list(scratch),
        compiler_params=pltpu.CompilerParams(vmem_limit_bytes=limit * MIB),
        cost_estimate=pl.CostEstimate(flops=flops, bytes_accessed=moved, transcendentals=0),
    )(*args)


def shape(dims, dtype=BF16):
    return jax.ShapeDtypeStruct(dims, dtype)


def route_kernel(experts, capacity, routes_hbm, gates_hbm, tokens_hbm, cotangent_hbm, *refs):
    blocks, place_refs, scratch = refs[:experts], refs[experts : experts + 2], refs[experts + 2 :]
    routes, gates, tokens, cotangent, sems = scratch
    copies = [
        pltpu.make_async_copy(source, target, sems.at[i])
        for i, (source, target) in enumerate(
            (
                (routes_hbm, routes),
                (gates_hbm, gates),
                (tokens_hbm, tokens),
                (cotangent_hbm, cotangent),
            )
        )
    ]
    for copy in copies:
        copy.start()
    tok_count, feat_width = tokens.shape
    slots_all = experts * capacity
    me = lax.axis_index("expert")
    rows = max(experts, 16)
    before = (
        lax.broadcasted_iota(jnp.int32, (tok_count, tok_count), 0)
        < lax.broadcasted_iota(jnp.int32, (tok_count, tok_count), 1)
    ).astype(F32).astype(BF16)
    expert_id = lax.broadcasted_iota(jnp.int32, (rows, tok_count), 0)
    slot_id = lax.broadcasted_iota(jnp.int32, (slots_all, tok_count), 0)
    taken = jnp.zeros((rows, 1), F32)
    places, gated = [], jnp.zeros((slots_all, tok_count), F32)
    copies[0].wait()
    copies[1].wait()
    for choice in range(2):
        chosen = routes[choice : choice + 1, :]
        one_hot = (expert_id == chosen).astype(F32)
        earlier = dot(one_hot.astype(BF16), before) + taken
        taken = taken + jnp.sum(one_hot, axis=1, keepdims=True)
        slot_pos = jnp.sum(earlier * one_hot, axis=0, keepdims=True).astype(jnp.int32)
        target = jnp.where(
            slot_pos < capacity, jnp.bitwise_xor(chosen, me) * capacity + slot_pos, slots_all
        )
        place = (slot_id == target).astype(F32)
        place_refs[choice][...] = place.astype(BF16)
        places.append(place)
        gated = gated + place * gates[choice : choice + 1, :].astype(F32)
    copies[2].wait()
    x = dot((places[0] + places[1]).astype(BF16), tokens[...]).astype(BF16)
    copies[3].wait()
    s = dot(gated.astype(BF16), cotangent[...]).astype(BF16)
    for k in range(experts):
        blocks[k][:, :feat_width] = x[k * capacity : (k + 1) * capacity]
        blocks[k][:, feat_width:] = s[k * capacity : (k + 1) * capacity]


def block_rows(me, k, capacity):
    return pl.ds(pl.multiple_of(jnp.bitwise_xor(me, k) * capacity, capacity), capacity)


def combine_kernel(experts, capacity, place0, place1, gates, back, token_grads, gate_grads, rows):
    tok_count, feat_width = token_grads.shape
    me = lax.axis_index("expert")
    for k in range(experts):
        rows[k * capacity : (k + 1) * capacity, :] = back[block_rows(me, k, capacity), :]
    either = (place0[...].astype(F32) + place1[...].astype(F32)).astype(BF16)
    token_grads[...] = dot(either, rows[:, :feat_width], (0, 0)).astype(BF16)
    dgate = rows[:, feat_width : feat_width + tok_count].astype(F32)
    taken = [
        jnp.sum(place[...].astype(F32) * dgate, axis=0, keepdims=True) for place in (place0, place1)
    ]
    gate_grads[...] = (jnp.concatenate(taken, axis=0) / gates[...].astype(F32)).astype(BF16)


def stack(refs, part, width):
    return jnp.concatenate([ref[:, part * width : (part + 1) * width] for ref in refs], axis=0)


def my_part(ref):
    width = ref.shape[1] // lax.axis_size("dp")
    return ref[:, pl.ds(pl.multiple_of(lax.axis_index("dp") * width, width), width)]


def fetcher(sems):
    count = iter(range(sems.shape[0]))

    def fetch(source, target):
        copy = pltpu.make_async_copy(source, target, sems.at[next(count)])
        copy.start()
        return copy

    return fetch


def own_kernel(tile, order, *refs):
    row_refs, refs = refs[:2], refs[2:]
    weight_in, weight_out, d_pre_hbm, h_cut_hbm, back_hbm, *scratch = refs
    hidden, d_pre, h_cut, back, sems = scratch
    me = lax.axis_index("expert")
    width, ffw = weight_in.shape
    tiles = [slice(at, at + tile) for at in range(0, ffw, tile)]
    fetch = fetcher(sems)
    x, s = stack(row_refs, 0, width), stack(row_refs, 1, width)
    slots_all = x.shape[0]
    capacity = slots_all // len(order)
    dgate = jnp.zeros((slots_all, LANES), F32)
    for cols in tiles:
        act, slope = activate(dot(x, weight_in[:, cols]))
        hidden[:, cols] = act
        d_hidden = dot(s, weight_out[cols, :], (1, 1))
        d_pre[:, cols] = (d_hidden * slope).astype(BF16)
        product = d_hidden * act.astype(F32)
        for lane in range(0, tile, LANES):
            dgate = dgate + product[:, lane : lane + LANES]
    h_cut[...] = my_part(hidden)
    dgate = jnp.broadcast_to(jnp.sum(dgate, axis=1, keepdims=True), (slots_all, LANES))
    places = [
        (slice(i * capacity, (i + 1) * capacity), block_rows(me, k, capacity))
        for i, k in enumerate(order)
    ]
    for rows, target in places:
        back[target, width:] = dgate[rows].astype(BF16)
    outs = [
        fetch(d_pre, d_pre_hbm),
        fetch(h_cut, h_cut_hbm),
        fetch(back.at[:, width:], back_hbm.at[:, width:]),
    ]
    wide = width // 4
    for at in range(0, width, wide):
        cols = slice(at, at + wide)
        dx = dot(d_pre[...], weight_in[cols, :], (1, 1)).astype(BF16)
        for rows, target in places:
            back[target, cols] = dx[rows]
        outs.append(fetch(back.at[:, cols], back_hbm.at[:, cols]))
    for copy in outs:
        copy.wait()


def early_kernel(tile, pieces, *refs):
    row_refs, refs = refs[:pieces], refs[pieces:]
    in_hbm, out_hbm, weight_in, weight_out, d_pre, h_cut, rows, hidden, sems = refs
    width, ffw = weight_in.shape
    piece = row_refs[0].shape[0]
    tiles = [slice(at, at + tile) for at in range(0, ffw, tile)]
    fetch = fetcher(sems)
    first = [fetch(ref, rows.at[pl.ds(i * piece, piece)]) for i, ref in enumerate(row_refs)]
    weights = [
        (
            fetch(in_hbm.at[:, cols], weight_in.at[:, cols]),
            fetch(out_hbm.at[cols, :], weight_out.at[cols, :]),
        )
        for cols in tiles
    ]
    for copy in first:
        copy.wait()
    x, s = rows[:, :width], rows[:, width:]
    for cols, (copy_in, copy_out) in zip(tiles, weights):
        copy_in.wait()
        copy_out.wait()
        act, slope = activate(dot(x, weight_in[:, cols]))
        hidden[:, cols] = act
        d_pre[:, cols] = (dot(s, weight_out[cols, :], (1, 1)) * slope).astype(BF16)
    h_cut[...] = my_part(hidden)


def grads_kernel(tile, pieces, late, *refs):
    row_refs, refs = refs[:pieces], refs[pieces:]
    d_pre_refs, h_cut_refs, refs = refs[:2], refs[2:4], refs[4:]
    weight_in, weight_out, grad_in_hbm, grad_out_hbm, *scratch = refs
    rows, hidden, h_cut, d_pre, grad_in, grad_out, sems, out_sems = scratch
    width, ffw = weight_in.shape
    tiles = [slice(at, at + tile) for at in range(0, ffw, tile)]
    piece = row_refs[0].shape[0]
    known = (pieces - late) * piece
    fetch, send = fetcher(sems), fetcher(out_sems)
    copies = [
        fetch(row_refs[i], rows.at[pl.ds(i * piece, piece)])
        for i in [*range(pieces - late, pieces), *range(pieces - late)]
    ]
    at = 0
    for source, cut_source in zip(d_pre_refs, h_cut_refs):
        span = pl.ds(at, source.shape[0])
        copies += [fetch(source, d_pre.at[span]), fetch(cut_source, h_cut.at[span])]
        at += source.shape[0]
    x, s = stack(row_refs[-late:], 0, width), stack(row_refs[-late:], 1, width)
    for cols in tiles:
        act, slope = activate(dot(x, weight_in[:, cols]))
        hidden[:, cols] = act
        d_pre[known:, cols] = (dot(s, weight_out[cols, :], (1, 1)) * slope).astype(BF16)
    for copy in copies:
        copy.wait()
    cut = grad_in.shape[0]
    mine = pl.ds(pl.multiple_of(lax.axis_index("dp") * cut, cut), cut)
    outs = []
    for at in range(0, ffw, ffw // 2):
        cols = slice(at, at + ffw // 2)
        grad_in[:, cols] = dot(rows[:, mine], d_pre[:, cols], (0, 0)).astype(BF16)
        outs.append(send(grad_in.at[:, cols], grad_in_hbm.at[:, cols]))
    h_cut[known:, :] = my_part(hidden)
    for at in range(0, tile, tile // 2):
        part = slice(at, at + tile // 2)
        grad_out[part, :] = dot(h_cut[:, part], rows[:, width:], (0, 0)).astype(BF16)
        outs.append(send(grad_out.at[part, :], grad_out_hbm.at[part, :]))
    for copy in outs:
        copy.wait()


def after(value, *first):
    return lax.optimization_barrier((value, *first))[0]


def permute(block, k):
    return lax.ppermute(block, "expert", [(i, i ^ k) for i in range(lax.axis_size("expert"))])


def swap_cores(rows):
    return lax.ppermute(rows, "dp", [(i, i ^ 1) for i in range(lax.axis_size("dp"))])


def shift_chips(rows, k):
    groups = lax.axis_size("dp")
    return lax.ppermute(rows, "dp", [(i, (i + 2 * k) % groups) for i in range(groups)])


def gather_groups(rows):
    others = [swap_cores(rows)]
    for k in range(1, lax.axis_size("dp") // 2):
        other = shift_chips(rows, k)
        others += [other, swap_cores(other)]
    return others


def local(tokens, cotangent, routes, gates, proj_in, proj_out):
    tok_count, feat_width = tokens.shape
    experts = lax.axis_size("expert")
    groups = lax.axis_size("dp")
    capacity = 2 * tok_count // experts
    slots_all = experts * capacity
    half = experts // 2
    ffw = proj_in.shape[2]
    tile = ffw // groups
    product = 2 * slots_all * feat_width * ffw
    place = shape((slots_all, tok_count))

    routed = call(
        functools.partial(route_kernel, experts, capacity),
        [shape((capacity, 2 * feat_width))] * experts + [place] * 2,
        [routes.T, gates.T, tokens, cotangent],
        30 * product,
        spaces=[pltpu.HBM] * 4,
        scratch=[
            pltpu.VMEM((2, tok_count), jnp.int32),
            pltpu.VMEM((2, tok_count), BF16),
            pltpu.VMEM((tok_count, feat_width), BF16),
            pltpu.VMEM((tok_count, feat_width), BF16),
            pltpu.SemaphoreType.DMA((4,)),
        ],
    )
    blocks, places = routed[:experts], routed[experts:]
    rest = list(range(experts - 1, 1, -1))
    order = [0, *rest[:2], 1, *rest[2:]]
    order_a, order_b = order[:half], order[half:]
    got_a = [blocks[0]] + [permute(blocks[k], k) for k in order_a[1:]]
    got_b = [
        permute(blocks[k] if i < 2 else after(blocks[k], got_a[-1]), k)
        for i, k in enumerate(order_b)
    ]
    rows_a = jnp.concatenate(got_a, axis=0)
    chips_a = [shift_chips(rows_a, k) for k in range(1, groups // 2)]
    core_a = swap_cores(after(rows_a, got_b[0]))
    rows_b = jnp.concatenate(got_b, axis=0)
    chips_b = [shift_chips(rows_b, k) for k in range(1, groups // 2)]
    core_b = swap_cores(rows_b)
    weights = [proj_in[0], proj_out[0]]
    weight_space = [pltpu.VMEM((feat_width, ffw), BF16), pltpu.VMEM((ffw, feat_width), BF16)]
    d_pre, h_cut, back = call(
        functools.partial(own_kernel, tile, order),
        [
            pltpu.HBM((slots_all, ffw), BF16),
            pltpu.HBM((slots_all, tile), BF16),
            pltpu.HBM((slots_all, feat_width + LANES), BF16),
        ],
        [
            rows_a,
            rows_b,
            *[pltpu.with_memory_space_constraint(w, pltpu.VMEM) for w in weights],
        ],
        20 * product,
        scratch=[
            pltpu.VMEM((slots_all, ffw), BF16),
            pltpu.VMEM((slots_all, ffw), BF16),
            pltpu.VMEM((slots_all, tile), BF16),
            pltpu.VMEM((slots_all, feat_width + LANES), BF16),
            pltpu.SemaphoreType.DMA((7,)),
        ],
    )
    back = lax.all_to_all(
        after(back, core_a, core_b).reshape(experts, capacity, feat_width + LANES),
        "expert",
        0,
        0,
        tiled=True,
    ).reshape(slots_all, feat_width + LANES)
    relayed_a = [swap_cores(after(rows, d_pre)) for rows in chips_a]
    relayed_b = [swap_cores(rows) for rows in chips_b]
    early = [core_a, core_b, *chips_a]
    late = [*relayed_a, *chips_b, *relayed_b]
    early_rows = sum(piece.shape[0] for piece in early)
    late_rows = sum(piece.shape[0] for piece in late)
    weight_in, weight_out, d_pre_early, h_cut_early = call(
        functools.partial(early_kernel, tile, len(early)),
        [*weight_space, shape((early_rows, ffw)), shape((early_rows, tile))],
        [*early, *weights],
        2 * product,
        scratch=[
            pltpu.VMEM((early_rows, 2 * feat_width), BF16),
            pltpu.VMEM((early_rows, ffw), BF16),
            pltpu.SemaphoreType.DMA((len(early) + 2 * groups,)),
        ],
        spaces=[pl.ANY] * len(early) + [pltpu.HBM] * 2,
    )
    pieces = [rows_a, rows_b, *early, *late]
    rows_all = groups * slots_all
    grad_in, grad_out = call(
        functools.partial(grads_kernel, tile, len(pieces), len(late)),
        [
            pltpu.HBM((feat_width // groups, ffw), BF16),
            pltpu.HBM((ffw // groups, feat_width), BF16),
        ],
        [
            *pieces,
            *[d_pre, d_pre_early, h_cut, h_cut_early],
            *[
                pltpu.with_memory_space_constraint(w, pltpu.VMEM)
                for w in (weight_in, weight_out)
            ],
        ],
        4 * product,
        limit=32,
        scratch=[
            pltpu.VMEM((rows_all, 2 * feat_width), BF16),
            pltpu.VMEM((late_rows, ffw), BF16),
            pltpu.VMEM((rows_all, tile), BF16),
            pltpu.VMEM((rows_all, ffw), BF16),
            pltpu.VMEM((feat_width // groups, ffw), BF16),
            pltpu.VMEM((ffw // groups, feat_width), BF16),
            pltpu.SemaphoreType.DMA((len(pieces) + 4,)),
            pltpu.SemaphoreType.DMA((4,)),
        ],
        spaces=[pl.ANY] * (len(pieces) - len(late))
        + [pltpu.VMEM] * len(late)
        + [pltpu.HBM, pl.ANY] * 2
        + [pltpu.VMEM] * 2,
    )
    token_grads, gate_grads = call(
        functools.partial(combine_kernel, experts, capacity),
        [shape((tok_count, feat_width)), shape((2, tok_count))],
        [*places, gates.T, after(back, grad_in)],
        scratch=[pltpu.VMEM((slots_all, feat_width + LANES), BF16)],
    )
    return (token_grads, gate_grads.T, grad_in[None], grad_out[None])


def local_small_blocks(tokens, cotangent, routes, gates, proj_in, proj_out):
    tok_count, feat_width = tokens.shape
    experts = lax.axis_size("expert")
    groups = lax.axis_size("dp")
    me = lax.axis_index("dp")
    capacity = 2 * tok_count // experts
    slots_all = experts * capacity
    weight_in, weight_out = proj_in[0], proj_out[0]
    ffw = weight_in.shape[1]
    chosen = jnp.concatenate([routes[:, 0], routes[:, 1]])
    one_hot = (chosen[:, None] == jnp.arange(experts, dtype=jnp.int32)[None, :]).astype(jnp.int32)
    slot_pos = jnp.sum((jnp.cumsum(one_hot, axis=0) - one_hot) * one_hot, axis=1)
    target = jnp.where(slot_pos < capacity, chosen * capacity + slot_pos, slots_all)
    placing = (jnp.arange(slots_all, dtype=jnp.int32)[:, None] == target[None, :]).astype(BF16)
    either = placing[:, :tok_count] + placing[:, tok_count:]
    scaled = [
        (gates[:, k : k + 1].astype(F32) * cotangent.astype(F32)).astype(BF16) for k in range(2)
    ]

    def swap_blocks(rows):
        return lax.all_to_all(
            rows.astype(BF16).reshape(experts, capacity, rows.shape[1]), "expert", 0, 0, tiled=True
        ).reshape(slots_all, rows.shape[1])

    x = swap_blocks(dot(either, tokens))
    s = swap_blocks(dot(placing, jnp.concatenate(scaled, axis=0)))
    hidden0, slope0 = activate(dot(x, weight_in))
    d_hidden0 = dot(s, weight_out, (1, 1))
    d_pre0 = (d_hidden0 * slope0).astype(BF16)
    dgate = jnp.sum(hidden0.astype(F32) * d_hidden0, axis=1, keepdims=True)
    dx = dot(d_pre0, weight_in, (1, 1))
    back = swap_blocks(
        jnp.concatenate([dx, jnp.broadcast_to(dgate, (slots_all, LANES))], axis=1)
    )
    x_all = jnp.concatenate([x, *gather_groups(x)], axis=0)
    s_all = jnp.concatenate([s, *gather_groups(s)], axis=0)
    hidden1, slope1 = activate(dot(x_all[slots_all:], weight_in))
    d_pre1 = (dot(s_all[slots_all:], weight_out, (1, 1)) * slope1).astype(BF16)
    hidden = jnp.concatenate([hidden0, hidden1], axis=0)
    d_pre = jnp.concatenate([d_pre0, d_pre1], axis=0)
    x_cut = lax.dynamic_slice_in_dim(x_all, me * (feat_width // groups), feat_width // groups, 1)
    h_cut = lax.dynamic_slice_in_dim(hidden, me * (ffw // groups), ffw // groups, 1)
    grad_in = dot(x_cut, d_pre, (0, 0)).astype(BF16)
    grad_out = dot(h_cut, s_all, (0, 0)).astype(BF16)
    token_grads = dot(either, back[:, :feat_width], (0, 0)).astype(BF16)
    taken = dot(placing, back[:, feat_width : feat_width + 1], (0, 0))
    gate_grads = jnp.concatenate([taken[:tok_count], taken[tok_count:]], axis=1)
    gate_grads = (gate_grads / gates.astype(F32)).astype(BF16)
    return (token_grads, gate_grads, grad_in[None], grad_out[None])


def solution(mesh):
    rows = P(("dp", "expert"), None)
    weights = P("expert", None, None)

    def whole(tokens, *others):
        experts = mesh.shape["expert"]
        capacity = 2 * tokens.shape[0] // (mesh.shape["dp"] * experts) // experts
        tiles = capacity % 16 == 0 and experts & (experts - 1) == 0
        return jax.shard_map(
            local if tiles else local_small_blocks,
            mesh=mesh,
            in_specs=(rows, rows, rows, rows, weights, weights),
            out_specs=(rows, rows, P("expert", "dp", None), P("expert", "dp", None)),
            check_vma=False,
        )(tokens, *others)

    return whole
```

```python
import functools

import jax
import jax.numpy as jnp
from jax import lax
from jax.experimental import pallas as pl
from jax.experimental.pallas import tpu as pltpu
from jax.sharding import PartitionSpec as P

BF16 = jnp.bfloat16
F32 = jnp.float32
LANES = 128
MIB = 1 << 20


def dot(a, b, over=(1, 0)):
    return lax.dot_general(
        a, b, (((over[0],), (over[1],)), ((), ())), preferred_element_type=F32
    )


def activate(pre_act):
    cdf = 0.5 * (1.0 + lax.erf(pre_act * 0.7071067811865476))
    pdf = jnp.exp(-0.5 * pre_act * pre_act) * 0.3989422804014327
    return (pre_act * cdf).astype(BF16), cdf + pre_act * pdf


def call(kernel, out_shape, args, flops=0, limit=24, scratch=(), spaces=None):
    spaces = spaces or [pltpu.VMEM] * len(args)
    moved = sum(a.size * a.dtype.itemsize for a in args)
    args = [
        pltpu.with_memory_space_constraint(a, space) if space == pltpu.HBM else a
        for a, space in zip(args, spaces)
    ]
    return pl.pallas_call(
        kernel,
        out_shape=out_shape,
        in_specs=[pl.BlockSpec(memory_space=space) for space in spaces],
        out_specs=[
            pl.BlockSpec(memory_space=getattr(out, "memory_space", pltpu.VMEM))
            for out in out_shape
        ],
        scratch_shapes=list(scratch),
        compiler_params=pltpu.CompilerParams(vmem_limit_bytes=limit * MIB),
        cost_estimate=pl.CostEstimate(flops=flops, bytes_accessed=moved, transcendentals=0),
    )(*args)


def shape(dims, dtype=BF16):
    return jax.ShapeDtypeStruct(dims, dtype)


def route_kernel(experts, capacity, routes_hbm, gates_hbm, tokens_hbm, cotangent_hbm, *refs):
    blocks, place_refs, scratch = refs[:experts], refs[experts : experts + 2], refs[experts + 2 :]
    routes, gates, tokens, cotangent, sems = scratch
    copies = [
        pltpu.make_async_copy(source, target, sems.at[i])
        for i, (source, target) in enumerate(
            (
                (routes_hbm, routes),
                (gates_hbm, gates),
                (tokens_hbm, tokens),
                (cotangent_hbm, cotangent),
            )
        )
    ]
    for copy in copies:
        copy.start()
    tok_count, feat_width = tokens.shape
    slots_all = experts * capacity
    me = lax.axis_index("expert")
    rows = max(experts, 16)
    before = (
        lax.broadcasted_iota(jnp.int32, (tok_count, tok_count), 0)
        < lax.broadcasted_iota(jnp.int32, (tok_count, tok_count), 1)
    ).astype(F32).astype(BF16)
    expert_id = lax.broadcasted_iota(jnp.int32, (rows, tok_count), 0)
    slot_id = lax.broadcasted_iota(jnp.int32, (slots_all, tok_count), 0)
    taken = jnp.zeros((rows, 1), F32)
    places, gated = [], jnp.zeros((slots_all, tok_count), F32)
    copies[0].wait()
    copies[1].wait()
    for choice in range(2):
        chosen = routes[choice : choice + 1, :]
        one_hot = (expert_id == chosen).astype(F32)
        earlier = dot(one_hot.astype(BF16), before) + taken
        taken = taken + jnp.sum(one_hot, axis=1, keepdims=True)
        slot_pos = jnp.sum(earlier * one_hot, axis=0, keepdims=True).astype(jnp.int32)
        target = jnp.where(
            slot_pos < capacity, jnp.bitwise_xor(chosen, me) * capacity + slot_pos, slots_all
        )
        place = (slot_id == target).astype(F32)
        place_refs[choice][...] = place.astype(BF16)
        places.append(place)
        gated = gated + place * gates[choice : choice + 1, :].astype(F32)
    copies[2].wait()
    x = dot((places[0] + places[1]).astype(BF16), tokens[...]).astype(BF16)
    copies[3].wait()
    s = dot(gated.astype(BF16), cotangent[...]).astype(BF16)
    for k in range(experts):
        blocks[k][:, :feat_width] = x[k * capacity : (k + 1) * capacity]
        blocks[k][:, feat_width:] = s[k * capacity : (k + 1) * capacity]


def block_rows(me, k, capacity):
    return pl.ds(pl.multiple_of(jnp.bitwise_xor(me, k) * capacity, capacity), capacity)


def combine_kernel(experts, capacity, place0, place1, gates, back, token_grads, gate_grads, rows):
    tok_count, feat_width = token_grads.shape
    me = lax.axis_index("expert")
    for k in range(experts):
        rows[k * capacity : (k + 1) * capacity, :] = back[block_rows(me, k, capacity), :]
    either = (place0[...].astype(F32) + place1[...].astype(F32)).astype(BF16)
    token_grads[...] = dot(either, rows[:, :feat_width], (0, 0)).astype(BF16)
    dgate = rows[:, feat_width : feat_width + tok_count].astype(F32)
    taken = [
        jnp.sum(place[...].astype(F32) * dgate, axis=0, keepdims=True) for place in (place0, place1)
    ]
    gate_grads[...] = (jnp.concatenate(taken, axis=0) / gates[...].astype(F32)).astype(BF16)


def stack(refs, part, width):
    return jnp.concatenate([ref[:, part * width : (part + 1) * width] for ref in refs], axis=0)


def my_part(ref):
    width = ref.shape[1] // lax.axis_size("dp")
    return ref[:, pl.ds(pl.multiple_of(lax.axis_index("dp") * width, width), width)]


def fetcher(sems):
    count = iter(range(sems.shape[0]))

    def fetch(source, target):
        copy = pltpu.make_async_copy(source, target, sems.at[next(count)])
        copy.start()
        return copy

    return fetch


def own_kernel(tile, order, *refs):
    row_refs, refs = refs[:2], refs[2:]
    weight_in, weight_out, d_pre_hbm, h_cut_hbm, back_hbm, kept, *scratch = refs
    hidden, d_pre, h_cut, back, sems = scratch
    me = lax.axis_index("expert")
    width, ffw = weight_in.shape
    tiles = [slice(at, at + tile) for at in range(0, ffw, tile)]
    fetch = fetcher(sems)
    keep = fetch(weight_in.at[:, tiles[0]], kept)
    x, s = stack(row_refs, 0, width), stack(row_refs, 1, width)
    slots_all = x.shape[0]
    capacity = slots_all // len(order)
    dgate = jnp.zeros((slots_all, LANES), F32)
    for cols in tiles:
        act, slope = activate(dot(x, weight_in[:, cols]))
        hidden[:, cols] = act
        d_hidden = dot(s, weight_out[cols, :], (1, 1))
        d_pre[:, cols] = (d_hidden * slope).astype(BF16)
        product = d_hidden * act.astype(F32)
        for lane in range(0, tile, LANES):
            dgate = dgate + product[:, lane : lane + LANES]
    h_cut[...] = my_part(hidden)
    dgate = jnp.broadcast_to(jnp.sum(dgate, axis=1, keepdims=True), (slots_all, LANES))
    places = [
        (slice(i * capacity, (i + 1) * capacity), block_rows(me, k, capacity))
        for i, k in enumerate(order)
    ]
    for rows, target in places:
        back[target, width:] = dgate[rows].astype(BF16)
    outs = [
        keep,
        fetch(d_pre, d_pre_hbm),
        fetch(h_cut, h_cut_hbm),
        fetch(back.at[:, width:], back_hbm.at[:, width:]),
    ]
    wide = width // 4
    for at in range(0, width, wide):
        cols = slice(at, at + wide)
        dx = dot(d_pre[...], weight_in[cols, :], (1, 1)).astype(BF16)
        for rows, target in places:
            back[target, cols] = dx[rows]
        outs.append(fetch(back.at[:, cols], back_hbm.at[:, cols]))
    for copy in outs:
        copy.wait()


def early_kernel(tile, pieces, *refs):
    row_refs, refs = refs[:pieces], refs[pieces:]
    kept, in_hbm, out_hbm, weight_in, weight_out, d_pre, h_cut, hidden, sems = refs
    width, ffw = weight_in.shape
    tiles = [slice(at, at + tile) for at in range(0, ffw, tile)]
    fetch = fetcher(sems)
    copies_out = [fetch(out_hbm.at[tiles[0], :], weight_out.at[tiles[0], :])]
    copies_in = []
    for cols in tiles[1:]:
        copies_in.append(fetch(in_hbm.at[:, cols], weight_in.at[:, cols]))
        copies_out.append(fetch(out_hbm.at[cols, :], weight_out.at[cols, :]))
    whole = fetch(kept, weight_in.at[:, tiles[0]])
    x, s = stack(row_refs, 0, width), stack(row_refs, 1, width)
    for t, cols in enumerate(tiles):
        if t:
            copies_in[t - 1].wait()
        act, slope = activate(dot(x, weight_in[:, cols] if t else kept[...]))
        hidden[:, cols] = act
        copies_out[t].wait()
        d_pre[:, cols] = (dot(s, weight_out[cols, :], (1, 1)) * slope).astype(BF16)
    h_cut[...] = my_part(hidden)
    whole.wait()


def grads_kernel(tile, pieces, late, *refs):
    row_refs, refs = refs[:pieces], refs[pieces:]
    d_pre_refs, h_cut_refs, refs = refs[:2], refs[2:4], refs[4:]
    weight_in, weight_out, grad_in_hbm, grad_out_hbm, *scratch = refs
    rows, hidden, h_cut, d_pre, grad_in, grad_out, sems, out_sems = scratch
    width, ffw = weight_in.shape
    tiles = [slice(at, at + tile) for at in range(0, ffw, tile)]
    piece = row_refs[0].shape[0]
    known = (pieces - late) * piece
    fetch, send = fetcher(sems), fetcher(out_sems)
    copies = [
        fetch(row_refs[i], rows.at[pl.ds(i * piece, piece)])
        for i in [*range(pieces - late, pieces), *range(pieces - late)]
    ]
    at = 0
    for source, cut_source in zip(d_pre_refs, h_cut_refs):
        span = pl.ds(at, source.shape[0])
        copies += [fetch(source, d_pre.at[span]), fetch(cut_source, h_cut.at[span])]
        at += source.shape[0]
    x, s = stack(row_refs[-late:], 0, width), stack(row_refs[-late:], 1, width)
    for cols in tiles:
        act, slope = activate(dot(x, weight_in[:, cols]))
        hidden[:, cols] = act
        d_pre[known:, cols] = (dot(s, weight_out[cols, :], (1, 1)) * slope).astype(BF16)
    for copy in copies:
        copy.wait()
    cut = grad_in.shape[0]
    mine = pl.ds(pl.multiple_of(lax.axis_index("dp") * cut, cut), cut)
    outs = []
    for at in range(0, ffw, ffw // 2):
        cols = slice(at, at + ffw // 2)
        grad_in[:, cols] = dot(rows[:, mine], d_pre[:, cols], (0, 0)).astype(BF16)
        outs.append(send(grad_in.at[:, cols], grad_in_hbm.at[:, cols]))
    h_cut[known:, :] = my_part(hidden)
    for at in range(0, tile, tile // 2):
        part = slice(at, at + tile // 2)
        grad_out[part, :] = dot(h_cut[:, part], rows[:, width:], (0, 0)).astype(BF16)
        outs.append(send(grad_out.at[part, :], grad_out_hbm.at[part, :]))
    for copy in outs:
        copy.wait()


def after(value, *first):
    return lax.optimization_barrier((value, *first))[0]


def permute(block, k):
    return lax.ppermute(block, "expert", [(i, i ^ k) for i in range(lax.axis_size("expert"))])


def swap_cores(rows):
    return lax.ppermute(rows, "dp", [(i, i ^ 1) for i in range(lax.axis_size("dp"))])


def shift_chips(rows, k):
    groups = lax.axis_size("dp")
    return lax.ppermute(rows, "dp", [(i, (i + 2 * k) % groups) for i in range(groups)])


def gather_groups(rows):
    others = [swap_cores(rows)]
    for k in range(1, lax.axis_size("dp") // 2):
        other = shift_chips(rows, k)
        others += [other, swap_cores(other)]
    return others


def local(tokens, cotangent, routes, gates, proj_in, proj_out):
    tok_count, feat_width = tokens.shape
    experts = lax.axis_size("expert")
    groups = lax.axis_size("dp")
    capacity = 2 * tok_count // experts
    slots_all = experts * capacity
    half = experts // 2
    ffw = proj_in.shape[2]
    tile = ffw // groups
    product = 2 * slots_all * feat_width * ffw
    place = shape((slots_all, tok_count))

    routed = call(
        functools.partial(route_kernel, experts, capacity),
        [shape((capacity, 2 * feat_width))] * experts + [place] * 2,
        [routes.T, gates.T, tokens, cotangent],
        30 * product,
        spaces=[pltpu.HBM] * 4,
        scratch=[
            pltpu.VMEM((2, tok_count), jnp.int32),
            pltpu.VMEM((2, tok_count), BF16),
            pltpu.VMEM((tok_count, feat_width), BF16),
            pltpu.VMEM((tok_count, feat_width), BF16),
            pltpu.SemaphoreType.DMA((4,)),
        ],
    )
    blocks, places = routed[:experts], routed[experts:]
    rest = list(range(experts - 1, 1, -1))
    order = [0, *rest[:2], 1, *rest[2:]]
    order_a, order_b = order[:half], order[half:]
    got_a = [blocks[0]] + [permute(blocks[k], k) for k in order_a[1:]]
    got_b = [
        permute(blocks[k] if i < 2 else after(blocks[k], got_a[-1]), k)
        for i, k in enumerate(order_b)
    ]
    rows_a = jnp.concatenate(got_a, axis=0)
    chips_a = [shift_chips(rows_a, k) for k in range(1, groups // 2)]
    core_a = swap_cores(after(rows_a, got_b[0]))
    rows_b = jnp.concatenate(got_b, axis=0)
    chips_b = [shift_chips(rows_b, k) for k in range(1, groups // 2)]
    core_b = swap_cores(rows_b)
    weights = [proj_in[0], proj_out[0]]
    weight_space = [pltpu.VMEM((feat_width, ffw), BF16), pltpu.VMEM((ffw, feat_width), BF16)]
    d_pre, h_cut, back, kept = call(
        functools.partial(own_kernel, tile, order),
        [
            pltpu.HBM((slots_all, ffw), BF16),
            pltpu.HBM((slots_all, tile), BF16),
            pltpu.HBM((slots_all, feat_width + LANES), BF16),
            pltpu.VMEM((feat_width, tile), BF16),
        ],
        [
            rows_a,
            rows_b,
            *[pltpu.with_memory_space_constraint(w, pltpu.VMEM) for w in weights],
        ],
        20 * product,
        scratch=[
            pltpu.VMEM((slots_all, ffw), BF16),
            pltpu.VMEM((slots_all, ffw), BF16),
            pltpu.VMEM((slots_all, tile), BF16),
            pltpu.VMEM((slots_all, feat_width + LANES), BF16),
            pltpu.SemaphoreType.DMA((8,)),
        ],
    )
    back = lax.all_to_all(
        after(back, core_a, core_b).reshape(experts, capacity, feat_width + LANES),
        "expert",
        0,
        0,
        tiled=True,
    ).reshape(slots_all, feat_width + LANES)
    relayed_a = [swap_cores(after(rows, d_pre)) for rows in chips_a]
    relayed_b = [swap_cores(rows) for rows in chips_b]
    early = [core_a, core_b, *chips_a]
    late = [*relayed_a, *chips_b, *relayed_b]
    early_rows = sum(piece.shape[0] for piece in early)
    late_rows = sum(piece.shape[0] for piece in late)
    weight_in, weight_out, d_pre_early, h_cut_early = call(
        functools.partial(early_kernel, tile, len(early)),
        [*weight_space, shape((early_rows, ffw)), shape((early_rows, tile))],
        [*early, pltpu.with_memory_space_constraint(kept, pltpu.VMEM), *weights],
        2 * product,
        scratch=[
            pltpu.VMEM((early_rows, ffw), BF16),
            pltpu.SemaphoreType.DMA((2 * groups,)),
        ],
        spaces=[pltpu.VMEM] * (len(early) + 1) + [pltpu.HBM] * 2,
    )
    pieces = [rows_a, rows_b, *early, *late]
    rows_all = groups * slots_all
    grad_in, grad_out = call(
        functools.partial(grads_kernel, tile, len(pieces), len(late)),
        [
            pltpu.HBM((feat_width // groups, ffw), BF16),
            pltpu.HBM((ffw // groups, feat_width), BF16),
        ],
        [
            *pieces,
            *[d_pre, d_pre_early, h_cut, h_cut_early],
            *[
                pltpu.with_memory_space_constraint(w, pltpu.VMEM)
                for w in (weight_in, weight_out)
            ],
        ],
        4 * product,
        limit=32,
        scratch=[
            pltpu.VMEM((rows_all, 2 * feat_width), BF16),
            pltpu.VMEM((late_rows, ffw), BF16),
            pltpu.VMEM((rows_all, tile), BF16),
            pltpu.VMEM((rows_all, ffw), BF16),
            pltpu.VMEM((feat_width // groups, ffw), BF16),
            pltpu.VMEM((ffw // groups, feat_width), BF16),
            pltpu.SemaphoreType.DMA((len(pieces) + 4,)),
            pltpu.SemaphoreType.DMA((4,)),
        ],
        spaces=[pl.ANY] * (len(pieces) - len(late))
        + [pltpu.VMEM] * len(late)
        + [pltpu.HBM, pl.ANY] * 2
        + [pltpu.VMEM] * 2,
    )
    token_grads, gate_grads = call(
        functools.partial(combine_kernel, experts, capacity),
        [shape((tok_count, feat_width)), shape((2, tok_count))],
        [*places, gates.T, after(back, grad_in)],
        scratch=[pltpu.VMEM((slots_all, feat_width + LANES), BF16)],
    )
    return (token_grads, gate_grads.T, grad_in[None], grad_out[None])


def local_small_blocks(tokens, cotangent, routes, gates, proj_in, proj_out):
    tok_count, feat_width = tokens.shape
    experts = lax.axis_size("expert")
    groups = lax.axis_size("dp")
    me = lax.axis_index("dp")
    capacity = 2 * tok_count // experts
    slots_all = experts * capacity
    weight_in, weight_out = proj_in[0], proj_out[0]
    ffw = weight_in.shape[1]
    chosen = jnp.concatenate([routes[:, 0], routes[:, 1]])
    one_hot = (chosen[:, None] == jnp.arange(experts, dtype=jnp.int32)[None, :]).astype(jnp.int32)
    slot_pos = jnp.sum((jnp.cumsum(one_hot, axis=0) - one_hot) * one_hot, axis=1)
    target = jnp.where(slot_pos < capacity, chosen * capacity + slot_pos, slots_all)
    placing = (jnp.arange(slots_all, dtype=jnp.int32)[:, None] == target[None, :]).astype(BF16)
    either = placing[:, :tok_count] + placing[:, tok_count:]
    scaled = [
        (gates[:, k : k + 1].astype(F32) * cotangent.astype(F32)).astype(BF16) for k in range(2)
    ]

    def swap_blocks(rows):
        return lax.all_to_all(
            rows.astype(BF16).reshape(experts, capacity, rows.shape[1]), "expert", 0, 0, tiled=True
        ).reshape(slots_all, rows.shape[1])

    x = swap_blocks(dot(either, tokens))
    s = swap_blocks(dot(placing, jnp.concatenate(scaled, axis=0)))
    hidden0, slope0 = activate(dot(x, weight_in))
    d_hidden0 = dot(s, weight_out, (1, 1))
    d_pre0 = (d_hidden0 * slope0).astype(BF16)
    dgate = jnp.sum(hidden0.astype(F32) * d_hidden0, axis=1, keepdims=True)
    dx = dot(d_pre0, weight_in, (1, 1))
    back = swap_blocks(
        jnp.concatenate([dx, jnp.broadcast_to(dgate, (slots_all, LANES))], axis=1)
    )
    x_all = jnp.concatenate([x, *gather_groups(x)], axis=0)
    s_all = jnp.concatenate([s, *gather_groups(s)], axis=0)
    hidden1, slope1 = activate(dot(x_all[slots_all:], weight_in))
    d_pre1 = (dot(s_all[slots_all:], weight_out, (1, 1)) * slope1).astype(BF16)
    hidden = jnp.concatenate([hidden0, hidden1], axis=0)
    d_pre = jnp.concatenate([d_pre0, d_pre1], axis=0)
    x_cut = lax.dynamic_slice_in_dim(x_all, me * (feat_width // groups), feat_width // groups, 1)
    h_cut = lax.dynamic_slice_in_dim(hidden, me * (ffw // groups), ffw // groups, 1)
    grad_in = dot(x_cut, d_pre, (0, 0)).astype(BF16)
    grad_out = dot(h_cut, s_all, (0, 0)).astype(BF16)
    token_grads = dot(either, back[:, :feat_width], (0, 0)).astype(BF16)
    taken = dot(placing, back[:, feat_width : feat_width + 1], (0, 0))
    gate_grads = jnp.concatenate([taken[:tok_count], taken[tok_count:]], axis=1)
    gate_grads = (gate_grads / gates.astype(F32)).astype(BF16)
    return (token_grads, gate_grads, grad_in[None], grad_out[None])


def solution(mesh):
    rows = P(("dp", "expert"), None)
    weights = P("expert", None, None)

    def whole(tokens, *others):
        experts = mesh.shape["expert"]
        capacity = 2 * tokens.shape[0] // (mesh.shape["dp"] * experts) // experts
        tiles = capacity % 16 == 0 and experts & (experts - 1) == 0
        return jax.shard_map(
            local if tiles else local_small_blocks,
            mesh=mesh,
            in_specs=(rows, rows, rows, rows, weights, weights),
            out_specs=(rows, rows, P("expert", "dp", None), P("expert", "dp", None)),
            check_vma=False,
        )(tokens, *others)

    return whole
```

```python
import functools

import jax
import jax.numpy as jnp
from jax import lax
from jax.experimental import pallas as pl
from jax.experimental.pallas import tpu as pltpu
from jax.sharding import PartitionSpec as P

BF16 = jnp.bfloat16
F32 = jnp.float32
LANES = 128
MIB = 1 << 20


def dot(a, b, over=(1, 0)):
    return lax.dot_general(
        a, b, (((over[0],), (over[1],)), ((), ())), preferred_element_type=F32
    )


def activate(pre_act):
    cdf = 0.5 * (1.0 + lax.erf(pre_act * 0.7071067811865476))
    pdf = jnp.exp(-0.5 * pre_act * pre_act) * 0.3989422804014327
    return (pre_act * cdf).astype(BF16), cdf + pre_act * pdf


def call(kernel, out_shape, args, flops=0, limit=24, scratch=(), spaces=None):
    spaces = spaces or [pltpu.VMEM] * len(args)
    moved = sum(a.size * a.dtype.itemsize for a in args)
    args = [
        pltpu.with_memory_space_constraint(a, space) if space == pltpu.HBM else a
        for a, space in zip(args, spaces)
    ]
    return pl.pallas_call(
        kernel,
        out_shape=out_shape,
        in_specs=[pl.BlockSpec(memory_space=space) for space in spaces],
        out_specs=[
            pl.BlockSpec(memory_space=getattr(out, "memory_space", pltpu.VMEM))
            for out in out_shape
        ],
        scratch_shapes=list(scratch),
        compiler_params=pltpu.CompilerParams(vmem_limit_bytes=limit * MIB),
        cost_estimate=pl.CostEstimate(flops=flops, bytes_accessed=moved, transcendentals=0),
    )(*args)


def shape(dims, dtype=BF16):
    return jax.ShapeDtypeStruct(dims, dtype)


def route_kernel(experts, capacity, routes_hbm, gates_hbm, tokens_hbm, cotangent_hbm, *refs):
    blocks, place_refs, scratch = refs[:experts], refs[experts : experts + 2], refs[experts + 2 :]
    routes, gates, tokens, cotangent, sems = scratch
    copies = [
        pltpu.make_async_copy(source, target, sems.at[i])
        for i, (source, target) in enumerate(
            (
                (routes_hbm, routes),
                (gates_hbm, gates),
                (tokens_hbm, tokens),
                (cotangent_hbm, cotangent),
            )
        )
    ]
    for copy in copies:
        copy.start()
    tok_count, feat_width = tokens.shape
    slots_all = experts * capacity
    me = lax.axis_index("expert")
    rows = max(experts, 16)
    before = (
        lax.broadcasted_iota(jnp.int32, (tok_count, tok_count), 0)
        < lax.broadcasted_iota(jnp.int32, (tok_count, tok_count), 1)
    ).astype(F32).astype(BF16)
    expert_id = lax.broadcasted_iota(jnp.int32, (rows, tok_count), 0)
    slot_id = lax.broadcasted_iota(jnp.int32, (slots_all, tok_count), 0)
    taken = jnp.zeros((rows, 1), F32)
    places, gated = [], jnp.zeros((slots_all, tok_count), F32)
    copies[0].wait()
    copies[1].wait()
    for choice in range(2):
        chosen = routes[choice : choice + 1, :]
        one_hot = (expert_id == chosen).astype(F32)
        earlier = dot(one_hot.astype(BF16), before) + taken
        taken = taken + jnp.sum(one_hot, axis=1, keepdims=True)
        slot_pos = jnp.sum(earlier * one_hot, axis=0, keepdims=True).astype(jnp.int32)
        target = jnp.where(
            slot_pos < capacity, jnp.bitwise_xor(chosen, me) * capacity + slot_pos, slots_all
        )
        place = (slot_id == target).astype(F32)
        place_refs[choice][...] = place.astype(BF16)
        places.append(place)
        gated = gated + place * gates[choice : choice + 1, :].astype(F32)
    copies[2].wait()
    x = dot((places[0] + places[1]).astype(BF16), tokens[...]).astype(BF16)
    copies[3].wait()
    s = dot(gated.astype(BF16), cotangent[...]).astype(BF16)
    for k in range(experts):
        blocks[k][:, :feat_width] = x[k * capacity : (k + 1) * capacity]
        blocks[k][:, feat_width:] = s[k * capacity : (k + 1) * capacity]


def block_rows(me, k, capacity):
    return pl.ds(pl.multiple_of(jnp.bitwise_xor(me, k) * capacity, capacity), capacity)


def combine_kernel(experts, capacity, place0, place1, gates, back, token_grads, gate_grads, rows):
    tok_count, feat_width = token_grads.shape
    me = lax.axis_index("expert")
    for k in range(experts):
        rows[k * capacity : (k + 1) * capacity, :] = back[block_rows(me, k, capacity), :]
    either = (place0[...].astype(F32) + place1[...].astype(F32)).astype(BF16)
    token_grads[...] = dot(either, rows[:, :feat_width], (0, 0)).astype(BF16)
    dgate = rows[:, feat_width : feat_width + tok_count].astype(F32)
    taken = [
        jnp.sum(place[...].astype(F32) * dgate, axis=0, keepdims=True) for place in (place0, place1)
    ]
    gate_grads[...] = (jnp.concatenate(taken, axis=0) / gates[...].astype(F32)).astype(BF16)


def stack(refs, part, width):
    return jnp.concatenate([ref[:, part * width : (part + 1) * width] for ref in refs], axis=0)


def my_part(ref):
    width = ref.shape[1] // lax.axis_size("dp")
    return ref[:, pl.ds(pl.multiple_of(lax.axis_index("dp") * width, width), width)]


def fetcher(sems):
    count = iter(range(sems.shape[0]))

    def fetch(source, target):
        copy = pltpu.make_async_copy(source, target, sems.at[next(count)])
        copy.start()
        return copy

    return fetch


def backward_tiles(tiles, x, s, weight_in, weight_out, arrived=lambda t: None):
    arrived(0)
    ahead = dot(x, weight_in[:, tiles[0]])
    for t, cols in enumerate(tiles):
        pre_act = ahead
        if t + 1 < len(tiles):
            arrived(t + 1)
            ahead = dot(x, weight_in[:, tiles[t + 1]])
        d_hidden = dot(s, weight_out[cols, :], (1, 1))
        act, slope = activate(pre_act)
        yield cols, act, d_hidden, (d_hidden * slope).astype(BF16)


def own_kernel(tile, order, *refs):
    row_refs, refs = refs[:2], refs[2:]
    weight_in, weight_out, d_pre_hbm, h_cut_hbm, back_hbm, *scratch = refs
    hidden, d_pre, h_cut, back, sems = scratch
    me = lax.axis_index("expert")
    width, ffw = weight_in.shape
    tiles = [slice(at, at + tile) for at in range(0, ffw, tile)]
    fetch = fetcher(sems)
    x, s = stack(row_refs, 0, width), stack(row_refs, 1, width)
    slots_all = x.shape[0]
    capacity = slots_all // len(order)
    dgate = jnp.zeros((slots_all, LANES), F32)
    for cols, act, d_hidden, part in backward_tiles(tiles, x, s, weight_in, weight_out):
        hidden[:, cols] = act
        d_pre[:, cols] = part
        product = d_hidden * act.astype(F32)
        for lane in range(0, tile, LANES):
            dgate = dgate + product[:, lane : lane + LANES]
    h_cut[...] = my_part(hidden)
    dgate = jnp.broadcast_to(jnp.sum(dgate, axis=1, keepdims=True), (slots_all, LANES))
    places = [
        (slice(i * capacity, (i + 1) * capacity), block_rows(me, k, capacity))
        for i, k in enumerate(order)
    ]
    for rows, target in places:
        back[target, width:] = dgate[rows].astype(BF16)
    outs = [
        fetch(d_pre, d_pre_hbm),
        fetch(h_cut, h_cut_hbm),
        fetch(back.at[:, width:], back_hbm.at[:, width:]),
    ]
    wide = width // 4
    for at in range(0, width, wide):
        cols = slice(at, at + wide)
        dx = dot(d_pre[...], weight_in[cols, :], (1, 1)).astype(BF16)
        for rows, target in places:
            back[target, cols] = dx[rows]
        outs.append(fetch(back.at[:, cols], back_hbm.at[:, cols]))
    for copy in outs:
        copy.wait()


def early_kernel(tile, pieces, *refs):
    row_refs, refs = refs[:pieces], refs[pieces:]
    in_hbm, out_hbm, weight_in, weight_out, d_pre, h_cut, hidden, sems = refs
    width, ffw = weight_in.shape
    tiles = [slice(at, at + tile) for at in range(0, ffw, tile)]
    fetch = fetcher(sems)
    copies = [
        (
            fetch(in_hbm.at[:, cols], weight_in.at[:, cols]),
            fetch(out_hbm.at[cols, :], weight_out.at[cols, :]),
        )
        for cols in tiles
    ]

    def arrived(t):
        for copy in copies[t]:
            copy.wait()

    x, s = stack(row_refs, 0, width), stack(row_refs, 1, width)
    for cols, act, _, part in backward_tiles(tiles, x, s, weight_in, weight_out, arrived):
        hidden[:, cols] = act
        d_pre[:, cols] = part
    h_cut[...] = my_part(hidden)


def grads_kernel(tile, pieces, late, *refs):
    row_refs, refs = refs[:pieces], refs[pieces:]
    d_pre_refs, h_cut_refs, refs = refs[:2], refs[2:4], refs[4:]
    weight_in, weight_out, grad_in_hbm, grad_out_hbm, *scratch = refs
    rows, hidden, h_cut, d_pre, grad_in, grad_out, sems, out_sems = scratch
    width, ffw = weight_in.shape
    tiles = [slice(at, at + tile) for at in range(0, ffw, tile)]
    piece = row_refs[0].shape[0]
    known = (pieces - late) * piece
    fetch, send = fetcher(sems), fetcher(out_sems)
    copies = [
        fetch(row_refs[i], rows.at[pl.ds(i * piece, piece)])
        for i in [*range(pieces - late, pieces), *range(pieces - late)]
    ]
    at = 0
    for source, cut_source in zip(d_pre_refs, h_cut_refs):
        span = pl.ds(at, source.shape[0])
        copies += [fetch(source, d_pre.at[span]), fetch(cut_source, h_cut.at[span])]
        at += source.shape[0]
    x, s = stack(row_refs[-late:], 0, width), stack(row_refs[-late:], 1, width)
    for cols, act, _, part in backward_tiles(tiles, x, s, weight_in, weight_out):
        hidden[:, cols] = act
        d_pre[known:, cols] = part
    for copy in copies:
        copy.wait()
    cut = grad_in.shape[0]
    mine = pl.ds(pl.multiple_of(lax.axis_index("dp") * cut, cut), cut)
    outs = []
    for at in range(0, ffw, ffw // 2):
        cols = slice(at, at + ffw // 2)
        grad_in[:, cols] = dot(rows[:, mine], d_pre[:, cols], (0, 0)).astype(BF16)
        outs.append(send(grad_in.at[:, cols], grad_in_hbm.at[:, cols]))
    h_cut[known:, :] = my_part(hidden)
    for at in range(0, tile, tile // 2):
        part = slice(at, at + tile // 2)
        grad_out[part, :] = dot(h_cut[:, part], rows[:, width:], (0, 0)).astype(BF16)
        outs.append(send(grad_out.at[part, :], grad_out_hbm.at[part, :]))
    for copy in outs:
        copy.wait()


def after(value, *first):
    return lax.optimization_barrier((value, *first))[0]


def permute(block, k):
    return lax.ppermute(block, "expert", [(i, i ^ k) for i in range(lax.axis_size("expert"))])


def swap_cores(rows):
    return lax.ppermute(rows, "dp", [(i, i ^ 1) for i in range(lax.axis_size("dp"))])


def shift_chips(rows, k):
    groups = lax.axis_size("dp")
    return lax.ppermute(rows, "dp", [(i, (i + 2 * k) % groups) for i in range(groups)])


def gather_groups(rows):
    others = [swap_cores(rows)]
    for k in range(1, lax.axis_size("dp") // 2):
        other = shift_chips(rows, k)
        others += [other, swap_cores(other)]
    return others


def local(tokens, cotangent, routes, gates, proj_in, proj_out):
    tok_count, feat_width = tokens.shape
    experts = lax.axis_size("expert")
    groups = lax.axis_size("dp")
    capacity = 2 * tok_count // experts
    slots_all = experts * capacity
    half = experts // 2
    ffw = proj_in.shape[2]
    tile = ffw // groups
    product = 2 * slots_all * feat_width * ffw
    place = shape((slots_all, tok_count))

    routed = call(
        functools.partial(route_kernel, experts, capacity),
        [shape((capacity, 2 * feat_width))] * experts + [place] * 2,
        [routes.T, gates.T, tokens, cotangent],
        30 * product,
        spaces=[pltpu.HBM] * 4,
        scratch=[
            pltpu.VMEM((2, tok_count), jnp.int32),
            pltpu.VMEM((2, tok_count), BF16),
            pltpu.VMEM((tok_count, feat_width), BF16),
            pltpu.VMEM((tok_count, feat_width), BF16),
            pltpu.SemaphoreType.DMA((4,)),
        ],
    )
    blocks, places = routed[:experts], routed[experts:]
    rest = list(range(experts - 1, 1, -1))
    order = [0, *rest[:2], 1, *rest[2:]]
    order_a, order_b = order[:half], order[half:]
    got_a = [blocks[0]] + [permute(blocks[k], k) for k in order_a[1:]]
    got_b = [
        permute(blocks[k] if i < 2 else after(blocks[k], got_a[-1]), k)
        for i, k in enumerate(order_b)
    ]
    rows_a = jnp.concatenate(got_a, axis=0)
    chips_a = [shift_chips(rows_a, k) for k in range(1, groups // 2)]
    core_a = swap_cores(after(rows_a, got_b[0]))
    rows_b = jnp.concatenate(got_b, axis=0)
    chips_b = [shift_chips(rows_b, k) for k in range(1, groups // 2)]
    core_b = swap_cores(rows_b)
    weights = [proj_in[0], proj_out[0]]
    weight_space = [pltpu.VMEM((feat_width, ffw), BF16), pltpu.VMEM((ffw, feat_width), BF16)]
    d_pre, h_cut, back = call(
        functools.partial(own_kernel, tile, order),
        [
            pltpu.HBM((slots_all, ffw), BF16),
            pltpu.HBM((slots_all, tile), BF16),
            pltpu.HBM((slots_all, feat_width + LANES), BF16),
        ],
        [
            rows_a,
            rows_b,
            *[pltpu.with_memory_space_constraint(w, pltpu.VMEM) for w in weights],
        ],
        20 * product,
        scratch=[
            pltpu.VMEM((slots_all, ffw), BF16),
            pltpu.VMEM((slots_all, ffw), BF16),
            pltpu.VMEM((slots_all, tile), BF16),
            pltpu.VMEM((slots_all, feat_width + LANES), BF16),
            pltpu.SemaphoreType.DMA((7,)),
        ],
    )
    back = lax.all_to_all(
        after(back, core_a, core_b).reshape(experts, capacity, feat_width + LANES),
        "expert",
        0,
        0,
        tiled=True,
    ).reshape(slots_all, feat_width + LANES)
    relayed_a = [swap_cores(after(rows, d_pre)) for rows in chips_a]
    relayed_b = [swap_cores(rows) for rows in chips_b]
    early = [core_a, core_b, *chips_a]
    late = [*relayed_a, *chips_b, *relayed_b]
    early_rows = sum(piece.shape[0] for piece in early)
    late_rows = sum(piece.shape[0] for piece in late)
    weight_in, weight_out, d_pre_early, h_cut_early = call(
        functools.partial(early_kernel, tile, len(early)),
        [*weight_space, shape((early_rows, ffw)), shape((early_rows, tile))],
        [*early, *weights],
        2 * product,
        scratch=[
            pltpu.VMEM((early_rows, ffw), BF16),
            pltpu.SemaphoreType.DMA((2 * groups,)),
        ],
        spaces=[pltpu.VMEM] * len(early) + [pltpu.HBM] * 2,
    )
    pieces = [rows_a, rows_b, *early, *late]
    rows_all = groups * slots_all
    grad_in, grad_out = call(
        functools.partial(grads_kernel, tile, len(pieces), len(late)),
        [
            pltpu.HBM((feat_width // groups, ffw), BF16),
            pltpu.HBM((ffw // groups, feat_width), BF16),
        ],
        [
            *pieces,
            *[d_pre, d_pre_early, h_cut, h_cut_early],
            *[
                pltpu.with_memory_space_constraint(w, pltpu.VMEM)
                for w in (weight_in, weight_out)
            ],
        ],
        4 * product,
        limit=32,
        scratch=[
            pltpu.VMEM((rows_all, 2 * feat_width), BF16),
            pltpu.VMEM((late_rows, ffw), BF16),
            pltpu.VMEM((rows_all, tile), BF16),
            pltpu.VMEM((rows_all, ffw), BF16),
            pltpu.VMEM((feat_width // groups, ffw), BF16),
            pltpu.VMEM((ffw // groups, feat_width), BF16),
            pltpu.SemaphoreType.DMA((len(pieces) + 4,)),
            pltpu.SemaphoreType.DMA((4,)),
        ],
        spaces=[pl.ANY] * (len(pieces) - len(late))
        + [pltpu.VMEM] * len(late)
        + [pltpu.HBM, pl.ANY] * 2
        + [pltpu.VMEM] * 2,
    )
    token_grads, gate_grads = call(
        functools.partial(combine_kernel, experts, capacity),
        [shape((tok_count, feat_width)), shape((2, tok_count))],
        [*places, gates.T, after(back, grad_in)],
        scratch=[pltpu.VMEM((slots_all, feat_width + LANES), BF16)],
    )
    return (token_grads, gate_grads.T, grad_in[None], grad_out[None])


def local_small_blocks(tokens, cotangent, routes, gates, proj_in, proj_out):
    tok_count, feat_width = tokens.shape
    experts = lax.axis_size("expert")
    groups = lax.axis_size("dp")
    me = lax.axis_index("dp")
    capacity = 2 * tok_count // experts
    slots_all = experts * capacity
    weight_in, weight_out = proj_in[0], proj_out[0]
    ffw = weight_in.shape[1]
    chosen = jnp.concatenate([routes[:, 0], routes[:, 1]])
    one_hot = (chosen[:, None] == jnp.arange(experts, dtype=jnp.int32)[None, :]).astype(jnp.int32)
    slot_pos = jnp.sum((jnp.cumsum(one_hot, axis=0) - one_hot) * one_hot, axis=1)
    target = jnp.where(slot_pos < capacity, chosen * capacity + slot_pos, slots_all)
    placing = (jnp.arange(slots_all, dtype=jnp.int32)[:, None] == target[None, :]).astype(BF16)
    either = placing[:, :tok_count] + placing[:, tok_count:]
    scaled = [
        (gates[:, k : k + 1].astype(F32) * cotangent.astype(F32)).astype(BF16) for k in range(2)
    ]

    def swap_blocks(rows):
        return lax.all_to_all(
            rows.astype(BF16).reshape(experts, capacity, rows.shape[1]), "expert", 0, 0, tiled=True
        ).reshape(slots_all, rows.shape[1])

    x = swap_blocks(dot(either, tokens))
    s = swap_blocks(dot(placing, jnp.concatenate(scaled, axis=0)))
    hidden0, slope0 = activate(dot(x, weight_in))
    d_hidden0 = dot(s, weight_out, (1, 1))
    d_pre0 = (d_hidden0 * slope0).astype(BF16)
    dgate = jnp.sum(hidden0.astype(F32) * d_hidden0, axis=1, keepdims=True)
    dx = dot(d_pre0, weight_in, (1, 1))
    back = swap_blocks(
        jnp.concatenate([dx, jnp.broadcast_to(dgate, (slots_all, LANES))], axis=1)
    )
    x_all = jnp.concatenate([x, *gather_groups(x)], axis=0)
    s_all = jnp.concatenate([s, *gather_groups(s)], axis=0)
    hidden1, slope1 = activate(dot(x_all[slots_all:], weight_in))
    d_pre1 = (dot(s_all[slots_all:], weight_out, (1, 1)) * slope1).astype(BF16)
    hidden = jnp.concatenate([hidden0, hidden1], axis=0)
    d_pre = jnp.concatenate([d_pre0, d_pre1], axis=0)
    x_cut = lax.dynamic_slice_in_dim(x_all, me * (feat_width // groups), feat_width // groups, 1)
    h_cut = lax.dynamic_slice_in_dim(hidden, me * (ffw // groups), ffw // groups, 1)
    grad_in = dot(x_cut, d_pre, (0, 0)).astype(BF16)
    grad_out = dot(h_cut, s_all, (0, 0)).astype(BF16)
    token_grads = dot(either, back[:, :feat_width], (0, 0)).astype(BF16)
    taken = dot(placing, back[:, feat_width : feat_width + 1], (0, 0))
    gate_grads = jnp.concatenate([taken[:tok_count], taken[tok_count:]], axis=1)
    gate_grads = (gate_grads / gates.astype(F32)).astype(BF16)
    return (token_grads, gate_grads, grad_in[None], grad_out[None])


def solution(mesh):
    rows = P(("dp", "expert"), None)
    weights = P("expert", None, None)

    def whole(tokens, *others):
        experts = mesh.shape["expert"]
        capacity = 2 * tokens.shape[0] // (mesh.shape["dp"] * experts) // experts
        tiles = capacity % 16 == 0 and experts & (experts - 1) == 0
        return jax.shard_map(
            local if tiles else local_small_blocks,
            mesh=mesh,
            in_specs=(rows, rows, rows, rows, weights, weights),
            out_specs=(rows, rows, P("expert", "dp", None), P("expert", "dp", None)),
            check_vma=False,
        )(tokens, *others)

    return whole
```

```python
import functools

import jax
import jax.numpy as jnp
from jax import lax
from jax.experimental import pallas as pl
from jax.experimental.pallas import tpu as pltpu
from jax.sharding import PartitionSpec as P

BF16 = jnp.bfloat16
F32 = jnp.float32
LANES = 128
MIB = 1 << 20


def dot(a, b, over=(1, 0)):
    return lax.dot_general(
        a, b, (((over[0],), (over[1],)), ((), ())), preferred_element_type=F32
    )


def activate(pre_act):
    cdf = 0.5 * (1.0 + lax.erf(pre_act * 0.7071067811865476))
    pdf = jnp.exp(-0.5 * pre_act * pre_act) * 0.3989422804014327
    return (pre_act * cdf).astype(BF16), cdf + pre_act * pdf


def call(kernel, out_shape, args, flops=0, limit=24, scratch=(), spaces=None):
    spaces = spaces or [pltpu.VMEM] * len(args)
    moved = sum(a.size * a.dtype.itemsize for a in args)
    args = [
        pltpu.with_memory_space_constraint(a, space) if space == pltpu.HBM else a
        for a, space in zip(args, spaces)
    ]
    return pl.pallas_call(
        kernel,
        out_shape=out_shape,
        in_specs=[pl.BlockSpec(memory_space=space) for space in spaces],
        out_specs=[
            pl.BlockSpec(memory_space=getattr(out, "memory_space", pltpu.VMEM))
            for out in out_shape
        ],
        scratch_shapes=list(scratch),
        compiler_params=pltpu.CompilerParams(vmem_limit_bytes=limit * MIB),
        cost_estimate=pl.CostEstimate(flops=flops, bytes_accessed=moved, transcendentals=0),
    )(*args)


def shape(dims, dtype=BF16):
    return jax.ShapeDtypeStruct(dims, dtype)


def route_kernel(experts, capacity, routes_hbm, gates_hbm, tokens_hbm, cotangent_hbm, *refs):
    blocks, place_refs, scratch = refs[:experts], refs[experts : experts + 2], refs[experts + 2 :]
    routes, gates, tokens, cotangent, sems = scratch
    copies = [
        pltpu.make_async_copy(source, target, sems.at[i])
        for i, (source, target) in enumerate(
            (
                (routes_hbm, routes),
                (gates_hbm, gates),
                (tokens_hbm, tokens),
                (cotangent_hbm, cotangent),
            )
        )
    ]
    for copy in copies:
        copy.start()
    tok_count, feat_width = tokens.shape
    slots_all = experts * capacity
    me = lax.axis_index("expert")
    rows = max(experts, 16)
    before = (
        lax.broadcasted_iota(jnp.int32, (tok_count, tok_count), 0)
        < lax.broadcasted_iota(jnp.int32, (tok_count, tok_count), 1)
    ).astype(F32).astype(BF16)
    expert_id = lax.broadcasted_iota(jnp.int32, (rows, tok_count), 0)
    slot_id = lax.broadcasted_iota(jnp.int32, (slots_all, tok_count), 0)
    taken = jnp.zeros((rows, 1), F32)
    places, gated = [], jnp.zeros((slots_all, tok_count), F32)
    copies[0].wait()
    copies[1].wait()
    for choice in range(2):
        chosen = routes[choice : choice + 1, :]
        one_hot = (expert_id == chosen).astype(F32)
        earlier = dot(one_hot.astype(BF16), before) + taken
        taken = taken + jnp.sum(one_hot, axis=1, keepdims=True)
        slot_pos = jnp.sum(earlier * one_hot, axis=0, keepdims=True).astype(jnp.int32)
        target = jnp.where(
            slot_pos < capacity, jnp.bitwise_xor(chosen, me) * capacity + slot_pos, slots_all
        )
        place = (slot_id == target).astype(F32)
        place_refs[choice][...] = place.astype(BF16)
        places.append(place)
        gated = gated + place * gates[choice : choice + 1, :].astype(F32)
    copies[2].wait()
    x = dot((places[0] + places[1]).astype(BF16), tokens[...]).astype(BF16)
    copies[3].wait()
    s = dot(gated.astype(BF16), cotangent[...]).astype(BF16)
    for k in range(experts):
        blocks[k][:, :feat_width] = x[k * capacity : (k + 1) * capacity]
        blocks[k][:, feat_width:] = s[k * capacity : (k + 1) * capacity]


def block_rows(me, k, capacity):
    return pl.ds(pl.multiple_of(jnp.bitwise_xor(me, k) * capacity, capacity), capacity)


def combine_kernel(experts, capacity, place0, place1, gates, back, token_grads, gate_grads, rows):
    tok_count, feat_width = token_grads.shape
    me = lax.axis_index("expert")
    for k in range(experts):
        rows[k * capacity : (k + 1) * capacity, :] = back[block_rows(me, k, capacity), :]
    either = (place0[...].astype(F32) + place1[...].astype(F32)).astype(BF16)
    token_grads[...] = dot(either, rows[:, :feat_width], (0, 0)).astype(BF16)
    dgate = rows[:, feat_width : feat_width + tok_count].astype(F32)
    taken = [
        jnp.sum(place[...].astype(F32) * dgate, axis=0, keepdims=True) for place in (place0, place1)
    ]
    gate_grads[...] = (jnp.concatenate(taken, axis=0) / gates[...].astype(F32)).astype(BF16)


def stack(refs, part, width):
    return jnp.concatenate([ref[:, part * width : (part + 1) * width] for ref in refs], axis=0)


def my_part(ref):
    width = ref.shape[1] // lax.axis_size("dp")
    return ref[:, pl.ds(pl.multiple_of(lax.axis_index("dp") * width, width), width)]


def fetcher(sems):
    count = iter(range(sems.shape[0]))

    def fetch(source, target):
        copy = pltpu.make_async_copy(source, target, sems.at[next(count)])
        copy.start()
        return copy

    return fetch


def own_kernel(tile, order, *refs):
    row_refs, refs = refs[:2], refs[2:]
    weight_in, weight_out, d_pre_hbm, h_cut_hbm, back_hbm, *scratch = refs
    hidden, d_pre, h_cut, back, sems = scratch
    me = lax.axis_index("expert")
    width, ffw = weight_in.shape
    tiles = [slice(at, at + tile) for at in range(0, ffw, tile)]
    fetch = fetcher(sems)
    x, s = stack(row_refs, 0, width), stack(row_refs, 1, width)
    slots_all = x.shape[0]
    capacity = slots_all // len(order)
    dgate = jnp.zeros((slots_all, LANES), F32)
    for cols in tiles:
        act, slope = activate(dot(x, weight_in[:, cols]))
        hidden[:, cols] = act
        d_hidden = dot(s, weight_out[cols, :], (1, 1))
        d_pre[:, cols] = (d_hidden * slope).astype(BF16)
        product = d_hidden * act.astype(F32)
        for lane in range(0, tile, LANES):
            dgate = dgate + product[:, lane : lane + LANES]
    h_cut[...] = my_part(hidden)
    dgate = jnp.broadcast_to(jnp.sum(dgate, axis=1, keepdims=True), (slots_all, LANES))
    places = [
        (slice(i * capacity, (i + 1) * capacity), block_rows(me, k, capacity))
        for i, k in enumerate(order)
    ]
    for rows, target in places:
        back[target, width:] = dgate[rows].astype(BF16)
    outs = [
        fetch(d_pre, d_pre_hbm),
        fetch(h_cut, h_cut_hbm),
        fetch(back.at[:, width:], back_hbm.at[:, width:]),
    ]
    wide = width // 4
    for at in range(0, width, wide):
        cols = slice(at, at + wide)
        dx = dot(d_pre[...], weight_in[cols, :], (1, 1)).astype(BF16)
        for rows, target in places:
            back[target, cols] = dx[rows]
        outs.append(fetch(back.at[:, cols], back_hbm.at[:, cols]))
    for copy in outs:
        copy.wait()


def early_kernel(tile, pieces, *refs):
    row_refs, (weight_in, weight_out, d_pre, h_cut, hidden) = refs[:pieces], refs[pieces:]
    width, ffw = weight_in.shape
    x, s = stack(row_refs, 0, width), stack(row_refs, 1, width)
    for at in range(0, ffw, tile):
        cols = slice(at, at + tile)
        act, slope = activate(dot(x, weight_in[:, cols]))
        hidden[:, cols] = act
        d_pre[:, cols] = (dot(s, weight_out[cols, :], (1, 1)) * slope).astype(BF16)
    h_cut[...] = my_part(hidden)


def grads_kernel(tile, pieces, late, *refs):
    row_refs, refs = refs[:pieces], refs[pieces:]
    d_pre_refs, h_cut_refs, refs = refs[:2], refs[2:4], refs[4:]
    in_hbm, out_hbm, grad_in_hbm, grad_out_hbm, weight_in, weight_out, *scratch = refs
    rows, hidden, h_cut, d_pre, grad_in, grad_out, sems, out_sems = scratch
    width, ffw = weight_in.shape
    tiles = [slice(at, at + tile) for at in range(0, ffw, tile)]
    piece = row_refs[0].shape[0]
    known = (pieces - late) * piece
    fetch, send = fetcher(sems), fetcher(out_sems)
    weights = [
        (
            fetch(in_hbm.at[:, cols], weight_in.at[:, cols]),
            fetch(out_hbm.at[cols, :], weight_out.at[cols, :]),
        )
        for cols in tiles
    ]
    copies = [
        fetch(row_refs[i], rows.at[pl.ds(i * piece, piece)])
        for i in [*range(pieces - late, pieces), *range(pieces - late)]
    ]
    at = 0
    for source, cut_source in zip(d_pre_refs, h_cut_refs):
        span = pl.ds(at, source.shape[0])
        copies += [fetch(source, d_pre.at[span]), fetch(cut_source, h_cut.at[span])]
        at += source.shape[0]
    x, s = stack(row_refs[-late:], 0, width), stack(row_refs[-late:], 1, width)
    for cols, pair in zip(tiles, weights):
        for copy in pair:
            copy.wait()
        act, slope = activate(dot(x, weight_in[:, cols]))
        hidden[:, cols] = act
        d_pre[known:, cols] = (dot(s, weight_out[cols, :], (1, 1)) * slope).astype(BF16)
    for copy in copies:
        copy.wait()
    cut = grad_in.shape[0]
    mine = pl.ds(pl.multiple_of(lax.axis_index("dp") * cut, cut), cut)
    outs = []
    for at in range(0, ffw, ffw // 2):
        cols = slice(at, at + ffw // 2)
        grad_in[:, cols] = dot(rows[:, mine], d_pre[:, cols], (0, 0)).astype(BF16)
        outs.append(send(grad_in.at[:, cols], grad_in_hbm.at[:, cols]))
    h_cut[known:, :] = my_part(hidden)
    for at in range(0, tile, tile // 2):
        part = slice(at, at + tile // 2)
        grad_out[part, :] = dot(h_cut[:, part], rows[:, width:], (0, 0)).astype(BF16)
        outs.append(send(grad_out.at[part, :], grad_out_hbm.at[part, :]))
    for copy in outs:
        copy.wait()


def after(value, *first):
    return lax.optimization_barrier((value, *first))[0]


def permute(block, k):
    return lax.ppermute(block, "expert", [(i, i ^ k) for i in range(lax.axis_size("expert"))])


def swap_cores(rows):
    return lax.ppermute(rows, "dp", [(i, i ^ 1) for i in range(lax.axis_size("dp"))])


def shift_chips(rows, k):
    groups = lax.axis_size("dp")
    return lax.ppermute(rows, "dp", [(i, (i + 2 * k) % groups) for i in range(groups)])


def gather_groups(rows):
    others = [swap_cores(rows)]
    for k in range(1, lax.axis_size("dp") // 2):
        other = shift_chips(rows, k)
        others += [other, swap_cores(other)]
    return others


def local(tokens, cotangent, routes, gates, proj_in, proj_out):
    tok_count, feat_width = tokens.shape
    experts = lax.axis_size("expert")
    groups = lax.axis_size("dp")
    capacity = 2 * tok_count // experts
    slots_all = experts * capacity
    half = experts // 2
    ffw = proj_in.shape[2]
    tile = ffw // groups
    product = 2 * slots_all * feat_width * ffw
    place = shape((slots_all, tok_count))

    routed = call(
        functools.partial(route_kernel, experts, capacity),
        [shape((capacity, 2 * feat_width))] * experts + [place] * 2,
        [routes.T, gates.T, tokens, cotangent],
        30 * product,
        spaces=[pltpu.HBM] * 4,
        scratch=[
            pltpu.VMEM((2, tok_count), jnp.int32),
            pltpu.VMEM((2, tok_count), BF16),
            pltpu.VMEM((tok_count, feat_width), BF16),
            pltpu.VMEM((tok_count, feat_width), BF16),
            pltpu.SemaphoreType.DMA((4,)),
        ],
    )
    blocks, places = routed[:experts], routed[experts:]
    rest = list(range(experts - 1, 1, -1))
    order = [0, *rest[:2], 1, *rest[2:]]
    order_a, order_b = order[:half], order[half:]
    got_a = [blocks[0]] + [permute(blocks[k], k) for k in order_a[1:]]
    got_b = [
        permute(blocks[k] if i < 2 else after(blocks[k], got_a[-1]), k)
        for i, k in enumerate(order_b)
    ]
    rows_a = jnp.concatenate(got_a, axis=0)
    chips_a = [shift_chips(rows_a, k) for k in range(1, groups // 2)]
    core_a = swap_cores(after(rows_a, got_b[0]))
    rows_b = jnp.concatenate(got_b, axis=0)
    chips_b = [shift_chips(rows_b, k) for k in range(1, groups // 2)]
    core_b = swap_cores(rows_b)
    weights = [proj_in[0], proj_out[0]]
    near_weights = [pltpu.with_memory_space_constraint(w, pltpu.VMEM) for w in weights]
    d_pre, h_cut, back = call(
        functools.partial(own_kernel, tile, order),
        [
            pltpu.HBM((slots_all, ffw), BF16),
            pltpu.HBM((slots_all, tile), BF16),
            pltpu.HBM((slots_all, feat_width + LANES), BF16),
        ],
        [rows_a, rows_b, *near_weights],
        20 * product,
        scratch=[
            pltpu.VMEM((slots_all, ffw), BF16),
            pltpu.VMEM((slots_all, ffw), BF16),
            pltpu.VMEM((slots_all, tile), BF16),
            pltpu.VMEM((slots_all, feat_width + LANES), BF16),
            pltpu.SemaphoreType.DMA((7,)),
        ],
    )
    early = [after(rows, d_pre) for rows in [core_a, core_b, *chips_a]]
    early_rows = sum(piece.shape[0] for piece in early)
    d_pre_early, h_cut_early = call(
        functools.partial(early_kernel, tile, len(early)),
        [shape((early_rows, ffw)), shape((early_rows, tile))],
        [*early, *near_weights],
        2 * product,
        scratch=[pltpu.VMEM((early_rows, ffw), BF16)],
    )
    back = lax.all_to_all(
        after(back, d_pre_early).reshape(experts, capacity, feat_width + LANES),
        "expert",
        0,
        0,
        tiled=True,
    ).reshape(slots_all, feat_width + LANES)
    relayed_a = [swap_cores(after(rows, d_pre)) for rows in chips_a]
    relayed_b = [swap_cores(after(rows, d_pre_early)) for rows in chips_b]
    late = [*relayed_a, *chips_b, *relayed_b]
    late_rows = sum(piece.shape[0] for piece in late)
    pieces = [rows_a, rows_b, *early, *late]
    rows_all = groups * slots_all
    grad_in, grad_out = call(
        functools.partial(grads_kernel, tile, len(pieces), len(late)),
        [
            pltpu.HBM((feat_width // groups, ffw), BF16),
            pltpu.HBM((ffw // groups, feat_width), BF16),
        ],
        [*pieces, *[d_pre, d_pre_early, h_cut, h_cut_early], *weights],
        4 * product,
        limit=36,
        scratch=[
            pltpu.VMEM((feat_width, ffw), BF16),
            pltpu.VMEM((ffw, feat_width), BF16),
            pltpu.VMEM((rows_all, 2 * feat_width), BF16),
            pltpu.VMEM((late_rows, ffw), BF16),
            pltpu.VMEM((rows_all, tile), BF16),
            pltpu.VMEM((rows_all, ffw), BF16),
            pltpu.VMEM((feat_width // groups, ffw), BF16),
            pltpu.VMEM((ffw // groups, feat_width), BF16),
            pltpu.SemaphoreType.DMA((len(pieces) + 4 + 2 * groups,)),
            pltpu.SemaphoreType.DMA((4,)),
        ],
        spaces=[pl.ANY] * (len(pieces) - len(late))
        + [pltpu.VMEM] * len(late)
        + [pltpu.HBM, pl.ANY] * 2
        + [pltpu.HBM] * 2,
    )
    token_grads, gate_grads = call(
        functools.partial(combine_kernel, experts, capacity),
        [shape((tok_count, feat_width)), shape((2, tok_count))],
        [*places, gates.T, after(back, grad_in)],
        scratch=[pltpu.VMEM((slots_all, feat_width + LANES), BF16)],
    )
    return (token_grads, gate_grads.T, grad_in[None], grad_out[None])


def local_small_blocks(tokens, cotangent, routes, gates, proj_in, proj_out):
    tok_count, feat_width = tokens.shape
    experts = lax.axis_size("expert")
    groups = lax.axis_size("dp")
    me = lax.axis_index("dp")
    capacity = 2 * tok_count // experts
    slots_all = experts * capacity
    weight_in, weight_out = proj_in[0], proj_out[0]
    ffw = weight_in.shape[1]
    chosen = jnp.concatenate([routes[:, 0], routes[:, 1]])
    one_hot = (chosen[:, None] == jnp.arange(experts, dtype=jnp.int32)[None, :]).astype(jnp.int32)
    slot_pos = jnp.sum((jnp.cumsum(one_hot, axis=0) - one_hot) * one_hot, axis=1)
    target = jnp.where(slot_pos < capacity, chosen * capacity + slot_pos, slots_all)
    placing = (jnp.arange(slots_all, dtype=jnp.int32)[:, None] == target[None, :]).astype(BF16)
    either = placing[:, :tok_count] + placing[:, tok_count:]
    scaled = [
        (gates[:, k : k + 1].astype(F32) * cotangent.astype(F32)).astype(BF16) for k in range(2)
    ]

    def swap_blocks(rows):
        return lax.all_to_all(
            rows.astype(BF16).reshape(experts, capacity, rows.shape[1]), "expert", 0, 0, tiled=True
        ).reshape(slots_all, rows.shape[1])

    x = swap_blocks(dot(either, tokens))
    s = swap_blocks(dot(placing, jnp.concatenate(scaled, axis=0)))
    hidden0, slope0 = activate(dot(x, weight_in))
    d_hidden0 = dot(s, weight_out, (1, 1))
    d_pre0 = (d_hidden0 * slope0).astype(BF16)
    dgate = jnp.sum(hidden0.astype(F32) * d_hidden0, axis=1, keepdims=True)
    dx = dot(d_pre0, weight_in, (1, 1))
    back = swap_blocks(
        jnp.concatenate([dx, jnp.broadcast_to(dgate, (slots_all, LANES))], axis=1)
    )
    x_all = jnp.concatenate([x, *gather_groups(x)], axis=0)
    s_all = jnp.concatenate([s, *gather_groups(s)], axis=0)
    hidden1, slope1 = activate(dot(x_all[slots_all:], weight_in))
    d_pre1 = (dot(s_all[slots_all:], weight_out, (1, 1)) * slope1).astype(BF16)
    hidden = jnp.concatenate([hidden0, hidden1], axis=0)
    d_pre = jnp.concatenate([d_pre0, d_pre1], axis=0)
    x_cut = lax.dynamic_slice_in_dim(x_all, me * (feat_width // groups), feat_width // groups, 1)
    h_cut = lax.dynamic_slice_in_dim(hidden, me * (ffw // groups), ffw // groups, 1)
    grad_in = dot(x_cut, d_pre, (0, 0)).astype(BF16)
    grad_out = dot(h_cut, s_all, (0, 0)).astype(BF16)
    token_grads = dot(either, back[:, :feat_width], (0, 0)).astype(BF16)
    taken = dot(placing, back[:, feat_width : feat_width + 1], (0, 0))
    gate_grads = jnp.concatenate([taken[:tok_count], taken[tok_count:]], axis=1)
    gate_grads = (gate_grads / gates.astype(F32)).astype(BF16)
    return (token_grads, gate_grads, grad_in[None], grad_out[None])


def solution(mesh):
    rows = P(("dp", "expert"), None)
    weights = P("expert", None, None)

    def whole(tokens, *others):
        experts = mesh.shape["expert"]
        capacity = 2 * tokens.shape[0] // (mesh.shape["dp"] * experts) // experts
        tiles = capacity % 16 == 0 and experts & (experts - 1) == 0
        return jax.shard_map(
            local if tiles else local_small_blocks,
            mesh=mesh,
            in_specs=(rows, rows, rows, rows, weights, weights),
            out_specs=(rows, rows, P("expert", "dp", None), P("expert", "dp", None)),
            check_vma=False,
        )(tokens, *others)

    return whole
```

```python
import functools

import jax
import jax.numpy as jnp
from jax import lax
from jax.experimental import pallas as pl
from jax.experimental.pallas import tpu as pltpu
from jax.sharding import PartitionSpec as P

BF16 = jnp.bfloat16
F32 = jnp.float32
LANES = 128
MIB = 1 << 20


def dot(a, b, over=(1, 0)):
    return lax.dot_general(
        a, b, (((over[0],), (over[1],)), ((), ())), preferred_element_type=F32
    )


def activate(pre_act):
    cdf = 0.5 * (1.0 + lax.erf(pre_act * 0.7071067811865476))
    pdf = jnp.exp(-0.5 * pre_act * pre_act) * 0.3989422804014327
    return (pre_act * cdf).astype(BF16), cdf + pre_act * pdf


def call(kernel, out_shape, args, flops=0, limit=24, scratch=(), spaces=None):
    spaces = spaces or [pltpu.VMEM] * len(args)
    moved = sum(a.size * a.dtype.itemsize for a in args)
    args = [
        pltpu.with_memory_space_constraint(a, space) if space == pltpu.HBM else a
        for a, space in zip(args, spaces)
    ]
    return pl.pallas_call(
        kernel,
        out_shape=out_shape,
        in_specs=[pl.BlockSpec(memory_space=space) for space in spaces],
        out_specs=[
            pl.BlockSpec(memory_space=getattr(out, "memory_space", pltpu.VMEM))
            for out in out_shape
        ],
        scratch_shapes=list(scratch),
        compiler_params=pltpu.CompilerParams(vmem_limit_bytes=limit * MIB),
        cost_estimate=pl.CostEstimate(flops=flops, bytes_accessed=moved, transcendentals=0),
    )(*args)


def shape(dims, dtype=BF16):
    return jax.ShapeDtypeStruct(dims, dtype)


def route_kernel(experts, capacity, routes_hbm, gates_hbm, tokens_hbm, cotangent_hbm, *refs):
    blocks, place_refs, scratch = refs[:experts], refs[experts : experts + 2], refs[experts + 2 :]
    routes, gates, tokens, cotangent, sems = scratch
    copies = [
        pltpu.make_async_copy(source, target, sems.at[i])
        for i, (source, target) in enumerate(
            (
                (routes_hbm, routes),
                (gates_hbm, gates),
                (tokens_hbm, tokens),
                (cotangent_hbm, cotangent),
            )
        )
    ]
    for copy in copies:
        copy.start()
    tok_count, feat_width = tokens.shape
    slots_all = experts * capacity
    me = lax.axis_index("expert")
    rows = max(experts, 16)
    before = (
        lax.broadcasted_iota(jnp.int32, (tok_count, tok_count), 0)
        < lax.broadcasted_iota(jnp.int32, (tok_count, tok_count), 1)
    ).astype(F32).astype(BF16)
    expert_id = lax.broadcasted_iota(jnp.int32, (rows, tok_count), 0)
    slot_id = lax.broadcasted_iota(jnp.int32, (slots_all, tok_count), 0)
    taken = jnp.zeros((rows, 1), F32)
    places, gated = [], jnp.zeros((slots_all, tok_count), F32)
    copies[0].wait()
    copies[1].wait()
    for choice in range(2):
        chosen = routes[choice : choice + 1, :]
        one_hot = (expert_id == chosen).astype(F32)
        earlier = dot(one_hot.astype(BF16), before) + taken
        taken = taken + jnp.sum(one_hot, axis=1, keepdims=True)
        slot_pos = jnp.sum(earlier * one_hot, axis=0, keepdims=True).astype(jnp.int32)
        target = jnp.where(
            slot_pos < capacity, jnp.bitwise_xor(chosen, me) * capacity + slot_pos, slots_all
        )
        place = (slot_id == target).astype(F32)
        place_refs[choice][...] = place.astype(BF16)
        places.append(place)
        gated = gated + place * gates[choice : choice + 1, :].astype(F32)
    copies[2].wait()
    x = dot((places[0] + places[1]).astype(BF16), tokens[...]).astype(BF16)
    copies[3].wait()
    s = dot(gated.astype(BF16), cotangent[...]).astype(BF16)
    for k in range(experts):
        blocks[k][:, :feat_width] = x[k * capacity : (k + 1) * capacity]
        blocks[k][:, feat_width:] = s[k * capacity : (k + 1) * capacity]


def block_rows(me, k, capacity):
    return pl.ds(pl.multiple_of(jnp.bitwise_xor(me, k) * capacity, capacity), capacity)


def combine_kernel(experts, capacity, place0, place1, gates, back, token_grads, gate_grads, rows):
    tok_count, feat_width = token_grads.shape
    me = lax.axis_index("expert")
    for k in range(experts):
        rows[k * capacity : (k + 1) * capacity, :] = back[block_rows(me, k, capacity), :]
    either = (place0[...].astype(F32) + place1[...].astype(F32)).astype(BF16)
    token_grads[...] = dot(either, rows[:, :feat_width], (0, 0)).astype(BF16)
    dgate = rows[:, feat_width : feat_width + tok_count].astype(F32)
    taken = [
        jnp.sum(place[...].astype(F32) * dgate, axis=0, keepdims=True) for place in (place0, place1)
    ]
    gate_grads[...] = (jnp.concatenate(taken, axis=0) / gates[...].astype(F32)).astype(BF16)


def stack(refs, part, width):
    return jnp.concatenate([ref[:, part * width : (part + 1) * width] for ref in refs], axis=0)


def my_part(ref):
    width = ref.shape[1] // lax.axis_size("dp")
    return ref[:, pl.ds(pl.multiple_of(lax.axis_index("dp") * width, width), width)]


def fetcher(sems):
    count = iter(range(sems.shape[0]))

    def fetch(source, target):
        copy = pltpu.make_async_copy(source, target, sems.at[next(count)])
        copy.start()
        return copy

    return fetch


def own_kernel(tile, order, *refs):
    row_refs, refs = refs[:2], refs[2:]
    weight_in, weight_out, d_pre_hbm, h_cut_hbm, back_hbm, *scratch = refs
    hidden, d_pre, h_cut, back, sems = scratch
    me = lax.axis_index("expert")
    width, ffw = weight_in.shape
    tiles = [slice(at, at + tile) for at in range(0, ffw, tile)]
    fetch = fetcher(sems)
    x, s = stack(row_refs, 0, width), stack(row_refs, 1, width)
    slots_all = x.shape[0]
    capacity = slots_all // len(order)
    dgate = jnp.zeros((slots_all, LANES), F32)
    for cols in tiles:
        act, slope = activate(dot(x, weight_in[:, cols]))
        hidden[:, cols] = act
        d_hidden = dot(s, weight_out[cols, :], (1, 1))
        d_pre[:, cols] = (d_hidden * slope).astype(BF16)
        product = d_hidden * act.astype(F32)
        for lane in range(0, tile, LANES):
            dgate = dgate + product[:, lane : lane + LANES]
    h_cut[...] = my_part(hidden)
    dgate = jnp.broadcast_to(jnp.sum(dgate, axis=1, keepdims=True), (slots_all, LANES))
    places = [
        (slice(i * capacity, (i + 1) * capacity), block_rows(me, k, capacity))
        for i, k in enumerate(order)
    ]
    for rows, target in places:
        back[target, width:] = dgate[rows].astype(BF16)
    outs = [
        fetch(d_pre, d_pre_hbm),
        fetch(h_cut, h_cut_hbm),
        fetch(back.at[:, width:], back_hbm.at[:, width:]),
    ]
    wide = width // 4
    for at in range(0, width, wide):
        cols = slice(at, at + wide)
        dx = dot(d_pre[...], weight_in[cols, :], (1, 1)).astype(BF16)
        for rows, target in places:
            back[target, cols] = dx[rows]
        outs.append(fetch(back.at[:, cols], back_hbm.at[:, cols]))
    for copy in outs:
        copy.wait()


def early_kernel(tile, pieces, *refs):
    row_refs, refs = refs[:pieces], refs[pieces:]
    in_hbm, out_hbm, weight_in, weight_out, d_pre, h_cut, rows, hidden, sems = refs
    width, ffw = weight_in.shape
    piece = row_refs[0].shape[0]
    tiles = [slice(at, at + tile) for at in range(0, ffw, tile)]
    fetch = fetcher(sems)
    first = [fetch(ref, rows.at[pl.ds(i * piece, piece)]) for i, ref in enumerate(row_refs)]
    weights = [
        (
            fetch(in_hbm.at[:, cols], weight_in.at[:, cols]),
            fetch(out_hbm.at[cols, :], weight_out.at[cols, :]),
        )
        for cols in tiles
    ]
    for copy in first:
        copy.wait()
    x, s = rows[:, :width], rows[:, width:]
    for cols, (copy_in, copy_out) in zip(tiles, weights):
        copy_in.wait()
        copy_out.wait()
        act, slope = activate(dot(x, weight_in[:, cols]))
        hidden[:, cols] = act
        d_pre[:, cols] = (dot(s, weight_out[cols, :], (1, 1)) * slope).astype(BF16)
    h_cut[...] = my_part(hidden)


def grads_kernel(tile, pieces, late, *refs):
    row_refs, refs = refs[:pieces], refs[pieces:]
    d_pre_refs, h_cut_refs, refs = refs[:2], refs[2:4], refs[4:]
    weight_in, weight_out, grad_in_hbm, grad_out_hbm, *scratch = refs
    rows, hidden, h_cut, d_pre, grad_in, grad_out, sems, out_sems = scratch
    width, ffw = weight_in.shape
    tiles = [slice(at, at + tile) for at in range(0, ffw, tile)]
    piece = row_refs[0].shape[0]
    known = (pieces - late) * piece
    fetch, send = fetcher(sems), fetcher(out_sems)
    copies = [
        fetch(row_refs[i], rows.at[pl.ds(i * piece, piece)])
        for i in [*range(pieces - late, pieces), *range(pieces - late)]
    ]
    at = 0
    for source, cut_source in zip(d_pre_refs, h_cut_refs):
        span = pl.ds(at, source.shape[0])
        copies += [fetch(source, d_pre.at[span]), fetch(cut_source, h_cut.at[span])]
        at += source.shape[0]
    x, s = stack(row_refs[-late:], 0, width), stack(row_refs[-late:], 1, width)
    for cols in tiles:
        act, slope = activate(dot(x, weight_in[:, cols]))
        hidden[:, cols] = act
        d_pre[known:, cols] = (dot(s, weight_out[cols, :], (1, 1)) * slope).astype(BF16)
    for copy in copies:
        copy.wait()
    cut = grad_in.shape[0]
    mine = pl.ds(pl.multiple_of(lax.axis_index("dp") * cut, cut), cut)
    outs = []
    for at in range(0, ffw, ffw // 2):
        cols = slice(at, at + ffw // 2)
        grad_in[:, cols] = dot(rows[:, mine], d_pre[:, cols], (0, 0)).astype(BF16)
        outs.append(send(grad_in.at[:, cols], grad_in_hbm.at[:, cols]))
    h_cut[known:, :] = my_part(hidden)
    wide = h_cut.shape[1] // 2
    for at in (0, wide):
        part = slice(at, at + wide)
        grad_out[part, :] = dot(h_cut[:, part], rows[:, width:], (0, 0)).astype(BF16)
        outs.append(send(grad_out.at[part, :], grad_out_hbm.at[part, :]))
    for copy in outs:
        copy.wait()


def after(value, *first):
    return lax.optimization_barrier((value, *first))[0]


def permute(block, k):
    return lax.ppermute(block, "expert", [(i, i ^ k) for i in range(lax.axis_size("expert"))])


def swap_cores(rows):
    return lax.ppermute(rows, "dp", [(i, i ^ 1) for i in range(lax.axis_size("dp"))])


def shift_chips(rows, k):
    groups = lax.axis_size("dp")
    return lax.ppermute(rows, "dp", [(i, (i + 2 * k) % groups) for i in range(groups)])


def gather_groups(rows):
    others = [swap_cores(rows)]
    for k in range(1, lax.axis_size("dp") // 2):
        other = shift_chips(rows, k)
        others += [other, swap_cores(other)]
    return others


def local(tokens, cotangent, routes, gates, proj_in, proj_out):
    tok_count, feat_width = tokens.shape
    experts = lax.axis_size("expert")
    groups = lax.axis_size("dp")
    capacity = 2 * tok_count // experts
    slots_all = experts * capacity
    half = experts // 2
    ffw = proj_in.shape[2]
    tile = ffw // groups
    product = 2 * slots_all * feat_width * ffw
    place = shape((slots_all, tok_count))

    routed = call(
        functools.partial(route_kernel, experts, capacity),
        [shape((capacity, 2 * feat_width))] * experts + [place] * 2,
        [routes.T, gates.T, tokens, cotangent],
        30 * product,
        spaces=[pltpu.HBM] * 4,
        scratch=[
            pltpu.VMEM((2, tok_count), jnp.int32),
            pltpu.VMEM((2, tok_count), BF16),
            pltpu.VMEM((tok_count, feat_width), BF16),
            pltpu.VMEM((tok_count, feat_width), BF16),
            pltpu.SemaphoreType.DMA((4,)),
        ],
    )
    blocks, places = routed[:experts], routed[experts:]
    rest = list(range(experts - 1, 1, -1))
    if len(rest) > 4:
        rest.insert(2, rest.pop(-2))
    order = [0, *rest[:2], 1, *rest[2:]]
    order_a, order_b = order[:half], order[half:]
    got_a = [blocks[0]] + [permute(blocks[k], k) for k in order_a[1:]]
    got_b = [
        permute(blocks[k] if i < 2 else after(blocks[k], got_a[-1]), k)
        for i, k in enumerate(order_b)
    ]
    rows_a = jnp.concatenate(got_a, axis=0)
    chips_a = [shift_chips(rows_a, k) for k in range(1, groups // 2)]
    core_a = swap_cores(after(rows_a, got_b[0]))
    rows_b = jnp.concatenate(got_b, axis=0)
    chips_b = [shift_chips(rows_b, k) for k in range(1, groups // 2)]
    core_b = swap_cores(rows_b)
    weights = [proj_in[0], proj_out[0]]
    weight_space = [pltpu.VMEM((feat_width, ffw), BF16), pltpu.VMEM((ffw, feat_width), BF16)]
    d_pre, h_cut, back = call(
        functools.partial(own_kernel, tile // 2, order),
        [
            pltpu.HBM((slots_all, ffw), BF16),
            pltpu.HBM((slots_all, tile), BF16),
            pltpu.HBM((slots_all, feat_width + LANES), BF16),
        ],
        [
            rows_a,
            rows_b,
            *[pltpu.with_memory_space_constraint(w, pltpu.VMEM) for w in weights],
        ],
        20 * product,
        scratch=[
            pltpu.VMEM((slots_all, ffw), BF16),
            pltpu.VMEM((slots_all, ffw), BF16),
            pltpu.VMEM((slots_all, tile), BF16),
            pltpu.VMEM((slots_all, feat_width + LANES), BF16),
            pltpu.SemaphoreType.DMA((7,)),
        ],
    )
    back = lax.all_to_all(
        after(back, core_a, core_b).reshape(experts, capacity, feat_width + LANES),
        "expert",
        0,
        0,
        tiled=True,
    ).reshape(slots_all, feat_width + LANES)
    relayed_a = [swap_cores(after(rows, d_pre)) for rows in chips_a]
    relayed_b = [swap_cores(rows) for rows in chips_b]
    early = [core_a, core_b, *chips_a]
    late = [*relayed_a, *chips_b, *relayed_b]
    early_rows = sum(piece.shape[0] for piece in early)
    late_rows = sum(piece.shape[0] for piece in late)
    weight_in, weight_out, d_pre_early, h_cut_early = call(
        functools.partial(early_kernel, tile, len(early)),
        [*weight_space, shape((early_rows, ffw)), shape((early_rows, tile))],
        [*early, *weights],
        2 * product,
        scratch=[
            pltpu.VMEM((early_rows, 2 * feat_width), BF16),
            pltpu.VMEM((early_rows, ffw), BF16),
            pltpu.SemaphoreType.DMA((len(early) + 2 * groups,)),
        ],
        spaces=[pl.ANY] * len(early) + [pltpu.HBM] * 2,
    )
    pieces = [rows_a, rows_b, *early, *late]
    rows_all = groups * slots_all
    grad_in, grad_out = call(
        functools.partial(grads_kernel, tile // 2, len(pieces), len(late)),
        [
            pltpu.HBM((feat_width // groups, ffw), BF16),
            pltpu.HBM((ffw // groups, feat_width), BF16),
        ],
        [
            *pieces,
            *[d_pre, d_pre_early, h_cut, h_cut_early],
            *[
                pltpu.with_memory_space_constraint(w, pltpu.VMEM)
                for w in (weight_in, weight_out)
            ],
        ],
        4 * product,
        limit=32,
        scratch=[
            pltpu.VMEM((rows_all, 2 * feat_width), BF16),
            pltpu.VMEM((late_rows, ffw), BF16),
            pltpu.VMEM((rows_all, tile), BF16),
            pltpu.VMEM((rows_all, ffw), BF16),
            pltpu.VMEM((feat_width // groups, ffw), BF16),
            pltpu.VMEM((ffw // groups, feat_width), BF16),
            pltpu.SemaphoreType.DMA((len(pieces) + 4,)),
            pltpu.SemaphoreType.DMA((4,)),
        ],
        spaces=[pl.ANY] * (len(pieces) - len(late))
        + [pltpu.VMEM] * len(late)
        + [pltpu.HBM, pl.ANY] * 2
        + [pltpu.VMEM] * 2,
    )
    token_grads, gate_grads = call(
        functools.partial(combine_kernel, experts, capacity),
        [shape((tok_count, feat_width)), shape((2, tok_count))],
        [*places, gates.T, after(back, grad_in)],
        scratch=[pltpu.VMEM((slots_all, feat_width + LANES), BF16)],
    )
    return (token_grads, gate_grads.T, grad_in[None], grad_out[None])


def local_small_blocks(tokens, cotangent, routes, gates, proj_in, proj_out):
    tok_count, feat_width = tokens.shape
    experts = lax.axis_size("expert")
    groups = lax.axis_size("dp")
    me = lax.axis_index("dp")
    capacity = 2 * tok_count // experts
    slots_all = experts * capacity
    weight_in, weight_out = proj_in[0], proj_out[0]
    ffw = weight_in.shape[1]
    chosen = jnp.concatenate([routes[:, 0], routes[:, 1]])
    one_hot = (chosen[:, None] == jnp.arange(experts, dtype=jnp.int32)[None, :]).astype(jnp.int32)
    slot_pos = jnp.sum((jnp.cumsum(one_hot, axis=0) - one_hot) * one_hot, axis=1)
    target = jnp.where(slot_pos < capacity, chosen * capacity + slot_pos, slots_all)
    placing = (jnp.arange(slots_all, dtype=jnp.int32)[:, None] == target[None, :]).astype(BF16)
    either = placing[:, :tok_count] + placing[:, tok_count:]
    scaled = [
        (gates[:, k : k + 1].astype(F32) * cotangent.astype(F32)).astype(BF16) for k in range(2)
    ]

    def swap_blocks(rows):
        return lax.all_to_all(
            rows.astype(BF16).reshape(experts, capacity, rows.shape[1]), "expert", 0, 0, tiled=True
        ).reshape(slots_all, rows.shape[1])

    x = swap_blocks(dot(either, tokens))
    s = swap_blocks(dot(placing, jnp.concatenate(scaled, axis=0)))
    hidden0, slope0 = activate(dot(x, weight_in))
    d_hidden0 = dot(s, weight_out, (1, 1))
    d_pre0 = (d_hidden0 * slope0).astype(BF16)
    dgate = jnp.sum(hidden0.astype(F32) * d_hidden0, axis=1, keepdims=True)
    dx = dot(d_pre0, weight_in, (1, 1))
    back = swap_blocks(
        jnp.concatenate([dx, jnp.broadcast_to(dgate, (slots_all, LANES))], axis=1)
    )
    x_all = jnp.concatenate([x, *gather_groups(x)], axis=0)
    s_all = jnp.concatenate([s, *gather_groups(s)], axis=0)
    hidden1, slope1 = activate(dot(x_all[slots_all:], weight_in))
    d_pre1 = (dot(s_all[slots_all:], weight_out, (1, 1)) * slope1).astype(BF16)
    hidden = jnp.concatenate([hidden0, hidden1], axis=0)
    d_pre = jnp.concatenate([d_pre0, d_pre1], axis=0)
    x_cut = lax.dynamic_slice_in_dim(x_all, me * (feat_width // groups), feat_width // groups, 1)
    h_cut = lax.dynamic_slice_in_dim(hidden, me * (ffw // groups), ffw // groups, 1)
    grad_in = dot(x_cut, d_pre, (0, 0)).astype(BF16)
    grad_out = dot(h_cut, s_all, (0, 0)).astype(BF16)
    token_grads = dot(either, back[:, :feat_width], (0, 0)).astype(BF16)
    taken = dot(placing, back[:, feat_width : feat_width + 1], (0, 0))
    gate_grads = jnp.concatenate([taken[:tok_count], taken[tok_count:]], axis=1)
    gate_grads = (gate_grads / gates.astype(F32)).astype(BF16)
    return (token_grads, gate_grads, grad_in[None], grad_out[None])


def solution(mesh):
    rows = P(("dp", "expert"), None)
    weights = P("expert", None, None)

    def whole(tokens, *others):
        experts = mesh.shape["expert"]
        capacity = 2 * tokens.shape[0] // (mesh.shape["dp"] * experts) // experts
        tiles = capacity % 16 == 0 and experts & (experts - 1) == 0
        return jax.shard_map(
            local if tiles else local_small_blocks,
            mesh=mesh,
            in_specs=(rows, rows, rows, rows, weights, weights),
            out_specs=(rows, rows, P("expert", "dp", None), P("expert", "dp", None)),
            check_vma=False,
        )(tokens, *others)

    return whole
```

```python
import functools

import jax
import jax.numpy as jnp
from jax import lax
from jax.experimental import pallas as pl
from jax.experimental.pallas import tpu as pltpu
from jax.sharding import PartitionSpec as P

BF16 = jnp.bfloat16
F32 = jnp.float32
LANES = 128
MIB = 1 << 20


def dot(a, b, over=(1, 0)):
    return lax.dot_general(
        a, b, (((over[0],), (over[1],)), ((), ())), preferred_element_type=F32
    )


def activate(pre_act):
    cdf = 0.5 * (1.0 + lax.erf(pre_act * 0.7071067811865476))
    pdf = jnp.exp(-0.5 * pre_act * pre_act) * 0.3989422804014327
    return (pre_act * cdf).astype(BF16), cdf + pre_act * pdf


def call(kernel, out_shape, args, flops=0, limit=24, scratch=(), spaces=None):
    spaces = spaces or [pltpu.VMEM] * len(args)
    moved = sum(a.size * a.dtype.itemsize for a in args)
    args = [
        pltpu.with_memory_space_constraint(a, space) if space == pltpu.HBM else a
        for a, space in zip(args, spaces)
    ]
    return pl.pallas_call(
        kernel,
        out_shape=out_shape,
        in_specs=[pl.BlockSpec(memory_space=space) for space in spaces],
        out_specs=[
            pl.BlockSpec(memory_space=getattr(out, "memory_space", pltpu.VMEM))
            for out in out_shape
        ],
        scratch_shapes=list(scratch),
        compiler_params=pltpu.CompilerParams(vmem_limit_bytes=limit * MIB),
        cost_estimate=pl.CostEstimate(flops=flops, bytes_accessed=moved, transcendentals=0),
    )(*args)


def shape(dims, dtype=BF16):
    return jax.ShapeDtypeStruct(dims, dtype)


def route_kernel(experts, capacity, routes_hbm, gates, tokens_hbm, cotangent_hbm, *refs):
    blocks, place_refs, scratch = refs[:experts], refs[experts : experts + 2], refs[experts + 2 :]
    routes, tokens, cotangent, sems = scratch
    copies = [
        pltpu.make_async_copy(source, target, sems.at[i])
        for i, (source, target) in enumerate(
            (
                (routes_hbm, routes),
                (tokens_hbm, tokens),
                (cotangent_hbm, cotangent),
            )
        )
    ]
    for copy in copies:
        copy.start()
    tok_count, feat_width = tokens.shape
    slots_all = experts * capacity
    me = lax.axis_index("expert")
    rows = max(experts, 16)
    before = (
        lax.broadcasted_iota(jnp.int32, (tok_count, tok_count), 0)
        < lax.broadcasted_iota(jnp.int32, (tok_count, tok_count), 1)
    ).astype(F32).astype(BF16)
    expert_id = lax.broadcasted_iota(jnp.int32, (rows, tok_count), 0)
    slot_id = lax.broadcasted_iota(jnp.int32, (slots_all, tok_count), 0)
    taken = jnp.zeros((rows, 1), F32)
    places, gated = [], jnp.zeros((slots_all, tok_count), F32)
    gate_rows = gates[...].astype(F32)
    copies[0].wait()
    for choice in range(2):
        chosen = routes[choice : choice + 1, :]
        one_hot = (expert_id == chosen).astype(F32)
        earlier = dot(one_hot.astype(BF16), before) + taken
        taken = taken + jnp.sum(one_hot, axis=1, keepdims=True)
        slot_pos = jnp.sum(earlier * one_hot, axis=0, keepdims=True).astype(jnp.int32)
        target = jnp.where(
            slot_pos < capacity, jnp.bitwise_xor(chosen, me) * capacity + slot_pos, slots_all
        )
        place = (slot_id == target).astype(F32)
        place_refs[choice][...] = place.astype(BF16)
        places.append(place)
        gated = gated + place * gate_rows[choice : choice + 1, :]
    copies[1].wait()
    x = dot((places[0] + places[1]).astype(BF16), tokens[...]).astype(BF16)
    copies[2].wait()
    s = dot(gated.astype(BF16), cotangent[...]).astype(BF16)
    for k in range(experts):
        blocks[k][:, :feat_width] = x[k * capacity : (k + 1) * capacity]
        blocks[k][:, feat_width:] = s[k * capacity : (k + 1) * capacity]


def block_rows(me, k, capacity):
    return pl.ds(pl.multiple_of(jnp.bitwise_xor(me, k) * capacity, capacity), capacity)


def combine_kernel(experts, capacity, place0, place1, gates, back, token_grads, gate_grads, rows):
    tok_count, feat_width = token_grads.shape
    me = lax.axis_index("expert")
    for k in range(experts):
        rows[k * capacity : (k + 1) * capacity, :] = back[block_rows(me, k, capacity), :]
    either = (place0[...].astype(F32) + place1[...].astype(F32)).astype(BF16)
    token_grads[...] = dot(either, rows[:, :feat_width], (0, 0)).astype(BF16)
    dgate = rows[:, feat_width : feat_width + tok_count].astype(F32)
    taken = [
        jnp.sum(place[...].astype(F32) * dgate, axis=0, keepdims=True) for place in (place0, place1)
    ]
    gate_grads[...] = (jnp.concatenate(taken, axis=0) / gates[...].astype(F32)).astype(BF16)


def stack(refs, part, width):
    return jnp.concatenate([ref[:, part * width : (part + 1) * width] for ref in refs], axis=0)


def my_part(ref):
    width = ref.shape[1] // lax.axis_size("dp")
    return ref[:, pl.ds(pl.multiple_of(lax.axis_index("dp") * width, width), width)]


def fetcher(sems):
    count = iter(range(sems.shape[0]))

    def fetch(source, target):
        copy = pltpu.make_async_copy(source, target, sems.at[next(count)])
        copy.start()
        return copy

    return fetch


def own_kernel(tile, order, *refs):
    row_refs, refs = refs[:2], refs[2:]
    weight_in, weight_out, d_pre_hbm, h_cut_hbm, back_hbm, *scratch = refs
    hidden, d_pre, h_cut, back, sems = scratch
    me = lax.axis_index("expert")
    width, ffw = weight_in.shape
    tiles = [slice(at, at + tile) for at in range(0, ffw, tile)]
    fetch = fetcher(sems)
    x, s = stack(row_refs, 0, width), stack(row_refs, 1, width)
    slots_all = x.shape[0]
    capacity = slots_all // len(order)
    dgate = jnp.zeros((slots_all, LANES), F32)
    for cols in tiles:
        act, slope = activate(dot(x, weight_in[:, cols]))
        hidden[:, cols] = act
        d_hidden = dot(s, weight_out[cols, :], (1, 1))
        d_pre[:, cols] = (d_hidden * slope).astype(BF16)
        product = d_hidden * act.astype(F32)
        for lane in range(0, tile, LANES):
            dgate = dgate + product[:, lane : lane + LANES]
    h_cut[...] = my_part(hidden)
    dgate = jnp.broadcast_to(jnp.sum(dgate, axis=1, keepdims=True), (slots_all, LANES))
    places = [
        (slice(i * capacity, (i + 1) * capacity), block_rows(me, k, capacity))
        for i, k in enumerate(order)
    ]
    for rows, target in places:
        back[target, width:] = dgate[rows].astype(BF16)
    outs = [
        fetch(d_pre, d_pre_hbm),
        fetch(h_cut, h_cut_hbm),
        fetch(back.at[:, width:], back_hbm.at[:, width:]),
    ]
    wide = width // 4
    for at in range(0, width, wide):
        cols = slice(at, at + wide)
        dx = dot(d_pre[...], weight_in[cols, :], (1, 1)).astype(BF16)
        for rows, target in places:
            back[target, cols] = dx[rows]
        outs.append(fetch(back.at[:, cols], back_hbm.at[:, cols]))
    for copy in outs:
        copy.wait()


def early_kernel(tile, pieces, *refs):
    row_refs, refs = refs[:pieces], refs[pieces:]
    in_hbm, out_hbm, weight_in, weight_out, d_pre, h_cut, rows, hidden, sems = refs
    width, ffw = weight_in.shape
    piece = row_refs[0].shape[0]
    tiles = [slice(at, at + tile) for at in range(0, ffw, tile)]
    fetch = fetcher(sems)
    first = [fetch(ref, rows.at[pl.ds(i * piece, piece)]) for i, ref in enumerate(row_refs)]
    weights = [
        (
            fetch(in_hbm.at[:, cols], weight_in.at[:, cols]),
            fetch(out_hbm.at[cols, :], weight_out.at[cols, :]),
        )
        for cols in tiles
    ]
    for copy in first:
        copy.wait()
    x, s = rows[:, :width], rows[:, width:]
    for cols, (copy_in, copy_out) in zip(tiles, weights):
        copy_in.wait()
        copy_out.wait()
        act, slope = activate(dot(x, weight_in[:, cols]))
        hidden[:, cols] = act
        d_pre[:, cols] = (dot(s, weight_out[cols, :], (1, 1)) * slope).astype(BF16)
    h_cut[...] = my_part(hidden)


def grads_kernel(tile, pieces, late, *refs):
    row_refs, refs = refs[:pieces], refs[pieces:]
    d_pre_refs, h_cut_refs, refs = refs[:2], refs[2:4], refs[4:]
    weight_in, weight_out, grad_in_hbm, grad_out_hbm, *scratch = refs
    rows, hidden, h_cut, d_pre, grad_in, grad_out, sems, out_sems = scratch
    width, ffw = weight_in.shape
    tiles = [slice(at, at + tile) for at in range(0, ffw, tile)]
    piece = row_refs[0].shape[0]
    known = (pieces - late) * piece
    fetch, send = fetcher(sems), fetcher(out_sems)
    copies = [
        fetch(row_refs[i], rows.at[pl.ds(i * piece, piece)])
        for i in [*range(pieces - late, pieces), *range(pieces - late)]
    ]
    at = 0
    for source, cut_source in zip(d_pre_refs, h_cut_refs):
        span = pl.ds(at, source.shape[0])
        copies += [fetch(source, d_pre.at[span]), fetch(cut_source, h_cut.at[span])]
        at += source.shape[0]
    x, s = stack(row_refs[-late:], 0, width), stack(row_refs[-late:], 1, width)
    for cols in tiles:
        act, slope = activate(dot(x, weight_in[:, cols]))
        hidden[:, cols] = act
        d_pre[known:, cols] = (dot(s, weight_out[cols, :], (1, 1)) * slope).astype(BF16)
    for copy in copies:
        copy.wait()
    cut = grad_in.shape[0]
    mine = pl.ds(pl.multiple_of(lax.axis_index("dp") * cut, cut), cut)
    outs = []
    for at in range(0, ffw, ffw // 2):
        cols = slice(at, at + ffw // 2)
        grad_in[:, cols] = dot(rows[:, mine], d_pre[:, cols], (0, 0)).astype(BF16)
        outs.append(send(grad_in.at[:, cols], grad_in_hbm.at[:, cols]))
    h_cut[known:, :] = my_part(hidden)
    wide = h_cut.shape[1] // 2
    for at in (0, wide):
        part = slice(at, at + wide)
        grad_out[part, :] = dot(h_cut[:, part], rows[:, width:], (0, 0)).astype(BF16)
        outs.append(send(grad_out.at[part, :], grad_out_hbm.at[part, :]))
    for copy in outs:
        copy.wait()


def after(value, *first):
    return lax.optimization_barrier((value, *first))[0]


def permute(block, k):
    return lax.ppermute(block, "expert", [(i, i ^ k) for i in range(lax.axis_size("expert"))])


def swap_cores(rows):
    return lax.ppermute(rows, "dp", [(i, i ^ 1) for i in range(lax.axis_size("dp"))])


def shift_chips(rows, k):
    groups = lax.axis_size("dp")
    return lax.ppermute(rows, "dp", [(i, (i + 2 * k) % groups) for i in range(groups)])


def gather_groups(rows):
    others = [swap_cores(rows)]
    for k in range(1, lax.axis_size("dp") // 2):
        other = shift_chips(rows, k)
        others += [other, swap_cores(other)]
    return others


def local(tokens, cotangent, routes, gates, proj_in, proj_out):
    tok_count, feat_width = tokens.shape
    experts = lax.axis_size("expert")
    groups = lax.axis_size("dp")
    capacity = 2 * tok_count // experts
    slots_all = experts * capacity
    half = experts // 2
    ffw = proj_in.shape[2]
    tile = ffw // groups
    product = 2 * slots_all * feat_width * ffw
    place = shape((slots_all, tok_count))

    routed = call(
        functools.partial(route_kernel, experts, capacity),
        [shape((capacity, 2 * feat_width))] * experts + [place] * 2,
        [routes.T, gates.T, tokens, cotangent],
        30 * product,
        spaces=[pltpu.HBM, pltpu.VMEM, pltpu.HBM, pltpu.HBM],
        scratch=[
            pltpu.VMEM((2, tok_count), jnp.int32),
            pltpu.VMEM((tok_count, feat_width), BF16),
            pltpu.VMEM((tok_count, feat_width), BF16),
            pltpu.SemaphoreType.DMA((4,)),
        ],
    )
    blocks, places = routed[:experts], routed[experts:]
    rest = list(range(experts - 1, 1, -1))
    if len(rest) > 4:
        rest.insert(2, rest.pop(-2))
    order = [0, *rest[:2], 1, *rest[2:]]
    order_a, order_b = order[:half], order[half:]
    got_a = [blocks[0]] + [permute(blocks[k], k) for k in order_a[1:]]
    got_b = [
        permute(blocks[k] if i < 2 else after(blocks[k], got_a[-1]), k)
        for i, k in enumerate(order_b)
    ]
    rows_a = jnp.concatenate(got_a, axis=0)
    chips_a = [shift_chips(rows_a, k) for k in range(1, groups // 2)]
    core_a = swap_cores(after(rows_a, got_b[0]))
    rows_b = jnp.concatenate(got_b, axis=0)
    chips_b = [shift_chips(rows_b, k) for k in range(1, groups // 2)]
    core_b = swap_cores(rows_b)
    weights = [proj_in[0], proj_out[0]]
    weight_space = [pltpu.VMEM((feat_width, ffw), BF16), pltpu.VMEM((ffw, feat_width), BF16)]
    d_pre, h_cut, back = call(
        functools.partial(own_kernel, tile // 2, order),
        [
            pltpu.HBM((slots_all, ffw), BF16),
            pltpu.HBM((slots_all, tile), BF16),
            pltpu.HBM((slots_all, feat_width + LANES), BF16),
        ],
        [
            rows_a,
            rows_b,
            *[pltpu.with_memory_space_constraint(w, pltpu.VMEM) for w in weights],
        ],
        20 * product,
        scratch=[
            pltpu.VMEM((slots_all, ffw), BF16),
            pltpu.VMEM((slots_all, ffw), BF16),
            pltpu.VMEM((slots_all, tile), BF16),
            pltpu.VMEM((slots_all, feat_width + LANES), BF16),
            pltpu.SemaphoreType.DMA((7,)),
        ],
    )
    back = lax.all_to_all(
        after(back, core_a, core_b).reshape(experts, capacity, feat_width + LANES),
        "expert",
        0,
        0,
        tiled=True,
    ).reshape(slots_all, feat_width + LANES)
    relayed_a = [swap_cores(after(rows, d_pre)) for rows in chips_a]
    relayed_b = [swap_cores(rows) for rows in chips_b]
    early = [core_a, core_b, *chips_a]
    late = [*relayed_a, *chips_b, *relayed_b]
    early_rows = sum(piece.shape[0] for piece in early)
    late_rows = sum(piece.shape[0] for piece in late)
    weight_in, weight_out, d_pre_early, h_cut_early = call(
        functools.partial(early_kernel, tile, len(early)),
        [*weight_space, shape((early_rows, ffw)), shape((early_rows, tile))],
        [*early, *weights],
        2 * product,
        scratch=[
            pltpu.VMEM((early_rows, 2 * feat_width), BF16),
            pltpu.VMEM((early_rows, ffw), BF16),
            pltpu.SemaphoreType.DMA((len(early) + 2 * groups,)),
        ],
        spaces=[pl.ANY] * len(early) + [pltpu.HBM] * 2,
    )
    pieces = [rows_a, rows_b, *early, *late]
    rows_all = groups * slots_all
    grad_in, grad_out = call(
        functools.partial(grads_kernel, tile // 2, len(pieces), len(late)),
        [
            pltpu.HBM((feat_width // groups, ffw), BF16),
            pltpu.HBM((ffw // groups, feat_width), BF16),
        ],
        [
            *pieces,
            *[d_pre, d_pre_early, h_cut, h_cut_early],
            *[
                pltpu.with_memory_space_constraint(w, pltpu.VMEM)
                for w in (weight_in, weight_out)
            ],
        ],
        4 * product,
        limit=32,
        scratch=[
            pltpu.VMEM((rows_all, 2 * feat_width), BF16),
            pltpu.VMEM((late_rows, ffw), BF16),
            pltpu.VMEM((rows_all, tile), BF16),
            pltpu.VMEM((rows_all, ffw), BF16),
            pltpu.VMEM((feat_width // groups, ffw), BF16),
            pltpu.VMEM((ffw // groups, feat_width), BF16),
            pltpu.SemaphoreType.DMA((len(pieces) + 4,)),
            pltpu.SemaphoreType.DMA((4,)),
        ],
        spaces=[pl.ANY] * (len(pieces) - len(late))
        + [pltpu.VMEM] * len(late)
        + [pltpu.HBM, pl.ANY] * 2
        + [pltpu.VMEM] * 2,
    )
    token_grads, gate_grads = call(
        functools.partial(combine_kernel, experts, capacity),
        [shape((tok_count, feat_width)), shape((2, tok_count))],
        [*places, gates.T, after(back, grad_in)],
        scratch=[pltpu.VMEM((slots_all, feat_width + LANES), BF16)],
    )
    return (token_grads, gate_grads.T, grad_in[None], grad_out[None])


def local_small_blocks(tokens, cotangent, routes, gates, proj_in, proj_out):
    tok_count, feat_width = tokens.shape
    experts = lax.axis_size("expert")
    groups = lax.axis_size("dp")
    me = lax.axis_index("dp")
    capacity = 2 * tok_count // experts
    slots_all = experts * capacity
    weight_in, weight_out = proj_in[0], proj_out[0]
    ffw = weight_in.shape[1]
    chosen = jnp.concatenate([routes[:, 0], routes[:, 1]])
    one_hot = (chosen[:, None] == jnp.arange(experts, dtype=jnp.int32)[None, :]).astype(jnp.int32)
    slot_pos = jnp.sum((jnp.cumsum(one_hot, axis=0) - one_hot) * one_hot, axis=1)
    target = jnp.where(slot_pos < capacity, chosen * capacity + slot_pos, slots_all)
    placing = (jnp.arange(slots_all, dtype=jnp.int32)[:, None] == target[None, :]).astype(BF16)
    either = placing[:, :tok_count] + placing[:, tok_count:]
    scaled = [
        (gates[:, k : k + 1].astype(F32) * cotangent.astype(F32)).astype(BF16) for k in range(2)
    ]

    def swap_blocks(rows):
        return lax.all_to_all(
            rows.astype(BF16).reshape(experts, capacity, rows.shape[1]), "expert", 0, 0, tiled=True
        ).reshape(slots_all, rows.shape[1])

    x = swap_blocks(dot(either, tokens))
    s = swap_blocks(dot(placing, jnp.concatenate(scaled, axis=0)))
    hidden0, slope0 = activate(dot(x, weight_in))
    d_hidden0 = dot(s, weight_out, (1, 1))
    d_pre0 = (d_hidden0 * slope0).astype(BF16)
    dgate = jnp.sum(hidden0.astype(F32) * d_hidden0, axis=1, keepdims=True)
    dx = dot(d_pre0, weight_in, (1, 1))
    back = swap_blocks(
        jnp.concatenate([dx, jnp.broadcast_to(dgate, (slots_all, LANES))], axis=1)
    )
    x_all = jnp.concatenate([x, *gather_groups(x)], axis=0)
    s_all = jnp.concatenate([s, *gather_groups(s)], axis=0)
    hidden1, slope1 = activate(dot(x_all[slots_all:], weight_in))
    d_pre1 = (dot(s_all[slots_all:], weight_out, (1, 1)) * slope1).astype(BF16)
    hidden = jnp.concatenate([hidden0, hidden1], axis=0)
    d_pre = jnp.concatenate([d_pre0, d_pre1], axis=0)
    x_cut = lax.dynamic_slice_in_dim(x_all, me * (feat_width // groups), feat_width // groups, 1)
    h_cut = lax.dynamic_slice_in_dim(hidden, me * (ffw // groups), ffw // groups, 1)
    grad_in = dot(x_cut, d_pre, (0, 0)).astype(BF16)
    grad_out = dot(h_cut, s_all, (0, 0)).astype(BF16)
    token_grads = dot(either, back[:, :feat_width], (0, 0)).astype(BF16)
    taken = dot(placing, back[:, feat_width : feat_width + 1], (0, 0))
    gate_grads = jnp.concatenate([taken[:tok_count], taken[tok_count:]], axis=1)
    gate_grads = (gate_grads / gates.astype(F32)).astype(BF16)
    return (token_grads, gate_grads, grad_in[None], grad_out[None])


def solution(mesh):
    rows = P(("dp", "expert"), None)
    weights = P("expert", None, None)

    def whole(tokens, *others):
        experts = mesh.shape["expert"]
        capacity = 2 * tokens.shape[0] // (mesh.shape["dp"] * experts) // experts
        tiles = capacity % 16 == 0 and experts & (experts - 1) == 0
        return jax.shard_map(
            local if tiles else local_small_blocks,
            mesh=mesh,
            in_specs=(rows, rows, rows, rows, weights, weights),
            out_specs=(rows, rows, P("expert", "dp", None), P("expert", "dp", None)),
            check_vma=False,
        )(tokens, *others)

    return whole
```

```python
import functools

import jax
import jax.numpy as jnp
from jax import lax
from jax.experimental import pallas as pl
from jax.experimental.pallas import tpu as pltpu
from jax.sharding import PartitionSpec as P

BF16 = jnp.bfloat16
F32 = jnp.float32
LANES = 128
MIB = 1 << 20


def dot(a, b, over=(1, 0)):
    return lax.dot_general(
        a, b, (((over[0],), (over[1],)), ((), ())), preferred_element_type=F32
    )


def activate(pre_act):
    cdf = 0.5 * (1.0 + lax.erf(pre_act * 0.7071067811865476))
    pdf = jnp.exp(-0.5 * pre_act * pre_act) * 0.3989422804014327
    return (pre_act * cdf).astype(BF16), cdf + pre_act * pdf


def call(kernel, out_shape, args, flops=0, limit=24, scratch=(), spaces=None):
    spaces = spaces or [pltpu.VMEM] * len(args)
    moved = sum(a.size * a.dtype.itemsize for a in args)
    args = [
        pltpu.with_memory_space_constraint(a, space) if space == pltpu.HBM else a
        for a, space in zip(args, spaces)
    ]
    return pl.pallas_call(
        kernel,
        out_shape=out_shape,
        in_specs=[pl.BlockSpec(memory_space=space) for space in spaces],
        out_specs=[
            pl.BlockSpec(memory_space=getattr(out, "memory_space", pltpu.VMEM))
            for out in out_shape
        ],
        scratch_shapes=list(scratch),
        compiler_params=pltpu.CompilerParams(vmem_limit_bytes=limit * MIB),
        cost_estimate=pl.CostEstimate(flops=flops, bytes_accessed=moved, transcendentals=0),
    )(*args)


def shape(dims, dtype=BF16):
    return jax.ShapeDtypeStruct(dims, dtype)


def route_kernel(experts, capacity, routes_hbm, gates_hbm, tokens_hbm, cotangent_hbm, *refs):
    blocks, place_refs, scratch = refs[:experts], refs[experts : experts + 2], refs[experts + 2 :]
    routes, gates, tokens, cotangent, sems = scratch
    copies = [
        pltpu.make_async_copy(source, target, sems.at[i])
        for i, (source, target) in enumerate(
            (
                (routes_hbm, routes),
                (gates_hbm, gates),
                (tokens_hbm, tokens),
                (cotangent_hbm, cotangent),
            )
        )
    ]
    for copy in copies:
        copy.start()
    tok_count, feat_width = tokens.shape
    slots_all = experts * capacity
    me = lax.axis_index("expert")
    rows = max(experts, 16)
    before = (
        lax.broadcasted_iota(jnp.int32, (tok_count, tok_count), 0)
        < lax.broadcasted_iota(jnp.int32, (tok_count, tok_count), 1)
    ).astype(F32).astype(BF16)
    expert_id = lax.broadcasted_iota(jnp.int32, (rows, tok_count), 0)
    slot_id = lax.broadcasted_iota(jnp.int32, (slots_all, tok_count), 0)
    taken = jnp.zeros((rows, 1), F32)
    places, gated = [], jnp.zeros((slots_all, tok_count), F32)
    copies[0].wait()
    copies[1].wait()
    for choice in range(2):
        chosen = routes[choice : choice + 1, :]
        one_hot = (expert_id == chosen).astype(F32)
        earlier = dot(one_hot.astype(BF16), before) + taken
        taken = taken + jnp.sum(one_hot, axis=1, keepdims=True)
        slot_pos = jnp.sum(earlier * one_hot, axis=0, keepdims=True).astype(jnp.int32)
        target = jnp.where(
            slot_pos < capacity, jnp.bitwise_xor(chosen, me) * capacity + slot_pos, slots_all
        )
        place = (slot_id == target).astype(F32)
        place_refs[choice][...] = place.astype(BF16)
        places.append(place)
        gated = gated + place * gates[choice : choice + 1, :].astype(F32)
    copies[2].wait()
    x = dot((places[0] + places[1]).astype(BF16), tokens[...]).astype(BF16)
    copies[3].wait()
    s = dot(gated.astype(BF16), cotangent[...]).astype(BF16)
    for k in range(experts):
        blocks[k][:, :feat_width] = x[k * capacity : (k + 1) * capacity]
        blocks[k][:, feat_width:] = s[k * capacity : (k + 1) * capacity]


def block_rows(me, k, capacity):
    return pl.ds(pl.multiple_of(jnp.bitwise_xor(me, k) * capacity, capacity), capacity)


def combine_kernel(experts, capacity, place0, place1, gates, back, token_grads, gate_grads, rows):
    tok_count, feat_width = token_grads.shape
    me = lax.axis_index("expert")
    for k in range(experts):
        rows[k * capacity : (k + 1) * capacity, :] = back[block_rows(me, k, capacity), :]
    either = (place0[...].astype(F32) + place1[...].astype(F32)).astype(BF16)
    token_grads[...] = dot(either, rows[:, :feat_width], (0, 0)).astype(BF16)
    dgate = rows[:, feat_width : feat_width + tok_count].astype(F32)
    taken = [
        jnp.sum(place[...].astype(F32) * dgate, axis=0, keepdims=True) for place in (place0, place1)
    ]
    gate_grads[...] = (jnp.concatenate(taken, axis=0) / gates[...].astype(F32)).astype(BF16)


def stack(refs, part, width):
    return jnp.concatenate([ref[:, part * width : (part + 1) * width] for ref in refs], axis=0)


def my_part(ref):
    width = ref.shape[1] // lax.axis_size("dp")
    return ref[:, pl.ds(pl.multiple_of(lax.axis_index("dp") * width, width), width)]


def fetcher(sems):
    count = iter(range(sems.shape[0]))

    def fetch(source, target):
        copy = pltpu.make_async_copy(source, target, sems.at[next(count)])
        copy.start()
        return copy

    return fetch


def own_kernel(tile, order, *refs):
    row_refs, refs = refs[:2], refs[2:]
    weight_in, weight_out, d_pre_hbm, h_cut_hbm, back_hbm, *scratch = refs
    hidden, d_pre, h_cut, back, sems = scratch
    me = lax.axis_index("expert")
    width, ffw = weight_in.shape
    tiles = [slice(at, at + tile) for at in range(0, ffw, tile)]
    fetch = fetcher(sems)
    x, s = stack(row_refs, 0, width), stack(row_refs, 1, width)
    slots_all = x.shape[0]
    capacity = slots_all // len(order)
    dgate = jnp.zeros((slots_all, LANES), F32)
    for cols in tiles:
        act, slope = activate(dot(x, weight_in[:, cols]))
        hidden[:, cols] = act
        d_hidden = dot(s, weight_out[cols, :], (1, 1))
        d_pre[:, cols] = (d_hidden * slope).astype(BF16)
        product = d_hidden * act.astype(F32)
        for lane in range(0, tile, LANES):
            dgate = dgate + product[:, lane : lane + LANES]
    h_cut[...] = my_part(hidden)
    dgate = jnp.broadcast_to(jnp.sum(dgate, axis=1, keepdims=True), (slots_all, LANES))
    places = [
        (slice(i * capacity, (i + 1) * capacity), block_rows(me, k, capacity))
        for i, k in enumerate(order)
    ]
    for rows, target in places:
        back[target, width:] = dgate[rows].astype(BF16)
    outs = [
        fetch(d_pre, d_pre_hbm),
        fetch(h_cut, h_cut_hbm),
        fetch(back.at[:, width:], back_hbm.at[:, width:]),
    ]
    wide = width // 4
    for at in range(0, width, wide):
        cols = slice(at, at + wide)
        dx = dot(d_pre[...], weight_in[cols, :], (1, 1)).astype(BF16)
        for rows, target in places:
            back[target, cols] = dx[rows]
        outs.append(fetch(back.at[:, cols], back_hbm.at[:, cols]))
    for copy in outs:
        copy.wait()


def early_kernel(tile, pieces, *refs):
    row_refs, refs = refs[:pieces], refs[pieces:]
    in_hbm, out_hbm, weight_in, weight_out, d_pre, h_cut, rows, hidden, sems = refs
    width, ffw = weight_in.shape
    piece = row_refs[0].shape[0]
    tiles = [slice(at, at + tile) for at in range(0, ffw, tile)]
    fetch = fetcher(sems)
    first = [fetch(ref, rows.at[pl.ds(i * piece, piece)]) for i, ref in enumerate(row_refs)]
    weights = [
        (
            fetch(in_hbm.at[:, cols], weight_in.at[:, cols]),
            fetch(out_hbm.at[cols, :], weight_out.at[cols, :]),
        )
        for cols in tiles
    ]
    for copy in first:
        copy.wait()
    x, s = rows[:, :width], rows[:, width:]
    for cols, (copy_in, copy_out) in zip(tiles, weights):
        copy_in.wait()
        copy_out.wait()
        act, slope = activate(dot(x, weight_in[:, cols]))
        hidden[:, cols] = act
        d_pre[:, cols] = (dot(s, weight_out[cols, :], (1, 1)) * slope).astype(BF16)
    h_cut[...] = my_part(hidden)


def grads_kernel(tile, pieces, late, *refs):
    row_refs, refs = refs[:pieces], refs[pieces:]
    d_pre_refs, h_cut_refs, refs = refs[:2], refs[2:4], refs[4:]
    weight_in, weight_out, grad_in_hbm, grad_out_hbm, *scratch = refs
    rows, hidden, h_cut, d_pre, grad_in, grad_out, sems, out_sems = scratch
    width, ffw = weight_in.shape
    tiles = [slice(at, at + tile) for at in range(0, ffw, tile)]
    piece = row_refs[0].shape[0]
    known = (pieces - late) * piece
    fetch, send = fetcher(sems), fetcher(out_sems)
    copies = [
        fetch(row_refs[i], rows.at[pl.ds(i * piece, piece)])
        for i in [*range(pieces - late, pieces), *range(pieces - late)]
    ]
    at = 0
    for source, cut_source in zip(d_pre_refs, h_cut_refs):
        span = pl.ds(at, source.shape[0])
        copies += [fetch(source, d_pre.at[span]), fetch(cut_source, h_cut.at[span])]
        at += source.shape[0]
    x, s = stack(row_refs[-late:], 0, width), stack(row_refs[-late:], 1, width)
    for cols in tiles:
        act, slope = activate(dot(x, weight_in[:, cols]))
        hidden[:, cols] = act
        d_pre[known:, cols] = (dot(s, weight_out[cols, :], (1, 1)) * slope).astype(BF16)
    for copy in copies:
        copy.wait()
    cut = grad_in.shape[0]
    mine = pl.ds(pl.multiple_of(lax.axis_index("dp") * cut, cut), cut)
    outs = []
    for at in range(0, ffw, ffw // 2):
        cols = slice(at, at + ffw // 2)
        grad_in[:, cols] = dot(rows[:, mine], d_pre[:, cols], (0, 0)).astype(BF16)
        outs.append(send(grad_in.at[:, cols], grad_in_hbm.at[:, cols]))
    h_cut[known:, :] = my_part(hidden)
    wide = h_cut.shape[1] // 2
    for at in (0, wide):
        part = slice(at, at + wide)
        grad_out[part, :] = dot(h_cut[:, part], rows[:, width:], (0, 0)).astype(BF16)
        outs.append(send(grad_out.at[part, :], grad_out_hbm.at[part, :]))
    for copy in outs:
        copy.wait()


def after(value, *first):
    return lax.optimization_barrier((value, *first))[0]


def permute(block, k):
    return lax.ppermute(block, "expert", [(i, i ^ k) for i in range(lax.axis_size("expert"))])


def swap_cores(rows):
    return lax.ppermute(rows, "dp", [(i, i ^ 1) for i in range(lax.axis_size("dp"))])


def shift_chips(rows, k):
    groups = lax.axis_size("dp")
    return lax.ppermute(rows, "dp", [(i, (i + 2 * k) % groups) for i in range(groups)])


def gather_groups(rows):
    others = [swap_cores(rows)]
    for k in range(1, lax.axis_size("dp") // 2):
        other = shift_chips(rows, k)
        others += [other, swap_cores(other)]
    return others


def local(tokens, cotangent, routes, gates, proj_in, proj_out):
    tok_count, feat_width = tokens.shape
    experts = lax.axis_size("expert")
    groups = lax.axis_size("dp")
    capacity = 2 * tok_count // experts
    slots_all = experts * capacity
    half = experts // 2
    ffw = proj_in.shape[2]
    tile = ffw // groups
    product = 2 * slots_all * feat_width * ffw
    place = shape((slots_all, tok_count))

    routed = call(
        functools.partial(route_kernel, experts, capacity),
        [shape((capacity, 2 * feat_width))] * experts + [place] * 2,
        [routes.T, gates.T, tokens, cotangent],
        30 * product,
        spaces=[pltpu.HBM] * 4,
        scratch=[
            pltpu.VMEM((2, tok_count), jnp.int32),
            pltpu.VMEM((2, tok_count), BF16),
            pltpu.VMEM((tok_count, feat_width), BF16),
            pltpu.VMEM((tok_count, feat_width), BF16),
            pltpu.SemaphoreType.DMA((4,)),
        ],
    )
    blocks, places = routed[:experts], routed[experts:]
    rest = list(range(experts - 1, 1, -1))
    if len(rest) > 4:
        rest.insert(2, rest.pop())
    order = [0, *rest[:2], 1, *rest[2:]]
    order_a, order_b = order[:half], order[half:]
    got_a = [blocks[0]] + [permute(blocks[k], k) for k in order_a[1:]]
    got_b = [
        permute(blocks[k] if i < 2 else after(blocks[k], got_a[-1]), k)
        for i, k in enumerate(order_b)
    ]
    rows_a = jnp.concatenate(got_a, axis=0)
    chips_a = [shift_chips(rows_a, k) for k in range(1, groups // 2)]
    core_a = swap_cores(after(rows_a, got_b[0]))
    rows_b = jnp.concatenate(got_b, axis=0)
    chips_b = [shift_chips(rows_b, k) for k in range(1, groups // 2)]
    core_b = swap_cores(rows_b)
    weights = [proj_in[0], proj_out[0]]
    weight_space = [pltpu.VMEM((feat_width, ffw), BF16), pltpu.VMEM((ffw, feat_width), BF16)]
    d_pre, h_cut, back = call(
        functools.partial(own_kernel, tile // 2, order),
        [
            pltpu.HBM((slots_all, ffw), BF16),
            pltpu.HBM((slots_all, tile), BF16),
            pltpu.HBM((slots_all, feat_width + LANES), BF16),
        ],
        [
            rows_a,
            rows_b,
            *[pltpu.with_memory_space_constraint(w, pltpu.VMEM) for w in weights],
        ],
        20 * product,
        scratch=[
            pltpu.VMEM((slots_all, ffw), BF16),
            pltpu.VMEM((slots_all, ffw), BF16),
            pltpu.VMEM((slots_all, tile), BF16),
            pltpu.VMEM((slots_all, feat_width + LANES), BF16),
            pltpu.SemaphoreType.DMA((7,)),
        ],
    )
    back = lax.all_to_all(
        after(back, core_a, core_b).reshape(experts, capacity, feat_width + LANES),
        "expert",
        0,
        0,
        tiled=True,
    ).reshape(slots_all, feat_width + LANES)
    relayed_a = [swap_cores(after(rows, d_pre)) for rows in chips_a]
    relayed_b = [swap_cores(rows) for rows in chips_b]
    early = [core_a, core_b, *chips_a]
    late = [*relayed_a, *chips_b, *relayed_b]
    early_rows = sum(piece.shape[0] for piece in early)
    late_rows = sum(piece.shape[0] for piece in late)
    weight_in, weight_out, d_pre_early, h_cut_early = call(
        functools.partial(early_kernel, tile, len(early)),
        [*weight_space, shape((early_rows, ffw)), shape((early_rows, tile))],
        [*early, *weights],
        2 * product,
        scratch=[
            pltpu.VMEM((early_rows, 2 * feat_width), BF16),
            pltpu.VMEM((early_rows, ffw), BF16),
            pltpu.SemaphoreType.DMA((len(early) + 2 * groups,)),
        ],
        spaces=[pl.ANY] * len(early) + [pltpu.HBM] * 2,
    )
    pieces = [rows_a, rows_b, *early, *late]
    rows_all = groups * slots_all
    grad_in, grad_out = call(
        functools.partial(grads_kernel, tile // 2, len(pieces), len(late)),
        [
            pltpu.HBM((feat_width // groups, ffw), BF16),
            pltpu.HBM((ffw // groups, feat_width), BF16),
        ],
        [
            *pieces,
            *[d_pre, d_pre_early, h_cut, h_cut_early],
            *[
                pltpu.with_memory_space_constraint(w, pltpu.VMEM)
                for w in (weight_in, weight_out)
            ],
        ],
        4 * product,
        limit=32,
        scratch=[
            pltpu.VMEM((rows_all, 2 * feat_width), BF16),
            pltpu.VMEM((late_rows, ffw), BF16),
            pltpu.VMEM((rows_all, tile), BF16),
            pltpu.VMEM((rows_all, ffw), BF16),
            pltpu.VMEM((feat_width // groups, ffw), BF16),
            pltpu.VMEM((ffw // groups, feat_width), BF16),
            pltpu.SemaphoreType.DMA((len(pieces) + 4,)),
            pltpu.SemaphoreType.DMA((4,)),
        ],
        spaces=[pl.ANY] * (len(pieces) - len(late))
        + [pltpu.VMEM] * len(late)
        + [pltpu.HBM, pl.ANY] * 2
        + [pltpu.VMEM] * 2,
    )
    token_grads, gate_grads = call(
        functools.partial(combine_kernel, experts, capacity),
        [shape((tok_count, feat_width)), shape((2, tok_count))],
        [*places, gates.T, after(back, grad_in)],
        scratch=[pltpu.VMEM((slots_all, feat_width + LANES), BF16)],
    )
    return (token_grads, gate_grads.T, grad_in[None], grad_out[None])


def local_small_blocks(tokens, cotangent, routes, gates, proj_in, proj_out):
    tok_count, feat_width = tokens.shape
    experts = lax.axis_size("expert")
    groups = lax.axis_size("dp")
    me = lax.axis_index("dp")
    capacity = 2 * tok_count // experts
    slots_all = experts * capacity
    weight_in, weight_out = proj_in[0], proj_out[0]
    ffw = weight_in.shape[1]
    chosen = jnp.concatenate([routes[:, 0], routes[:, 1]])
    one_hot = (chosen[:, None] == jnp.arange(experts, dtype=jnp.int32)[None, :]).astype(jnp.int32)
    slot_pos = jnp.sum((jnp.cumsum(one_hot, axis=0) - one_hot) * one_hot, axis=1)
    target = jnp.where(slot_pos < capacity, chosen * capacity + slot_pos, slots_all)
    placing = (jnp.arange(slots_all, dtype=jnp.int32)[:, None] == target[None, :]).astype(BF16)
    either = placing[:, :tok_count] + placing[:, tok_count:]
    scaled = [
        (gates[:, k : k + 1].astype(F32) * cotangent.astype(F32)).astype(BF16) for k in range(2)
    ]

    def swap_blocks(rows):
        return lax.all_to_all(
            rows.astype(BF16).reshape(experts, capacity, rows.shape[1]), "expert", 0, 0, tiled=True
        ).reshape(slots_all, rows.shape[1])

    x = swap_blocks(dot(either, tokens))
    s = swap_blocks(dot(placing, jnp.concatenate(scaled, axis=0)))
    hidden0, slope0 = activate(dot(x, weight_in))
    d_hidden0 = dot(s, weight_out, (1, 1))
    d_pre0 = (d_hidden0 * slope0).astype(BF16)
    dgate = jnp.sum(hidden0.astype(F32) * d_hidden0, axis=1, keepdims=True)
    dx = dot(d_pre0, weight_in, (1, 1))
    back = swap_blocks(
        jnp.concatenate([dx, jnp.broadcast_to(dgate, (slots_all, LANES))], axis=1)
    )
    x_all = jnp.concatenate([x, *gather_groups(x)], axis=0)
    s_all = jnp.concatenate([s, *gather_groups(s)], axis=0)
    hidden1, slope1 = activate(dot(x_all[slots_all:], weight_in))
    d_pre1 = (dot(s_all[slots_all:], weight_out, (1, 1)) * slope1).astype(BF16)
    hidden = jnp.concatenate([hidden0, hidden1], axis=0)
    d_pre = jnp.concatenate([d_pre0, d_pre1], axis=0)
    x_cut = lax.dynamic_slice_in_dim(x_all, me * (feat_width // groups), feat_width // groups, 1)
    h_cut = lax.dynamic_slice_in_dim(hidden, me * (ffw // groups), ffw // groups, 1)
    grad_in = dot(x_cut, d_pre, (0, 0)).astype(BF16)
    grad_out = dot(h_cut, s_all, (0, 0)).astype(BF16)
    token_grads = dot(either, back[:, :feat_width], (0, 0)).astype(BF16)
    taken = dot(placing, back[:, feat_width : feat_width + 1], (0, 0))
    gate_grads = jnp.concatenate([taken[:tok_count], taken[tok_count:]], axis=1)
    gate_grads = (gate_grads / gates.astype(F32)).astype(BF16)
    return (token_grads, gate_grads, grad_in[None], grad_out[None])


def solution(mesh):
    rows = P(("dp", "expert"), None)
    weights = P("expert", None, None)

    def whole(tokens, *others):
        experts = mesh.shape["expert"]
        capacity = 2 * tokens.shape[0] // (mesh.shape["dp"] * experts) // experts
        tiles = capacity % 16 == 0 and experts & (experts - 1) == 0
        return jax.shard_map(
            local if tiles else local_small_blocks,
            mesh=mesh,
            in_specs=(rows, rows, rows, rows, weights, weights),
            out_specs=(rows, rows, P("expert", "dp", None), P("expert", "dp", None)),
            check_vma=False,
        )(tokens, *others)

    return whole
```
